128 devices in a mesh: ctx: 16 (over z, x), head: 8 (over y, core).
Axes of the slice: x: 4, y: 4, z: 4, core: 2. Of those that a mesh axis runs over, the one named last changes fastest.
Arguments:
- ssm_input: bfloat16 [16384, 8192], P(('ctx', 'head')), may hold values from -6 to 6
- gate_input: bfloat16 [16384, 8192], P(('ctx', 'head')), may hold values from -6 to 6
- b_input: bfloat16 [16384, 1024], P(('ctx', 'head')), may hold values from -3 to 3
- c_input: bfloat16 [16384, 1024], P(('ctx', 'head')), may hold values from -3 to 3
- dt_raw: bfloat16 [16384, 128], P(('ctx', 'head')), may hold values from -13 to 0
- dt_bias: float32 [128], replicated, may hold values from -0.25 to 0.25
- a_log: float32 [128], replicated, may hold values from -6 to 3
- skip_gain: float32 [128], replicated, may hold values from 0.5 to 1.5
- out_grad: bfloat16 [16384, 8192], P(('ctx', 'head')), may hold values from -6 to 6
Outputs:
- gated_out: bfloat16 [16384, 8192], P(('ctx', 'head'))
- input_grad: float32 [16384, 8192], P(('ctx', 'head'))
- b_grad: float32 [16384, 1024], P(('ctx', 'head'))
- c_grad: float32 [16384, 1024], P(('ctx', 'head'))
The draws below stay inside these ranges and needn't reach their ends.
All inputs are finite; a program needn't handle non-finite values.
Results may differ from the reference program's by a relative error of at most 0.014.
Values may be sent and summed in bfloat16 or wider, within the bound.
No kernel may reach another device: no remote copies, remote signals or barrier semaphores. Data moves between devices by JAX's collectives and lax.ppermute only.
A program may use at most 128 MiB of HBM per device.

```python
import math
import jax
import jax.numpy as jnp
from jax import lax

NH = 128
P_SIZE = 64
N = 128
NG = 8
SEQ = 16384


def head_plan(key, slow_share, medium_share):
    plan_keys = jax.random.split(jax.random.fold_in(key, 101), 7)
    chooser = jax.random.uniform(plan_keys[0], (NH,))
    slow_head = chooser < slow_share
    medium_head = (chooser >= slow_share) & (chooser < slow_share + medium_share)
    fast_step = jnp.exp(jax.random.uniform(plan_keys[1], (NH,), minval=math.log(0.05), maxval=math.log(0.12)))
    fast_rate = 1.0 / jax.random.uniform(plan_keys[2], (NH,), minval=30.0, maxval=50.0)
    medium_step = jnp.exp(jax.random.uniform(plan_keys[3], (NH,), minval=math.log(0.015), maxval=math.log(0.03)))
    medium_rate = jax.random.uniform(plan_keys[4], (NH,), minval=1.0, maxval=1.8) * (16.0 / SEQ)
    slow_step = jnp.exp(jax.random.uniform(plan_keys[5], (NH,), minval=math.log(0.35), maxval=math.log(0.6))) / math.sqrt(SEQ)
    slow_rate = jax.random.uniform(plan_keys[6], (NH,), minval=0.3, maxval=1.2) / SEQ
    base_step = jnp.where(slow_head, slow_step, jnp.where(medium_head, medium_step, fast_step))
    base_rate = jnp.where(slow_head, slow_rate, jnp.where(medium_head, medium_rate, fast_rate))
    return (base_step, base_rate)


def draw_a_log(key, part):
    slow_share = 0.5
    medium_share = 0.25
    base_step, base_rate = head_plan(key, slow_share, medium_share)
    return jnp.log(base_rate / base_step).astype(jnp.float32)


def draw_dt_raw(key, part):
    slow_share = 0.5
    medium_share = 0.25
    base_step, base_rate = head_plan(key, slow_share, medium_share)
    key = jax.random.fold_in(key, 3)
    random_subkeys = jax.random.split(key, 7)
    region = jnp.exp(jax.random.uniform(random_subkeys[3], (16,), minval=-0.4, maxval=0.4))
    roughness = jnp.exp(jax.random.uniform(random_subkeys[4], (SEQ, NH), minval=-0.5, maxval=0.5))
    token_positions = jnp.arange(SEQ)
    interval_width = base_step[None, :] * roughness * region[token_positions // (SEQ // 16)][:, None]
    quarter_length = SEQ // 4
    segment_rows = jax.random.randint(random_subkeys[5], (3,), 0, quarter_length) + jnp.arange(3) * quarter_length
    level_heights = jax.random.uniform(random_subkeys[6], (3, NH), minval=0.4, maxval=0.5)
    for segment_index in range(3):
        interval_width = jnp.where((token_positions == segment_rows[segment_index])[:, None], level_heights[segment_index][None, :], interval_width)
    return jnp.log(jnp.expm1(interval_width)).astype(jnp.bfloat16)


def level_of(key, extent, pieces, low, high):
    level = 1.0
    for position, blocks in pieces:
        heights = jax.random.uniform(jax.random.fold_in(jax.random.fold_in(key, 6), position), (blocks,), jnp.float32, low / len(pieces), high / len(pieces))
        level = level * jnp.repeat(jnp.exp(heights), extent[position] // blocks).reshape((-1,) + (1,) * (len(extent) - 1 - position))
    return level


def centred(stream_key, extent, scale, reach, pieces=(), kind=jnp.bfloat16):
    level = level_of(stream_key, extent, pieces, -0.22, 0.18) if pieces else 1.0
    result = jax.random.normal(stream_key, extent, jnp.float32) * scale * level
    return jnp.minimum(jnp.maximum(result, -reach), reach).astype(kind)


def setup_inputs(seed: int = 0) -> dict:
    arg_keys = jax.random.split(jax.random.key(seed), 10)
    return {
        "ssm_input": centred(arg_keys[0], (SEQ, NH * P_SIZE), 1.0, 6.0, ((0, 128),)),
        "gate_input": centred(arg_keys[1], (SEQ, NH * P_SIZE), 1.0, 6.0, ((0, 128),)),
        "b_input": centred(arg_keys[2], (SEQ, NG * N), 0.5, 3.0, ((0, 128),)),
        "c_input": centred(arg_keys[3], (SEQ, NG * N), 0.5, 3.0, ((0, 128),)),
        "dt_raw": draw_dt_raw(jax.random.fold_in(arg_keys[9], 71), 0),
        "dt_bias": jnp.clip(jax.random.uniform(arg_keys[5], (NH,), jnp.float32, -0.25, 0.25), -0.25, 0.25),
        "a_log": draw_a_log(jax.random.fold_in(arg_keys[9], 71), 0),
        "skip_gain": jnp.clip(jax.random.uniform(arg_keys[7], (NH,), jnp.float32, 0.5, 1.5), 0.5, 1.5),
        "out_grad": centred(arg_keys[8], (SEQ, NH * P_SIZE), 1.0, 6.0, ((0, 128),)),
    }


HIGHEST = lax.Precision.HIGHEST


def decay_table(running, row_count):
    below_diag = jnp.arange(row_count)[:, None] >= jnp.arange(row_count)[None, :]
    inside = below_diag[:, :, None]
    spread = running[:, None, :] - running[None, :, :]
    return jnp.where(inside, jnp.exp(jnp.where(inside, spread, 0.0)), 0.0)


def reference(ssm_input, gate_input, b_input, c_input, dt_raw, dt_bias, a_log, skip_gain, out_grad):
    length = ssm_input.shape[0]
    per_group = NH // NG
    row_count = math.gcd(256, length)
    blocks = length // row_count
    col_width = per_group * P_SIZE
    gate_value = jax.nn.silu(gate_input.astype(jnp.float32))
    head_grad = (out_grad.astype(jnp.float32) * gate_value).astype(jnp.bfloat16)
    step_all = jax.nn.softplus(dt_raw.astype(jnp.float32) + dt_bias[None, :])
    rate_all = -step_all * jnp.exp(a_log)[None, :]

    def one_group(group_index):
        x_group = lax.dynamic_slice_in_dim(ssm_input, group_index * col_width, col_width, 1).astype(jnp.float32).reshape(blocks, row_count, per_group, P_SIZE)
        g_group = lax.dynamic_slice_in_dim(head_grad, group_index * col_width, col_width, 1).astype(jnp.float32).reshape(blocks, row_count, per_group, P_SIZE)
        b_group = lax.dynamic_slice_in_dim(b_input, group_index * N, N, 1).astype(jnp.float32).reshape(blocks, row_count, N)
        c_group = lax.dynamic_slice_in_dim(c_input, group_index * N, N, 1).astype(jnp.float32).reshape(blocks, row_count, N)
        dt_group = lax.dynamic_slice_in_dim(step_all, group_index * per_group, per_group, 1).reshape(blocks, row_count, per_group)
        rate_group = lax.dynamic_slice_in_dim(rate_all, group_index * per_group, per_group, 1).reshape(blocks, row_count, per_group)
        skip_group = lax.dynamic_slice_in_dim(skip_gain, group_index * per_group, per_group, 0)

        def forward(carried_state, block_items):
            x_block, b_block, c_block, dt_block, rate_block = block_items
            running = jnp.cumsum(rate_block, axis=0)
            block_total = running[-1]
            decays = decay_table(running, row_count)
            intersection = jnp.dot(c_block, b_block.T, precision=HIGHEST)
            weights = decays * intersection[:, :, None] * dt_block[None, :, :]
            mixed_part = jnp.einsum('tsh,shp->thp', weights, x_block, precision=HIGHEST)
            carried = jnp.einsum('tn,hnp->thp', c_block, carried_state, precision=HIGHEST)
            mixed_part = mixed_part + jnp.exp(running)[:, :, None] * carried
            to_end = (jnp.exp(block_total[None, :] - running) * dt_block)[:, :, None] * x_block
            state_next = jnp.exp(block_total)[:, None, None] * carried_state + jnp.einsum('sn,shp->hnp', b_block, to_end, precision=HIGHEST)
            return state_next, (mixed_part, carried_state)

        def backward(later_state, block_items):
            x_block, b_block, c_block, dt_block, rate_block, g_block, entering = block_items
            running = jnp.cumsum(rate_block, axis=0)
            block_total = running[-1]
            decays = decay_table(running, row_count)
            intersection = jnp.dot(c_block, b_block.T, precision=HIGHEST)
            joint = decays * intersection[:, :, None]
            dx_block = dt_block[:, :, None] * jnp.einsum('tsh,thp->shp', joint, g_block, precision=HIGHEST)
            inner = jnp.einsum('thp,shp->tsh', g_block, x_block, precision=HIGHEST)
            mass = jnp.sum(decays * dt_block[None, :, :] * inner, axis=2)
            from_start = jnp.exp(running)[:, :, None]
            to_end = (jnp.exp(block_total[None, :] - running) * dt_block)[:, :, None]
            dc_block = jnp.dot(mass, b_block, precision=HIGHEST) + jnp.einsum('thp,hnp->tn', from_start * g_block, entering, precision=HIGHEST)
            dx_block = dx_block + to_end * jnp.einsum('sn,hnp->shp', b_block, later_state, precision=HIGHEST)
            db_block = jnp.dot(mass.T, c_block, precision=HIGHEST) + jnp.einsum('shp,hnp->sn', to_end * x_block, later_state, precision=HIGHEST)
            later_next = jnp.einsum('tn,thp->hnp', c_block, from_start * g_block, precision=HIGHEST) + jnp.exp(block_total)[:, None, None] * later_state
            return later_next, (dx_block, db_block, dc_block)

        zero_state = jnp.zeros((per_group, N, P_SIZE), jnp.float32)
        unused, (mixed_blocks, entering_all) = lax.scan(forward, zero_state, (x_group, b_group, c_group, dt_group, rate_group))
        unused_back, (dx_blocks, db_blocks, dc_blocks) = lax.scan(backward, zero_state, (x_group, b_group, c_group, dt_group, rate_group, g_group, entering_all), reverse=True)
        mixed_all = (mixed_blocks + skip_group[None, None, :, None] * x_group).reshape(length, col_width)
        dx_all = (dx_blocks + skip_group[None, None, :, None] * g_group).reshape(length, col_width)
        return mixed_all, dx_all, db_blocks.reshape(length, N), dc_blocks.reshape(length, N)

    mixed_g, dx_g, db_g, dc_g = lax.map(one_group, jnp.arange(NG, dtype=jnp.int32))

    def side_by_side(stacked):
        return jnp.moveaxis(stacked, 0, 1).reshape(length, -1)

    mixed = side_by_side(mixed_g).astype(jnp.bfloat16)
    mixed = lax.optimization_barrier(mixed)
    gated_out = (mixed.astype(jnp.float32) * gate_value).astype(jnp.bfloat16)
    return gated_out, side_by_side(dx_g), side_by_side(db_g), side_by_side(dc_g)
```

```python
import functools

import jax
import jax.numpy as jnp
from jax import lax
from jax.experimental import pallas as pl
from jax.experimental.pallas import tpu as pltpu
from jax.sharding import PartitionSpec as P

NH = 128
P_SIZE = 64
N = 128
NG = 8
PER = NH // NG
W = PER * P_SIZE
T = 128
HALF = NG // 2
LANES = 128
WIDE = 2 * W + LANES
F32 = jnp.float32
BF16 = jnp.bfloat16


def params():
    return pltpu.CompilerParams(
        dimension_semantics=("arbitrary",), vmem_limit_bytes=48 * 1024 * 1024
    )


def lane(shape):
    return lax.broadcasted_iota(jnp.int32, shape, len(shape) - 1)


def fill_spread(e_ref):
    row = lax.broadcasted_iota(jnp.int32, (LANES, W), 0)
    col = lax.broadcasted_iota(jnp.int32, (LANES, W), 1)
    hit = ((row & (PER - 1)) == (col >> 6)) & (row < 2 * PER)
    e_ref[...] = jnp.where(hit, 1.0, 0.0).astype(BF16)


def to_front(values, group):
    return pltpu.roll(values, lax.rem(LANES - PER * group, LANES), 1)


def pair_up(front):
    high = front.astype(BF16).astype(F32)
    low = front - high
    where = lane(front.shape)
    return jnp.where(
        where < PER, high, jnp.where(where < 2 * PER, pltpu.roll(low, PER, 1), 0.0)
    ).astype(BF16)


def spread(values, group, e_ref):
    return jnp.dot(pair_up(to_front(values, group)), e_ref[...], preferred_element_type=F32)


def silu(v):
    return v * (0.5 * jnp.tanh(0.5 * v) + 0.5)


def steps_of(dt_ref, bias_ref, alog_ref):
    u = jnp.exp(dt_ref[...].astype(F32) + bias_ref[...])
    one = 1.0 + u
    step = jnp.where(one == 1.0, u, jnp.log(one) * (u / jnp.where(one == 1.0, 1.0, one - 1.0)))
    rate = -step * jnp.exp(alog_ref[...])
    row = lax.broadcasted_iota(jnp.int32, (T, T), 0)
    col = lax.broadcasted_iota(jnp.int32, (T, T), 1)
    tri = jnp.where(row >= col, 1.0, 0.0).astype(BF16)
    running = jnp.zeros((T, NH), F32)
    for _ in range(3):
        piece = rate.astype(BF16)
        running = running + jnp.dot(tri, piece, preferred_element_type=F32)
        rate = rate - piece.astype(F32)
    from_start = jnp.exp(running)
    to_end = jnp.exp(running[T - 1 : T] - running) * step
    return step, running, from_start, to_end


def states_kernel(first, sc_ref, *refs):
    if first:
        dt_ref, bias_ref, alog_ref, x_ref, z_ref, og_ref, b_ref, c_ref = refs[:8]
        st_ref, hg_ref, aux_ref, e_ref = refs[8:]
    else:
        aux_ref, x_ref, z_ref, og_ref, b_ref, c_ref = refs[:6]
        st_ref, hg_ref, e_ref = refs[6:]
    i = pl.program_id(0)
    group = sc_ref[0] + i

    @pl.when(i == 0)
    def _():
        fill_spread(e_ref)
        if first:
            for k, v in enumerate(steps_of(dt_ref, bias_ref, alog_ref)):
                aux_ref[k] = v

    from_start = aux_ref[2]
    to_end = aux_ref[3]
    head_grad = (og_ref[...].astype(F32) * silu(z_ref[...].astype(F32))).astype(BF16)
    hg_ref[...] = head_grad
    xs = (x_ref[...].astype(F32) * spread(to_end, group, e_ref)).astype(BF16)
    st_ref[:, :W] = jnp.dot(b_ref[...].T, xs, preferred_element_type=F32).astype(BF16)
    gs = (head_grad.astype(F32) * spread(from_start, group, e_ref)).astype(BF16)
    st_ref[:, W : 2 * W] = jnp.dot(c_ref[...].T, gs, preferred_element_type=F32).astype(BF16)
    decay = jnp.broadcast_to(from_start[T - 1 : T], (8, NH))
    decay = pair_up(to_front(decay, group)).astype(F32)
    st_ref[:, 2 * W :] = jnp.broadcast_to(decay[0:1], (N, LANES)).astype(BF16)


def cols(i, sc):
    return (0, sc[0] + i)


def whole2(i, sc):
    return (0, 0)


def whole3(i, sc):
    return (0, 0, 0)


def rows(i, sc):
    return (i, 0)


TOKEN_BLOCK = pl.BlockSpec((T, W), cols)
BC_BLOCK = pl.BlockSpec((T, N), cols)
AUX_BLOCK = pl.BlockSpec((4, T, NH), whole3)
ROW_BLOCK = pl.BlockSpec((1, NH), whole2)
STATE_BLOCK = pl.BlockSpec((N, WIDE), rows)
EL_BLOCK = pl.BlockSpec((N, 2 * W), rows)
LOCAL_BLOCK = pl.BlockSpec((T, W), lambda i, sc: (0, i))
LOCAL_BC = pl.BlockSpec((T, N), lambda i, sc: (0, i))
SPREAD = pltpu.VMEM((LANES, W), BF16)


def states(first, sc, *args):
    out_shape = [
        jax.ShapeDtypeStruct((HALF * N, WIDE), BF16),
        jax.ShapeDtypeStruct((T, HALF * W), BF16),
    ]
    out_specs = [STATE_BLOCK, LOCAL_BLOCK]
    if first:
        in_specs = [pl.BlockSpec((T, NH), whole2), ROW_BLOCK, ROW_BLOCK]
        out_shape.append(jax.ShapeDtypeStruct((4, T, NH), F32))
        out_specs.append(AUX_BLOCK)
    else:
        in_specs = [AUX_BLOCK]
    in_specs += [TOKEN_BLOCK] * 3 + [BC_BLOCK] * 2
    return pl.pallas_call(
        functools.partial(states_kernel, first),
        grid_spec=pltpu.PrefetchScalarGridSpec(
            num_scalar_prefetch=1,
            grid=(HALF,),
            in_specs=in_specs,
            out_specs=out_specs,
            scratch_shapes=[SPREAD],
        ),
        out_shape=out_shape,
        compiler_params=params(),
        name="states_send" if first else "states_keep",
    )(sc, *args)


def decay_row(state_ref, e_ref):
    return jnp.dot(state_ref[0:16, 2 * W :], e_ref[...], preferred_element_type=F32)[0:1]


def merge_kernel(sc_ref, own_ref, got_ref, out_ref, e_ref):
    @pl.when(pl.program_id(0) == 0)
    def _():
        fill_spread(e_ref)

    def merge(r0, r1):
        d0 = decay_row(r0, e_ref)
        d1 = decay_row(r1, e_ref)
        forward = d1 * r0[:, :W].astype(F32) + r1[:, :W].astype(F32)
        backward = r0[:, W : 2 * W].astype(F32) + d0 * r1[:, W : 2 * W].astype(F32)
        out_ref[:, :, :W] = forward.reshape(N // 8, 8, W).astype(BF16)
        out_ref[:, :, W : 2 * W] = backward.reshape(N // 8, 8, W).astype(BF16)
        p0 = r0[0:16, 2 * W :].astype(F32)
        p1 = r1[0:16, 2 * W :].astype(F32)
        p0 = p0 + pltpu.roll(p0, LANES - PER, 1)
        p1 = p1 + pltpu.roll(p1, LANES - PER, 1)
        both = pair_up(p0 * p1).astype(F32)[0:8]
        out_ref[:, :, 2 * W :] = jnp.broadcast_to(both[None], (N // 8, 8, LANES)).astype(BF16)

    @pl.when(sc_ref[1] == 0)
    def _():
        merge(own_ref, got_ref)

    @pl.when(sc_ref[1] != 0)
    def _():
        merge(got_ref, own_ref)


def merge(sc, own, got):
    return pl.pallas_call(
        merge_kernel,
        grid_spec=pltpu.PrefetchScalarGridSpec(
            num_scalar_prefetch=1,
            grid=(HALF,),
            in_specs=[STATE_BLOCK, STATE_BLOCK],
            out_specs=pl.BlockSpec((N // 8, 8, WIDE), lambda i, sc: (i, 0, 0)),
            scratch_shapes=[SPREAD],
        ),
        out_shape=jax.ShapeDtypeStruct((HALF * N // 8, 8, WIDE), BF16),
        compiler_params=params(),
        name="merge_cores",
    )(sc, own, got)


def scan_kernel(chips, in_ref, after_ref, out_ref, e_ref, d_ref):
    fill_spread(e_ref)
    pairs = in_ref[:, :, 2 * W :].astype(F32).reshape(chips * 8, LANES).astype(BF16)
    d_ref[...] = jnp.dot(pairs, e_ref[...], preferred_element_type=F32).reshape(chips, 8, W)

    def step(k, carry):
        e, l = carry
        out_ref[k, :, :W] = e.astype(BF16)
        e = d_ref[k] * e + in_ref[k, :, :W].astype(F32)
        j = chips - 1 - k
        out_ref[j, :, W:] = l.astype(BF16)
        l = d_ref[j] * l + in_ref[j, :, W : 2 * W].astype(F32)
        return e, l

    zero = jnp.zeros((8, W), F32)
    lax.fori_loop(0, chips, step, (zero, zero), unroll=4)


def scan(parts, after):
    chips = parts.shape[0]
    return pl.pallas_call(
        functools.partial(scan_kernel, chips),
        in_specs=[pl.BlockSpec(memory_space=pltpu.VMEM), pl.BlockSpec(memory_space=pl.ANY)],
        out_specs=pl.BlockSpec(memory_space=pltpu.VMEM),
        out_shape=jax.ShapeDtypeStruct((chips, 8, 2 * W), BF16),
        scratch_shapes=[SPREAD, pltpu.VMEM((chips, 8, W), F32)],
        compiler_params=pltpu.CompilerParams(vmem_limit_bytes=48 * 1024 * 1024),
        name="scan_chips",
    )(parts, after)


def pass_on_kernel(sc_ref, el_ref, own_ref, after_ref, out_ref, e_ref):
    @pl.when(pl.program_id(0) == 0)
    def _():
        fill_spread(e_ref)

    d = decay_row(own_ref, e_ref)

    @pl.when(sc_ref[1] == 0)
    def _():
        e = d * el_ref[:, :W].astype(F32) + own_ref[:, :W].astype(F32)
        out_ref[:, :W] = e.astype(BF16)
        out_ref[:, W:] = el_ref[:, W:]

    @pl.when(sc_ref[1] != 0)
    def _():
        l = d * el_ref[:, W:].astype(F32) + own_ref[:, W : 2 * W].astype(F32)
        out_ref[:, :W] = el_ref[:, :W]
        out_ref[:, W:] = l.astype(BF16)


def pass_on(sc, el, own, after):
    return pl.pallas_call(
        pass_on_kernel,
        grid_spec=pltpu.PrefetchScalarGridSpec(
            num_scalar_prefetch=1,
            grid=(HALF,),
            in_specs=[EL_BLOCK, STATE_BLOCK, pl.BlockSpec(memory_space=pl.ANY)],
            out_specs=EL_BLOCK,
            scratch_shapes=[SPREAD],
        ),
        out_shape=jax.ShapeDtypeStruct((HALF * N, 2 * W), BF16),
        compiler_params=params(),
        name="pass_on",
    )(sc, el, own, after)


NT = (((1,), (1,)), ((), ()))


def local_kernel(
    sc_ref, aux_ref, skip_ref, x_ref, hg_ref, b_ref, c_ref, y_ref, dx_ref, db_ref, dc_ref, e_ref, runt_ref, stept_ref
):
    i = pl.program_id(0)
    group = sc_ref[0] + i

    @pl.when(i == 0)
    def _():
        fill_spread(e_ref)
        stept_ref[...] = aux_ref[0].T
        runt_ref[...] = aux_ref[1].T

    first = pl.multiple_of(group * PER, PER)
    run_rows = runt_ref[pl.ds(first, PER), :]
    step_rows = stept_ref[pl.ds(first, PER), :]
    run_cols = to_front(aux_ref[1], group)
    skip = spread(jnp.broadcast_to(skip_ref[...], (8, NH)), group, e_ref)[0:1]
    b, c = b_ref[...], c_ref[...]
    cb = lax.dot_general(c, b, NT, preferred_element_type=F32)
    row = lax.broadcasted_iota(jnp.int32, (T, T), 0)
    col = lax.broadcasted_iota(jnp.int32, (T, T), 1)
    below = row >= col
    left = col < P_SIZE
    mass = jnp.zeros((T, T), F32)
    for pair in range(PER // 2):
        here = slice(pair * LANES, (pair + 1) * LANES)
        x = x_ref[:, here]
        g = hg_ref[:, here]
        ys, dxs = [], []
        for k in range(2):
            j = 2 * pair + k
            gap = run_cols[:, j : j + 1] - run_rows[j : j + 1, :]
            weight = jnp.exp(jnp.where(below, gap, -1e30)) * step_rows[j : j + 1, :]
            mine = left if k == 0 else ~left
            inner = lax.dot_general(
                jnp.where(mine, g, jnp.zeros_like(g)), x, NT, preferred_element_type=F32
            )
            mass = mass + weight * inner
            joint = (weight * cb).astype(BF16)
            ys.append(jnp.dot(joint, x, preferred_element_type=F32))
            dxs.append(jnp.dot(joint.T, g, preferred_element_type=F32))
        y_ref[:, here] = jnp.where(left, ys[0], ys[1]) + skip[:, here] * x.astype(F32)
        dx_ref[:, here] = jnp.where(left, dxs[0], dxs[1]) + skip[:, here] * g.astype(F32)
    high = mass.astype(BF16)
    low = (mass - high.astype(F32)).astype(BF16)
    dc_ref[...] = jnp.dot(high, b, preferred_element_type=F32) + jnp.dot(
        low, b, preferred_element_type=F32
    )
    db_ref[...] = jnp.dot(high.T, c, preferred_element_type=F32) + jnp.dot(
        low.T, c, preferred_element_type=F32
    )


def local(name, sc, aux, skip, x, hg, b, c):
    return pl.pallas_call(
        local_kernel,
        grid_spec=pltpu.PrefetchScalarGridSpec(
            num_scalar_prefetch=1,
            grid=(HALF,),
            in_specs=[AUX_BLOCK, ROW_BLOCK, TOKEN_BLOCK, LOCAL_BLOCK, BC_BLOCK, BC_BLOCK],
            out_specs=[LOCAL_BLOCK, LOCAL_BLOCK, LOCAL_BC, LOCAL_BC],
            scratch_shapes=[SPREAD, pltpu.VMEM((NH, T), F32), pltpu.VMEM((NH, T), F32)],
        ),
        out_shape=[
            jax.ShapeDtypeStruct((T, HALF * W), F32),
            jax.ShapeDtypeStruct((T, HALF * W), F32),
            jax.ShapeDtypeStruct((T, HALF * N), F32),
            jax.ShapeDtypeStruct((T, HALF * N), F32),
        ],
        compiler_params=params(),
        name=name,
    )(sc, aux, skip, x, hg, b, c)


def final_kernel(own, sc_ref, *refs):
    aux_ref, x_ref, hg_ref, z_ref, b_ref, c_ref, yl_ref, dxl_ref, dbl_ref, dcl_ref, el_ref = refs[:11]
    if own:
        got_ref, out_ref, dx_ref, db_ref, dc_ref, e_ref, cur_ref = refs[11:]
    else:
        out_ref, dx_ref, db_ref, dc_ref, e_ref = refs[15:]
        cur_ref = el_ref
    i = pl.program_id(0)
    group = sc_ref[0] + i

    @pl.when(i == 0)
    def _():
        fill_spread(e_ref)

    if own:
        d = decay_row(got_ref, e_ref)

        @pl.when(sc_ref[1] == 0)
        def _():
            l = d * el_ref[:, W:].astype(F32) + got_ref[:, W : 2 * W].astype(F32)
            cur_ref[:, :W] = el_ref[:, :W]
            cur_ref[:, W:] = l.astype(BF16)

        @pl.when(sc_ref[1] != 0)
        def _():
            e = d * el_ref[:, :W].astype(F32) + got_ref[:, :W].astype(F32)
            cur_ref[:, :W] = e.astype(BF16)
            cur_ref[:, W:] = el_ref[:, W:]

    entering = cur_ref[:, :W]
    later = cur_ref[:, W:]
    from_start = spread(aux_ref[2], group, e_ref)
    to_end = spread(aux_ref[3], group, e_ref)
    b, c = b_ref[...], c_ref[...]
    mixed = yl_ref[...] + from_start * jnp.dot(c, entering, preferred_element_type=F32)
    out_ref[...] = (mixed.astype(BF16).astype(F32) * silu(z_ref[...].astype(F32))).astype(BF16)
    dx_ref[...] = dxl_ref[...] + to_end * jnp.dot(b, later, preferred_element_type=F32)
    xs = (x_ref[...].astype(F32) * to_end).astype(BF16)
    gs = (hg_ref[...].astype(F32) * from_start).astype(BF16)
    db_ref[...] = dbl_ref[...] + lax.dot_general(xs, later, NT, preferred_element_type=F32)
    dc_ref[...] = dcl_ref[...] + lax.dot_general(gs, entering, NT, preferred_element_type=F32)


def final(own, sc, aux, x, hg, z, b, c, local_parts, el, extra):
    in_specs = [AUX_BLOCK, TOKEN_BLOCK, LOCAL_BLOCK, TOKEN_BLOCK, BC_BLOCK, BC_BLOCK]
    in_specs += [LOCAL_BLOCK, LOCAL_BLOCK, LOCAL_BC, LOCAL_BC, EL_BLOCK]
    scratch = [SPREAD]
    aliases = {}
    if own:
        in_specs.append(STATE_BLOCK)
        scratch.append(pltpu.VMEM((N, 2 * W), BF16))
    else:
        aliases = {1 + len(in_specs) + k: k for k in range(4)}
        in_specs += [pl.BlockSpec(memory_space=pl.ANY)] * 4
    return pl.pallas_call(
        functools.partial(final_kernel, own),
        grid_spec=pltpu.PrefetchScalarGridSpec(
            num_scalar_prefetch=1,
            grid=(HALF,),
            in_specs=in_specs,
            out_specs=[TOKEN_BLOCK, TOKEN_BLOCK, BC_BLOCK, BC_BLOCK],
            scratch_shapes=scratch,
        ),
        out_shape=[
            jax.ShapeDtypeStruct((T, NH * P_SIZE), BF16),
            jax.ShapeDtypeStruct((T, NH * P_SIZE), F32),
            jax.ShapeDtypeStruct((T, NG * N), F32),
            jax.ShapeDtypeStruct((T, NG * N), F32),
        ],
        input_output_aliases=aliases,
        compiler_params=params(),
        name="final_own" if own else "final_other",
    )(sc, aux, x, hg, z, b, c, *local_parts, el, *extra)


def body(ssm_input, gate_input, b_input, c_input, dt_raw, dt_bias, a_log, skip_gain, out_grad):
    ctx_count = lax.axis_size("ctx")
    head_count = lax.axis_size("head")
    core = (lax.axis_index("head") % 2).astype(jnp.int32)
    sc_other = jnp.stack([HALF * (1 - core), core])
    sc_own = jnp.stack([HALF * core, core])
    bias, alog, skip = dt_bias[None, :], a_log[None, :], skip_gain[None, :]
    swap = [(k, k ^ 1) for k in range(head_count)]
    chips = [[2 * k + c for k in range(ctx_count * head_count // 2)] for c in range(2)]

    def exchange(parts):
        return lax.all_to_all(
            parts, ("ctx", "head"), split_axis=0, concat_axis=0, tiled=True, axis_index_groups=chips
        )

    tokens = (ssm_input, gate_input, out_grad, b_input, c_input)
    send, hg_other, aux = states(True, sc_other, dt_raw, bias, alog, *tokens)
    got = lax.ppermute(send, "head", swap)
    keep, hg_own = states(False, sc_own, aux, *tokens)
    gathered = exchange(merge(sc_own, keep, got))
    loc_own = local("local_own", sc_own, aux, skip, ssm_input, hg_own, b_input, c_input)
    back = exchange(scan(gathered, loc_own[3]))
    loc_other = local("local_other", sc_other, aux, skip, ssm_input, hg_other, b_input, c_input)
    el = back.reshape(HALF * N, 2 * W)
    el_other = lax.ppermute(pass_on(sc_own, el, keep, loc_other[3]), "head", swap)
    shared = (gate_input, b_input, c_input)
    outs = final(True, sc_own, aux, ssm_input, hg_own, *shared, loc_own, el, (got,))
    return tuple(
        final(False, sc_other, aux, ssm_input, hg_other, *shared, loc_other, el_other, tuple(outs))
    )


def solution(mesh):
    row_spec = P(("ctx", "head"), None)
    in_specs = (row_spec,) * 5 + (P(), P(), P(), row_spec)
    return jax.shard_map(
        body, mesh=mesh, in_specs=in_specs, out_specs=(row_spec,) * 4, check_vma=False
    )
```

```python
import functools

import jax
import jax.numpy as jnp
from jax import lax
from jax.experimental import pallas as pl
from jax.experimental.pallas import tpu as pltpu
from jax.sharding import PartitionSpec as P

NH = 128
P_SIZE = 64
N = 128
NG = 8
PER = NH // NG
W = PER * P_SIZE
T = 128
HALF = NG // 2
LANES = 128
WIDE = 2 * W + LANES
F32 = jnp.float32
BF16 = jnp.bfloat16


MIB = 1024 * 1024
NT = (((1,), (1,)), ((), ()))
CHUNK = 256
HBM_SPEC = pl.BlockSpec(memory_space=pl.ANY)
VMEM_SPEC = pl.BlockSpec(memory_space=pltpu.VMEM)
SMEM_SPEC = pl.BlockSpec(memory_space=pltpu.SMEM)
SPREAD = pltpu.VMEM((LANES, W), BF16)


def in_hbm(values):
    return pltpu.with_memory_space_constraint(values, pltpu.HBM)


def params(mib):
    return pltpu.CompilerParams(vmem_limit_bytes=mib * MIB)


def lane(shape):
    return lax.broadcasted_iota(jnp.int32, shape, len(shape) - 1)


def fill_spread(e_ref):
    row = lax.broadcasted_iota(jnp.int32, (LANES, W), 0)
    col = lax.broadcasted_iota(jnp.int32, (LANES, W), 1)
    e_ref[...] = jnp.where((row & 63) == (col >> 6), 1.0, 0.0).astype(BF16)


def to_half(values, base):
    return pltpu.roll(values, lax.rem(LANES - PER * base, LANES), 1)


def pair_up(values):
    high = values.astype(BF16).astype(F32)
    low = values - high
    return jnp.where(lane(values.shape) < 64, high, pltpu.roll(low, 64, 1))


def of_group(pairs, i):
    if i:
        pairs = pltpu.roll(pairs, LANES - PER * i, 1)
    return pairs.astype(BF16)


def silu(v):
    return v * (0.5 * jnp.tanh(0.5 * v) + 0.5)


def steps_of(dt_ref, bias_ref, alog_ref):
    u = jnp.exp(dt_ref[...].astype(F32) + bias_ref[...])
    one = 1.0 + u
    step = jnp.where(one == 1.0, u, jnp.log(one) * (u / jnp.where(one == 1.0, 1.0, one - 1.0)))
    rate = -step * jnp.exp(alog_ref[...])
    row = lax.broadcasted_iota(jnp.int32, (T, T), 0)
    col = lax.broadcasted_iota(jnp.int32, (T, T), 1)
    tri = jnp.where(row >= col, 1.0, 0.0).astype(BF16)
    running = jnp.zeros((T, NH), F32)
    for _ in range(3):
        piece = rate.astype(BF16)
        running = running + jnp.dot(tri, piece, preferred_element_type=F32)
        rate = rate - piece.astype(F32)
    from_start = jnp.exp(running)
    to_end = jnp.exp(running[T - 1 : T] - running) * step
    return step, running, from_start, to_end


def columns(base, i, width):
    return pl.ds(pl.multiple_of((base + i) * width, width), width)


def states_kernel(first, sc_ref, *refs):
    if first:
        dt_hbm, bias_hbm, alog_hbm, x_hbm, z_hbm, og_hbm, b_hbm, c_hbm, st_hbm, aux_hbm = refs[:10]
        small = ((dt_hbm, refs[-3]), (bias_hbm, refs[-2]), (alog_hbm, refs[-1]))
    else:
        aux_hbm, x_hbm, z_hbm, og_hbm, b_hbm, c_hbm, st_hbm = refs[:7]
    e_ref, x_ref, z_ref, og_ref, b_ref, c_ref, st_ref, aux_ref, sem, sem_out, sem_small = refs[
        (10 if first else 7) : (21 if first else 18)
    ]
    base = sc_ref[0]
    if not first:
        small = ((aux_hbm, aux_ref),)
    smalls = [pltpu.make_async_copy(s, d, sem_small.at[k]) for k, (s, d) in enumerate(small)]
    for copy in smalls:
        copy.start()
    copies = []
    for i in range(HALF):
        row = []
        for k, (src, dst, width) in enumerate(
            (
                (b_hbm, b_ref, N),
                (x_hbm, x_ref, W),
                (c_hbm, c_ref, N),
                (z_hbm, z_ref, W),
                (og_hbm, og_ref, W),
            )
        ):
            row.append(
                pltpu.make_async_copy(src.at[:, columns(base, i, width)], dst.at[i], sem.at[i, k])
            )
            row[-1].start()
        copies.append(row)
    fill_spread(e_ref)
    for copy in smalls:
        copy.wait()
    stores = []
    if first:
        for k, v in enumerate(steps_of(refs[-3], refs[-2], refs[-1])):
            aux_ref[k] = v
        stores.append(pltpu.make_async_copy(aux_ref, aux_hbm, sem_small.at[3]))
        stores[0].start()
    from_start = pair_up(to_half(aux_ref[2], base))
    to_end = pair_up(to_half(aux_ref[3], base))
    for i in range(HALF):
        for copy in copies[i]:
            copy.wait()
        here = slice(i * N, (i + 1) * N)
        te = of_group(to_end, i)
        fs = of_group(from_start, i)
        bt = b_ref[i].T
        ct = c_ref[i].T
        for k in range(W // CHUNK):
            cut = slice(k * CHUNK, (k + 1) * CHUNK)
            e = e_ref[:, cut]
            xs = x_ref[i, :, cut].astype(F32) * jnp.dot(te, e, preferred_element_type=F32)
            st_ref[here, cut] = jnp.dot(
                bt, xs.astype(BF16), preferred_element_type=F32
            ).astype(BF16)
            gate = silu(z_ref[i, :, cut].astype(F32))
            hg = (og_ref[i, :, cut].astype(F32) * gate).astype(BF16)
            gs = hg.astype(F32) * jnp.dot(fs, e, preferred_element_type=F32)
            st_ref[here, slice(W + k * CHUNK, W + (k + 1) * CHUNK)] = jnp.dot(
                ct, gs.astype(BF16), preferred_element_type=F32
            ).astype(BF16)
        decay = jnp.broadcast_to(fs[T - 16 : T].astype(F32)[15:16], (N, LANES))
        st_ref[here, 2 * W :] = decay.astype(BF16)
        stores.append(pltpu.make_async_copy(st_ref.at[here], st_hbm.at[here], sem_out.at[i]))
        stores[-1].start()
    for store in stores:
        store.wait()


def states(first, sc, *args):
    out_shape = [pltpu.HBM((HALF * N, WIDE), BF16)]
    scratch = (
        [SPREAD]
        + [pltpu.VMEM((HALF, T, W), BF16)] * 3
        + [pltpu.VMEM((HALF, T, N), BF16)] * 2
        + [pltpu.VMEM((HALF * N, WIDE), BF16), pltpu.VMEM((4, T, NH), F32)]
        + [pltpu.SemaphoreType.DMA((HALF, 5)), pltpu.SemaphoreType.DMA((HALF,))]
        + [pltpu.SemaphoreType.DMA((4,))]
    )
    if first:
        out_shape.append(pltpu.HBM((4, T, NH), F32))
        scratch += [pltpu.VMEM((T, NH), BF16), pltpu.VMEM((1, NH), F32), pltpu.VMEM((1, NH), F32)]
    return pl.pallas_call(
        functools.partial(states_kernel, first),
        in_specs=[SMEM_SPEC] + [HBM_SPEC] * len(args),
        out_specs=[HBM_SPEC] * len(out_shape),
        out_shape=out_shape,
        scratch_shapes=scratch,
        compiler_params=params(24),
        name="states_send" if first else "states_keep",
    )(sc, *[in_hbm(a) for a in args])


def decay_row(state_ref, at, e_ref):
    pairs = state_ref[at : at + 16, 2 * W :]
    return jnp.dot(pairs, e_ref[...], preferred_element_type=F32)[0:1]


def merge_kernel(sc_ref, own_hbm, got_hbm, out_hbm, e_ref, own_ref, got_ref, out_ref, sem, sem_out):
    loads = []
    for i in range(HALF):
        here = slice(i * N, (i + 1) * N)
        pair = (
            pltpu.make_async_copy(own_hbm.at[here], own_ref.at[here], sem.at[i, 0]),
            pltpu.make_async_copy(got_hbm.at[here], got_ref.at[here], sem.at[i, 1]),
        )
        for copy in pair:
            copy.start()
        loads.append(pair)
    fill_spread(e_ref)

    def merge(r0, r1):
        stores = []
        for i in range(HALF):
            for copy in loads[i]:
                copy.wait()
            here = slice(i * N, (i + 1) * N)
            there = slice(i * N // 8, (i + 1) * N // 8)
            d0 = decay_row(r0, i * N, e_ref)
            d1 = decay_row(r1, i * N, e_ref)
            for k in range(W // CHUNK):
                cut = slice(k * CHUNK, (k + 1) * CHUNK)
                forward = d1[:, cut] * r0[here, cut].astype(F32) + r1[here, cut].astype(F32)
                out_ref[there, :, cut] = forward.reshape(N // 8, 8, CHUNK).astype(BF16)
                back = slice(W + k * CHUNK, W + (k + 1) * CHUNK)
                backward = r0[here, back].astype(F32) + d0[:, cut] * r1[here, back].astype(F32)
                out_ref[there, :, back] = backward.reshape(N // 8, 8, CHUNK).astype(BF16)
            p0 = r0[i * N : i * N + 16, 2 * W :].astype(F32)
            p1 = r1[i * N : i * N + 16, 2 * W :].astype(F32)
            p0 = p0 + pltpu.roll(p0, 64, 1)
            p1 = p1 + pltpu.roll(p1, 64, 1)
            both = pair_up(p0 * p1)[0:8]
            both = jnp.broadcast_to(both[None], (N // 8, 8, LANES))
            out_ref[there, :, 2 * W :] = both.astype(BF16)
            stores.append(pltpu.make_async_copy(out_ref.at[there], out_hbm.at[there], sem_out.at[i]))
            stores[-1].start()
        for store in stores:
            store.wait()

    @pl.when(sc_ref[1] == 0)
    def _():
        merge(own_ref, got_ref)

    @pl.when(sc_ref[1] != 0)
    def _():
        merge(got_ref, own_ref)


def merge(sc, own, got):
    return pl.pallas_call(
        merge_kernel,
        in_specs=[SMEM_SPEC, HBM_SPEC, HBM_SPEC],
        out_specs=HBM_SPEC,
        out_shape=pltpu.HBM((HALF * N // 8, 8, WIDE), BF16),
        scratch_shapes=[
            SPREAD,
            pltpu.VMEM((HALF * N, WIDE), BF16),
            pltpu.VMEM((HALF * N, WIDE), BF16),
            pltpu.VMEM((HALF * N // 8, 8, WIDE), BF16),
            pltpu.SemaphoreType.DMA((HALF, 2)),
            pltpu.SemaphoreType.DMA((HALF,)),
        ],
        compiler_params=params(16),
        name="merge_cores",
    )(sc, in_hbm(own), in_hbm(got))


def scan_kernel(chips, in_ref, after_ref, out_hbm, e_ref, d_ref, out_ref, sem):
    fill_spread(e_ref)
    pairs = in_ref[:, :, 2 * W :].astype(F32).reshape(chips * 8, LANES).astype(BF16)
    d_ref[...] = jnp.dot(pairs, e_ref[...], preferred_element_type=F32).reshape(chips, 8, W)
    zero = jnp.zeros((8, W), F32)

    def forward(k, e):
        out_ref[k, :, :W] = e.astype(BF16)
        return d_ref[k] * e + in_ref[k, :, :W].astype(F32)

    def backward(k, l):
        j = chips - 1 - k
        out_ref[j, :, W:] = l.astype(BF16)
        return d_ref[j] * l + in_ref[j, :, W : 2 * W].astype(F32)

    parts = ((0, chips, slice(0, W)), (chips // 2, chips, slice(W, 2 * W)), (0, chips // 2, slice(W, 2 * W)))
    stores = [
        pltpu.make_async_copy(out_ref.at[a:b, :, cut], out_hbm.at[a:b, :, cut], sem.at[k])
        for k, (a, b, cut) in enumerate(parts)
    ]
    lax.fori_loop(0, chips, forward, zero, unroll=8)
    stores[0].start()
    l = lax.fori_loop(0, chips // 2, backward, zero, unroll=8)
    stores[1].start()
    lax.fori_loop(chips // 2, chips, backward, l, unroll=8)
    stores[2].start()
    for store in stores:
        store.wait()


def scan(parts, after):
    chips = parts.shape[0]
    return pl.pallas_call(
        functools.partial(scan_kernel, chips),
        in_specs=[VMEM_SPEC, HBM_SPEC],
        out_specs=HBM_SPEC,
        out_shape=pltpu.HBM((chips, 8, 2 * W), BF16),
        scratch_shapes=[
            SPREAD,
            pltpu.VMEM((chips, 8, W), F32),
            pltpu.VMEM((chips, 8, 2 * W), BF16),
            pltpu.SemaphoreType.DMA((3,)),
        ],
        compiler_params=params(16),
        name="scan_chips",
    )(parts, in_hbm(after))


def local_kernel(
    sc_ref, aux_ref, skip_ref, got_ref, x_hbm, z_hbm, og_hbm, b_hbm, c_hbm,
    y_ref, dx_ref, xs_ref, gs_ref, pair_ref, db_ref, dc_ref,
    e_ref, x_ref, z_ref, og_ref, b_ref, c_ref, ysum_ref, dxsum_ref, hg_ref,
    runc_ref, run_ref, step_ref, plain_ref, sem,
):
    base = sc_ref[0]
    core = sc_ref[1]
    copies = []
    for i in range(HALF):
        for k, (src, dst, width) in enumerate(
            (
                (x_hbm, x_ref, W),
                (z_hbm, z_ref, W),
                (og_hbm, og_ref, W),
                (b_hbm, b_ref, N),
                (c_hbm, c_ref, N),
            )
        ):
            copies.append(
                pltpu.make_async_copy(src.at[:, columns(base, i, width)], dst.at[i], sem.at[i, k])
            )
            copies[-1].start()
    fill_spread(e_ref)
    start = to_half(aux_ref[2], base)
    end = to_half(aux_ref[3], base)
    gain = to_half(jnp.broadcast_to(skip_ref[...], (16, NH)), base)
    run = to_half(aux_ref[1], base)
    run_t = run.T
    step_t = to_half(aux_ref[0], base).T
    for i in range(HALF):
        decay = got_ref[i * N : i * N + 16, 2 * W :].astype(F32)
        decay = (decay + pltpu.roll(decay, 64, 1))[0:1]
        fs, te, skip, run_c = [pltpu.roll(v, LANES - PER * i, 1) if i else v for v in (start, end, gain, run)]
        plain_ref[i, 0:T] = pair_up(fs).astype(BF16)
        plain_ref[i, T : 2 * T] = pair_up(te).astype(BF16)
        plain_ref[i, 2 * T : 2 * T + 16] = pair_up(skip).astype(BF16)
        pair_ref[i, 0:T] = pair_up(jnp.where(core == 0, fs, fs * decay)).astype(BF16)
        pair_ref[i, T : 2 * T] = pair_up(jnp.where(core == 0, te * decay, te)).astype(BF16)
        runc_ref[i] = run_c
        run_ref[i] = run_t[i * PER : (i + 1) * PER]
        step_ref[i] = step_t[i * PER : (i + 1) * PER]
    for copy in copies:
        copy.wait()
    row = lax.broadcasted_iota(jnp.int32, (T, T), 0)
    col = lax.broadcasted_iota(jnp.int32, (T, T), 1)
    below = row >= col
    left = col < P_SIZE

    def one_group(i, unused):
        b, c = b_ref[i], c_ref[i]
        cb = lax.dot_general(c, b, NT, preferred_element_type=F32)
        run_cols, run_rows, step_rows = runc_ref[i], run_ref[i], step_ref[i]
        mass = jnp.zeros((T, T), F32)
        for pair in range(PER // 2):
            here = slice(pair * LANES, (pair + 1) * LANES)
            e = e_ref[:, here]
            both = jnp.dot(pair_ref[i], e, preferred_element_type=F32)
            skip = jnp.dot(plain_ref[i, 2 * T : 2 * T + 16], e, preferred_element_type=F32)[0:1]
            x = x_ref[i, :, here]
            g = (og_ref[i, :, here].astype(F32) * silu(z_ref[i, :, here].astype(F32))).astype(BF16)
            hg_ref[:, here] = g
            gs_ref[i, :, here] = (g.astype(F32) * both[0:T]).astype(BF16)
            xs_ref[i, :, here] = (x.astype(F32) * both[T : 2 * T]).astype(BF16)
            ys, dxs = [], []
            for k in range(2):
                j = 2 * pair + k
                gap = run_cols[:, j : j + 1] - run_rows[j : j + 1, :]
                weight = jnp.exp(jnp.where(below, gap, -1e30)) * step_rows[j : j + 1, :]
                mine = left if k == 0 else ~left
                inner = lax.dot_general(
                    jnp.where(mine, g, jnp.zeros_like(g)), x, NT, preferred_element_type=F32
                )
                mass = mass + weight * inner
                joint = (weight * cb).astype(BF16)
                ys.append(jnp.dot(joint, x, preferred_element_type=F32))
                dxs.append(jnp.dot(joint.T, g, preferred_element_type=F32))
            ysum_ref[:, here] = jnp.where(left, ys[0], ys[1]) + skip * x.astype(F32)
            dxsum_ref[:, here] = jnp.where(left, dxs[0], dxs[1]) + skip * g.astype(F32)
        high = mass.astype(BF16)
        low = (mass - high.astype(F32)).astype(BF16)
        dc_ref[i] = jnp.dot(high, b, preferred_element_type=F32) + jnp.dot(
            low, b, preferred_element_type=F32
        )
        db_ref[i] = jnp.dot(high.T, c, preferred_element_type=F32) + jnp.dot(
            low.T, c, preferred_element_type=F32
        )
        rows = pl.ds(pl.multiple_of(i * N, N), N)

        @pl.when(core != 0)
        def _():
            partner = got_ref[rows, :W]
            fs = jnp.dot(plain_ref[i, 0:T], e_ref[...], preferred_element_type=F32)
            ysum_ref[...] += fs * jnp.dot(c, partner, preferred_element_type=F32)
            gs = (hg_ref[...].astype(F32) * fs).astype(BF16)
            dc_ref[i] += lax.dot_general(gs, partner, NT, preferred_element_type=F32)

        @pl.when(core == 0)
        def _():
            partner = got_ref[rows, W : 2 * W]
            te = jnp.dot(plain_ref[i, T : 2 * T], e_ref[...], preferred_element_type=F32)
            dxsum_ref[...] += te * jnp.dot(b, partner, preferred_element_type=F32)
            xs = (x_ref[i].astype(F32) * te).astype(BF16)
            db_ref[i] += lax.dot_general(xs, partner, NT, preferred_element_type=F32)

        y_ref[i] = ysum_ref[...].astype(BF16)
        dx_ref[i] = dxsum_ref[...].astype(BF16)
        return unused

    lax.fori_loop(0, HALF, one_group, 0)


def local(name, sc, aux, skip, got, *tokens):
    wide = pltpu.HBM((HALF, T, W), BF16)
    thin = pltpu.HBM((HALF, T, N), F32)
    args = [in_hbm(a) for a in (aux, skip, got, *tokens)]
    return pl.pallas_call(
        local_kernel,
        in_specs=[SMEM_SPEC, VMEM_SPEC, VMEM_SPEC, VMEM_SPEC] + [HBM_SPEC] * 5,
        out_specs=[VMEM_SPEC] * 7,
        out_shape=[wide] * 4 + [pltpu.HBM((HALF, 2 * T, LANES), BF16)] + [thin] * 2,
        scratch_shapes=[SPREAD]
        + [pltpu.VMEM((HALF, T, W), BF16)] * 3
        + [pltpu.VMEM((HALF, T, N), BF16)] * 2
        + [pltpu.VMEM((T, W), F32)] * 2
        + [pltpu.VMEM((T, W), BF16)]
        + [pltpu.VMEM((HALF, T, LANES), F32)]
        + [pltpu.VMEM((HALF, PER, T), F32)] * 2
        + [pltpu.VMEM((HALF, 2 * T + 16, LANES), BF16)]
        + [pltpu.SemaphoreType.DMA((HALF, 5))],
        compiler_params=params(24),
        name=name,
    )(sc, *args)


def final_kernel(aliased, sc_ref, el_ref, *refs):
    sources = refs[:10]
    refs = refs[10 + (4 if aliased else 0) :]
    out_hbm, dx_hbm, db_hbm, dc_hbm = refs[:4]
    e_ref, *targets = refs[4:15]
    out_ref, dx_ref, db_ref, dc_ref, sem_in, sem_out = refs[15:]
    b_ref, c_ref, pair_ref, y_ref, z_ref, dxl_ref, xs_ref, gs_ref, dbl_ref, dcl_ref = targets
    base = sc_ref[0]
    loads = []
    for i in range(HALF):
        row = []
        for k, (src, dst) in enumerate(zip(sources, targets)):
            if k in (0, 1, 4):
                src = src.at[:, columns(base, i, W if k == 4 else N)]
            else:
                src = src.at[i]
            row.append(pltpu.make_async_copy(src, dst.at[i], sem_in.at[i, k]))
            row[-1].start()
        loads.append(row)
    fill_spread(e_ref)
    stores = []
    for i in range(HALF):
        for load in loads[i]:
            load.wait()
        b, c = b_ref[i], c_ref[i]
        rows = slice(i * N, (i + 1) * N)
        for k in range(W // CHUNK):
            cut = slice(k * CHUNK, (k + 1) * CHUNK)
            far = slice(W + k * CHUNK, W + (k + 1) * CHUNK)
            scale = jnp.dot(pair_ref[i], e_ref[:, cut], preferred_element_type=F32)
            mixed = y_ref[i, :, cut].astype(F32) + scale[0:T] * jnp.dot(
                c, el_ref[rows, cut], preferred_element_type=F32
            )
            mixed = mixed.astype(BF16).astype(F32)
            out_ref[i, :, cut] = (mixed * silu(z_ref[i, :, cut].astype(F32))).astype(BF16)
            dx_ref[i, :, cut] = dxl_ref[i, :, cut].astype(F32) + scale[T : 2 * T] * jnp.dot(
                b, el_ref[rows, far], preferred_element_type=F32
            )
        db_ref[i] = dbl_ref[i] + lax.dot_general(
            xs_ref[i], el_ref[rows, W:], NT, preferred_element_type=F32
        )
        dc_ref[i] = dcl_ref[i] + lax.dot_general(
            gs_ref[i], el_ref[rows, :W], NT, preferred_element_type=F32
        )
        for k, (src, dst, width) in enumerate(
            ((out_ref, out_hbm, W), (dx_ref, dx_hbm, W), (db_ref, db_hbm, N), (dc_ref, dc_hbm, N))
        ):
            stores.append(
                pltpu.make_async_copy(src.at[i], dst.at[:, columns(base, i, width)], sem_out.at[i, k])
            )
            stores[-1].start()
    for store in stores:
        store.wait()


def final(name, sc, el, local_parts, z, b, c, earlier):
    y, dx, xs, gs, pairs, db, dc = local_parts
    operands = [in_hbm(a) for a in (b, c, pairs, y, z, dx, xs, gs, db, dc)]
    wide = pltpu.VMEM((HALF, T, W), BF16)
    thin = pltpu.VMEM((HALF, T, N), F32)
    short = pltpu.VMEM((HALF, T, N), BF16)
    return pl.pallas_call(
        functools.partial(final_kernel, bool(earlier)),
        in_specs=[SMEM_SPEC, VMEM_SPEC] + [HBM_SPEC] * (10 + len(earlier)),
        out_specs=[HBM_SPEC] * 4,
        out_shape=[
            pltpu.HBM((T, NH * P_SIZE), BF16),
            pltpu.HBM((T, NH * P_SIZE), F32),
            pltpu.HBM((T, NG * N), F32),
            pltpu.HBM((T, NG * N), F32),
        ],
        input_output_aliases={12 + k: k for k in range(len(earlier))},
        scratch_shapes=[
            SPREAD, short, short, pltpu.VMEM((HALF, 2 * T, LANES), BF16),
            wide, wide, wide, wide, wide, thin, thin,
            wide, pltpu.VMEM((HALF, T, W), F32), thin, thin,
            pltpu.SemaphoreType.DMA((HALF, 10)),
            pltpu.SemaphoreType.DMA((HALF, 4)),
        ],
        compiler_params=params(24),
        name=name,
    )(sc, el, *operands, *earlier)


def body(ssm_input, gate_input, b_input, c_input, dt_raw, dt_bias, a_log, skip_gain, out_grad):
    ctx_count = lax.axis_size("ctx")
    head_count = lax.axis_size("head")
    core = (lax.axis_index("head") % 2).astype(jnp.int32)
    sc_other = jnp.stack([HALF * (1 - core), core])
    sc_own = jnp.stack([HALF * core, core])
    bias, alog, skip = dt_bias[None, :], a_log[None, :], skip_gain[None, :]
    swap = [(k, k ^ 1) for k in range(head_count)]
    chips = [[2 * k + c for k in range(ctx_count * head_count // 2)] for c in range(2)]

    def exchange(parts):
        return lax.all_to_all(
            parts, ("ctx", "head"), split_axis=0, concat_axis=0, tiled=True, axis_index_groups=chips
        )

    tokens = (ssm_input, gate_input, out_grad, b_input, c_input)
    send, aux = states(True, sc_other, dt_raw, bias, alog, *tokens)
    got = lax.ppermute(send, "head", swap)
    keep = states(False, sc_own, aux, *tokens)[0]
    gathered = exchange(merge(sc_own, keep, got))
    got_other = lax.ppermute(keep, "head", swap)
    loc_own = local("local_own", sc_own, aux, skip, got, *tokens)
    back = exchange(scan(gathered, loc_own[6]))
    loc_other = local("local_other", sc_other, aux, skip, got_other, *tokens)
    back, loc_other = lax.optimization_barrier((back, loc_other))
    el = back.reshape(HALF * N, 2 * W)
    el_other = lax.ppermute(el, "head", swap)
    shared = (gate_input, b_input, c_input)
    outs = final("final_own", sc_own, el, loc_own, *shared, ())
    return tuple(final("final_other", sc_other, el_other, loc_other, *shared, tuple(outs)))


def solution(mesh):
    row_spec = P(("ctx", "head"), None)
    in_specs = (row_spec,) * 5 + (P(), P(), P(), row_spec)
    return jax.shard_map(
        body, mesh=mesh, in_specs=in_specs, out_specs=(row_spec,) * 4, check_vma=False
    )
```

```python
import functools

import jax
import jax.numpy as jnp
from jax import lax
from jax.experimental import pallas as pl
from jax.experimental.pallas import tpu as pltpu
from jax.sharding import PartitionSpec as P

NH = 128
P_SIZE = 64
N = 128
NG = 8
PER = NH // NG
W = PER * P_SIZE
T = 128
HALF = NG // 2
LANES = 128
WIDE = 2 * W + LANES
F32 = jnp.float32
BF16 = jnp.bfloat16


MIB = 1024 * 1024
NT = (((1,), (1,)), ((), ()))
CHUNK = 256
HBM_SPEC = pl.BlockSpec(memory_space=pl.ANY)
VMEM_SPEC = pl.BlockSpec(memory_space=pltpu.VMEM)
SMEM_SPEC = pl.BlockSpec(memory_space=pltpu.SMEM)
SPREAD = pltpu.VMEM((LANES, W), BF16)


def in_hbm(values):
    return pltpu.with_memory_space_constraint(values, pltpu.HBM)


def params(mib):
    return pltpu.CompilerParams(vmem_limit_bytes=mib * MIB)


def lane(shape):
    return lax.broadcasted_iota(jnp.int32, shape, len(shape) - 1)


def fill_spread(e_ref):
    row = lax.broadcasted_iota(jnp.int32, (LANES, W), 0)
    col = lax.broadcasted_iota(jnp.int32, (LANES, W), 1)
    e_ref[...] = jnp.where((row & 63) == (col >> 6), 1.0, 0.0).astype(BF16)


def to_half(values, base):
    return pltpu.roll(values, lax.rem(LANES - PER * base, LANES), 1)


def pair_up(values):
    high = values.astype(BF16).astype(F32)
    low = values - high
    return jnp.where(lane(values.shape) < 64, high, pltpu.roll(low, 64, 1))


def of_group(pairs, i):
    if i:
        pairs = pltpu.roll(pairs, LANES - PER * i, 1)
    return pairs.astype(BF16)


def silu(v):
    return v * (0.5 * jnp.tanh(0.5 * v) + 0.5)


def steps_of(dt_ref, bias_ref, alog_ref):
    u = jnp.exp(dt_ref[...].astype(F32) + bias_ref[...])
    one = 1.0 + u
    step = jnp.where(one == 1.0, u, jnp.log(one) * (u / jnp.where(one == 1.0, 1.0, one - 1.0)))
    rate = -step * jnp.exp(alog_ref[...])
    row = lax.broadcasted_iota(jnp.int32, (T, T), 0)
    col = lax.broadcasted_iota(jnp.int32, (T, T), 1)
    tri = jnp.where(row >= col, 1.0, 0.0).astype(BF16)
    running = jnp.zeros((T, NH), F32)
    for _ in range(3):
        piece = rate.astype(BF16)
        running = running + jnp.dot(tri, piece, preferred_element_type=F32)
        rate = rate - piece.astype(F32)
    from_start = jnp.exp(running)
    to_end = jnp.exp(running[T - 1 : T] - running) * step
    return step, running, from_start, to_end


def base_of(own, sc_ref):
    return HALF * sc_ref[0] if own else HALF * (1 - sc_ref[0])


def columns(base, i, width):
    return pl.ds(pl.multiple_of((base + i) * width, width), width)


def states_kernel(own, sc_ref, *refs):
    if own:
        aux_ref, b_ref, x_ref, c_ref, z_ref, og_ref, st_ref, part_hbm, e_ref, sem_out = refs
    else:
        dt_hbm, bias_hbm, alog_hbm = refs[:3]
        tokens = refs[3:8]
        st_ref, aux_ref, aux_hbm = refs[8:11]
        kept = refs[11:16]
        e_ref = refs[16]
        b_ref, x_ref, c_ref, z_ref, og_ref = used = refs[17:22]
        small = refs[22:25]
        sem, sem_small = refs[25:]
    base = base_of(own, sc_ref)
    copies = []
    stores = []
    if not own:
        smalls = [
            pltpu.make_async_copy(s, d, sem_small.at[k])
            for k, (s, d) in enumerate(zip((dt_hbm, bias_hbm, alog_hbm), small))
        ]
        for copy in smalls:
            copy.start()
        for half, (first, targets) in enumerate(((base, used), (base_of(True, sc_ref), kept))):
            for i in range(HALF):
                row = []
                for k, (src, dst) in enumerate(zip(tokens, targets)):
                    cut = columns(first, i, dst.shape[-1])
                    row.append(pltpu.make_async_copy(src.at[:, cut], dst.at[i], sem.at[half, i, k]))
                    row[-1].start()
                copies.append(row)
    fill_spread(e_ref)
    if not own:
        for copy in smalls:
            copy.wait()
        for k, v in enumerate(steps_of(*small)):
            aux_ref[k] = v
        stores.append(pltpu.make_async_copy(aux_ref, aux_hbm, sem_small.at[3]))
        stores[0].start()
    from_start = pair_up(to_half(aux_ref[2], base))
    to_end = pair_up(to_half(aux_ref[3], base))
    for i in range(HALF):
        if not own:
            for copy in copies[i]:
                copy.wait()
        here = slice(i * N, (i + 1) * N)
        te = of_group(to_end, i)
        fs = of_group(from_start, i)
        bt = b_ref[i].T
        ct = c_ref[i].T
        for k in range(W // CHUNK):
            cut = slice(k * CHUNK, (k + 1) * CHUNK)
            e = e_ref[:, cut]
            xs = x_ref[i, :, cut].astype(F32) * jnp.dot(te, e, preferred_element_type=F32)
            st_ref[here, cut] = jnp.dot(
                bt, xs.astype(BF16), preferred_element_type=F32
            ).astype(BF16)
            gate = silu(z_ref[i, :, cut].astype(F32))
            hg = (og_ref[i, :, cut].astype(F32) * gate).astype(BF16)
            gs = hg.astype(F32) * jnp.dot(fs, e, preferred_element_type=F32)
            st_ref[here, slice(W + k * CHUNK, W + (k + 1) * CHUNK)] = jnp.dot(
                ct, gs.astype(BF16), preferred_element_type=F32
            ).astype(BF16)
        decay = jnp.broadcast_to(fs[T - 16 : T].astype(F32)[15:16], (N, LANES))
        st_ref[here, 2 * W :] = decay.astype(BF16)
        if own:
            stores += part_copies(st_ref, part_hbm, here, sc_ref[0], sem_out.at[i])
            for store in stores[-2:]:
                store.start()
    if not own:
        for row in copies[HALF:]:
            for copy in row:
                copy.wait()
    for store in stores:
        store.wait()


def part_copies(st_ref, part_hbm, here, which, sem):
    cut = pl.ds(pl.multiple_of(which * W, W), W)
    return [
        pltpu.make_async_copy(st_ref.at[here, cut], part_hbm.at[here, :W], sem.at[0]),
        pltpu.make_async_copy(st_ref.at[here, 2 * W :], part_hbm.at[here, W:], sem.at[1]),
    ]


STATE = jax.ShapeDtypeStruct((HALF * N, WIDE), BF16)
PART = pltpu.HBM((HALF * N, W + LANES), BF16)


def states_send(sc, dt, bias, alog, *tokens):
    shapes = [(HALF, T, N), (HALF, T, W), (HALF, T, N), (HALF, T, W), (HALF, T, W)]
    aux = jax.ShapeDtypeStruct((4, T, NH), F32)
    return pl.pallas_call(
        functools.partial(states_kernel, False),
        in_specs=[SMEM_SPEC] + [HBM_SPEC] * 8,
        out_specs=[VMEM_SPEC, VMEM_SPEC, HBM_SPEC] + [VMEM_SPEC] * 5,
        out_shape=[STATE, aux, pltpu.HBM((4, T, NH), F32)]
        + [jax.ShapeDtypeStruct(s, BF16) for s in shapes],
        scratch_shapes=[SPREAD]
        + [pltpu.VMEM(s, BF16) for s in shapes]
        + [pltpu.VMEM((T, NH), BF16), pltpu.VMEM((1, NH), F32), pltpu.VMEM((1, NH), F32)]
        + [pltpu.SemaphoreType.DMA((2, HALF, 5)), pltpu.SemaphoreType.DMA((4,))],
        compiler_params=params(24),
        name="states_send",
    )(sc, *[in_hbm(a) for a in (dt, bias, alog, *tokens)])


def states_keep(sc, aux, *tokens):
    return pl.pallas_call(
        functools.partial(states_kernel, True),
        in_specs=[SMEM_SPEC] + [VMEM_SPEC] * 6,
        out_specs=[VMEM_SPEC, HBM_SPEC],
        out_shape=[STATE, PART],
        scratch_shapes=[SPREAD, pltpu.SemaphoreType.DMA((HALF, 2))],
        compiler_params=params(12),
        name="states_keep",
    )(sc, aux, *tokens)


def decay_row(state_ref, at, e_ref):
    pairs = state_ref[at : at + 16, 2 * W :]
    return jnp.dot(pairs, e_ref[...], preferred_element_type=F32)[0:1]


def merge_kernel(sc_ref, own_ref, got_ref, out_hbm, part_hbm, e_ref, out_ref, sem, sem_out):
    fill_spread(e_ref)
    core = sc_ref[0]

    def merge(r0, r1):
        stores = []
        for i in range(HALF):
            here = slice(i * N, (i + 1) * N)
            there = slice(i * N // 8, (i + 1) * N // 8)
            d0 = decay_row(r0, i * N, e_ref)
            d1 = decay_row(r1, i * N, e_ref)
            for k in range(W // CHUNK):
                cut = slice(k * CHUNK, (k + 1) * CHUNK)
                forward = d1[:, cut] * r0[here, cut].astype(F32) + r1[here, cut].astype(F32)
                out_ref[there, :, cut] = forward.reshape(N // 8, 8, CHUNK).astype(BF16)
                back = slice(W + k * CHUNK, W + (k + 1) * CHUNK)
                backward = r0[here, back].astype(F32) + d0[:, cut] * r1[here, back].astype(F32)
                out_ref[there, :, back] = backward.reshape(N // 8, 8, CHUNK).astype(BF16)
            p0 = r0[i * N : i * N + 16, 2 * W :].astype(F32)
            p1 = r1[i * N : i * N + 16, 2 * W :].astype(F32)
            p0 = p0 + pltpu.roll(p0, 64, 1)
            p1 = p1 + pltpu.roll(p1, 64, 1)
            both = pair_up(p0 * p1)[0:8]
            both = jnp.broadcast_to(both[None], (N // 8, 8, LANES))
            out_ref[there, :, 2 * W :] = both.astype(BF16)
            stores.append(pltpu.make_async_copy(out_ref.at[there], out_hbm.at[there], sem_out.at[i]))
            stores[-1].start()
        stores += part_copies(got_ref, part_hbm, slice(0, HALF * N), 1 - core, sem)
        for store in stores[-2:]:
            store.start()
        for store in stores:
            store.wait()

    @pl.when(core == 0)
    def _():
        merge(own_ref, got_ref)

    @pl.when(core != 0)
    def _():
        merge(got_ref, own_ref)


def merge(sc, own, got):
    return pl.pallas_call(
        merge_kernel,
        in_specs=[SMEM_SPEC, VMEM_SPEC, VMEM_SPEC],
        out_specs=[HBM_SPEC, HBM_SPEC],
        out_shape=[pltpu.HBM((HALF * N // 8, 8, WIDE), BF16), PART],
        scratch_shapes=[
            SPREAD,
            pltpu.VMEM((HALF * N // 8, 8, WIDE), BF16),
            pltpu.SemaphoreType.DMA((2,)),
            pltpu.SemaphoreType.DMA((HALF,)),
        ],
        compiler_params=params(16),
        name="merge_cores",
    )(sc, own, got)


def scan_kernel(chips, in_ref, after_ref, out_hbm, e_ref, d_ref, out_ref, sem):
    fill_spread(e_ref)
    pairs = in_ref[:, :, 2 * W :].astype(F32).reshape(chips * 8, LANES).astype(BF16)
    d_ref[...] = jnp.dot(pairs, e_ref[...], preferred_element_type=F32).reshape(chips, 8, W)
    zero = jnp.zeros((8, W), F32)

    def forward(k, e):
        out_ref[k, :, :W] = e.astype(BF16)
        return d_ref[k] * e + in_ref[k, :, :W].astype(F32)

    def backward(k, l):
        j = chips - 1 - k
        out_ref[j, :, W:] = l.astype(BF16)
        return d_ref[j] * l + in_ref[j, :, W : 2 * W].astype(F32)

    parts = ((0, chips, slice(0, W)), (chips // 2, chips, slice(W, 2 * W)), (0, chips // 2, slice(W, 2 * W)))
    stores = [
        pltpu.make_async_copy(out_ref.at[a:b, :, cut], out_hbm.at[a:b, :, cut], sem.at[k])
        for k, (a, b, cut) in enumerate(parts)
    ]
    lax.fori_loop(0, chips, forward, zero, unroll=8)
    stores[0].start()
    l = lax.fori_loop(0, chips // 2, backward, zero, unroll=8)
    stores[1].start()
    lax.fori_loop(chips // 2, chips, backward, l, unroll=8)
    stores[2].start()
    for store in stores:
        store.wait()


def scan(parts, after):
    chips = parts.shape[0]
    return pl.pallas_call(
        functools.partial(scan_kernel, chips),
        in_specs=[VMEM_SPEC, HBM_SPEC],
        out_specs=HBM_SPEC,
        out_shape=pltpu.HBM((chips, 8, 2 * W), BF16),
        scratch_shapes=[
            SPREAD,
            pltpu.VMEM((chips, 8, W), F32),
            pltpu.VMEM((chips, 8, 2 * W), BF16),
            pltpu.SemaphoreType.DMA((3,)),
        ],
        compiler_params=params(16),
        name="scan_chips",
    )(parts, in_hbm(after))


def local_kernel(
    own, sc_ref, aux_ref, skip_ref, got_ref, b_hbm, x_hbm, c_hbm, z_hbm, og_hbm,
    y_ref, dx_ref, xs_ref, gs_ref, pair_ref, db_ref, dc_ref,
    e_ref, x_ref, z_ref, og_ref, b_ref, c_ref, ysum_ref, dxsum_ref, hg_ref,
    runc_ref, run_ref, step_ref, plain_ref, sem,
):
    base = base_of(own, sc_ref)
    core = sc_ref[0]
    copies = []
    for i in range(HALF):
        for k, (src, dst, width) in enumerate(
            (
                (b_hbm, b_ref, N),
                (x_hbm, x_ref, W),
                (c_hbm, c_ref, N),
                (z_hbm, z_ref, W),
                (og_hbm, og_ref, W),
            )
        ):
            copies.append(
                pltpu.make_async_copy(src.at[:, columns(base, i, width)], dst.at[i], sem.at[i, k])
            )
            copies[-1].start()
    fill_spread(e_ref)
    start = to_half(aux_ref[2], base)
    end = to_half(aux_ref[3], base)
    gain = to_half(jnp.broadcast_to(skip_ref[...], (16, NH)), base)
    run = to_half(aux_ref[1], base)
    run_t = run.T
    step_t = to_half(aux_ref[0], base).T
    for i in range(HALF):
        decay = got_ref[i * N : i * N + 16, W:].astype(F32)
        decay = (decay + pltpu.roll(decay, 64, 1))[0:1]
        fs, te, skip, run_c = [pltpu.roll(v, LANES - PER * i, 1) if i else v for v in (start, end, gain, run)]
        plain_ref[i, 0:T] = pair_up(fs).astype(BF16)
        plain_ref[i, T : 2 * T] = pair_up(te).astype(BF16)
        plain_ref[i, 2 * T : 2 * T + 16] = pair_up(skip).astype(BF16)
        pair_ref[i, 0:T] = pair_up(jnp.where(core == 0, fs, fs * decay)).astype(BF16)
        pair_ref[i, T : 2 * T] = pair_up(jnp.where(core == 0, te * decay, te)).astype(BF16)
        runc_ref[i] = run_c
        run_ref[i] = run_t[i * PER : (i + 1) * PER]
        step_ref[i] = step_t[i * PER : (i + 1) * PER]
    for copy in copies:
        copy.wait()
    row = lax.broadcasted_iota(jnp.int32, (T, T), 0)
    col = lax.broadcasted_iota(jnp.int32, (T, T), 1)
    below = row >= col
    left = col < P_SIZE

    def one_group(i, unused):
        b, c = b_ref[i], c_ref[i]
        cb = lax.dot_general(c, b, NT, preferred_element_type=F32)
        run_cols, run_rows, step_rows = runc_ref[i], run_ref[i], step_ref[i]
        mass = jnp.zeros((T, T), F32)
        for pair in range(PER // 2):
            here = slice(pair * LANES, (pair + 1) * LANES)
            e = e_ref[:, here]
            both = jnp.dot(pair_ref[i], e, preferred_element_type=F32)
            skip = jnp.dot(plain_ref[i, 2 * T : 2 * T + 16], e, preferred_element_type=F32)[0:1]
            x = x_ref[i, :, here]
            g = (og_ref[i, :, here].astype(F32) * silu(z_ref[i, :, here].astype(F32))).astype(BF16)
            hg_ref[:, here] = g
            gs_ref[i, :, here] = (g.astype(F32) * both[0:T]).astype(BF16)
            xs_ref[i, :, here] = (x.astype(F32) * both[T : 2 * T]).astype(BF16)
            ys, dxs = [], []
            for k in range(2):
                j = 2 * pair + k
                gap = run_cols[:, j : j + 1] - run_rows[j : j + 1, :]
                weight = jnp.exp(jnp.where(below, gap, -1e30)) * step_rows[j : j + 1, :]
                mine = left if k == 0 else ~left
                inner = lax.dot_general(
                    jnp.where(mine, g, jnp.zeros_like(g)), x, NT, preferred_element_type=F32
                )
                mass = mass + weight * inner
                joint = (weight * cb).astype(BF16)
                ys.append(jnp.dot(joint, x, preferred_element_type=F32))
                dxs.append(jnp.dot(joint.T, g, preferred_element_type=F32))
            ysum_ref[:, here] = jnp.where(left, ys[0], ys[1]) + skip * x.astype(F32)
            dxsum_ref[:, here] = jnp.where(left, dxs[0], dxs[1]) + skip * g.astype(F32)
        high = mass.astype(BF16)
        low = (mass - high.astype(F32)).astype(BF16)
        dc_ref[i] = jnp.dot(high, b, preferred_element_type=F32) + jnp.dot(
            low, b, preferred_element_type=F32
        )
        db_ref[i] = jnp.dot(high.T, c, preferred_element_type=F32) + jnp.dot(
            low.T, c, preferred_element_type=F32
        )
        rows = pl.ds(pl.multiple_of(i * N, N), N)

        @pl.when(core != 0)
        def _():
            partner = got_ref[rows, :W]
            fs = jnp.dot(plain_ref[i, 0:T], e_ref[...], preferred_element_type=F32)
            ysum_ref[...] += fs * jnp.dot(c, partner, preferred_element_type=F32)
            gs = (hg_ref[...].astype(F32) * fs).astype(BF16)
            dc_ref[i] += lax.dot_general(gs, partner, NT, preferred_element_type=F32)

        @pl.when(core == 0)
        def _():
            partner = got_ref[rows, :W]
            te = jnp.dot(plain_ref[i, T : 2 * T], e_ref[...], preferred_element_type=F32)
            dxsum_ref[...] += te * jnp.dot(b, partner, preferred_element_type=F32)
            xs = (x_ref[i].astype(F32) * te).astype(BF16)
            db_ref[i] += lax.dot_general(xs, partner, NT, preferred_element_type=F32)

        y_ref[i] = ysum_ref[...].astype(BF16)
        dx_ref[i] = dxsum_ref[...].astype(BF16)
        return unused

    lax.fori_loop(0, HALF, one_group, 0)


def local(own, sc, aux, skip, got, *tokens):
    wide = pltpu.HBM((HALF, T, W), BF16)
    thin = pltpu.HBM((HALF, T, N), F32)
    args = [in_hbm(a) for a in (aux, skip, got, *tokens)]
    return pl.pallas_call(
        functools.partial(local_kernel, own),
        in_specs=[SMEM_SPEC, VMEM_SPEC, VMEM_SPEC, VMEM_SPEC] + [HBM_SPEC] * 5,
        out_specs=[VMEM_SPEC] * 7,
        out_shape=[wide] * 4 + [pltpu.HBM((HALF, 2 * T, LANES), BF16)] + [thin] * 2,
        scratch_shapes=[SPREAD]
        + [pltpu.VMEM((HALF, T, W), BF16)] * 3
        + [pltpu.VMEM((HALF, T, N), BF16)] * 2
        + [pltpu.VMEM((T, W), F32)] * 2
        + [pltpu.VMEM((T, W), BF16)]
        + [pltpu.VMEM((HALF, T, LANES), F32)]
        + [pltpu.VMEM((HALF, PER, T), F32)] * 2
        + [pltpu.VMEM((HALF, 2 * T + 16, LANES), BF16)]
        + [pltpu.SemaphoreType.DMA((HALF, 5))],
        compiler_params=params(24),
        name="local_own" if own else "local_other",
    )(sc, *args)


def final_kernel(own, sc_ref, el_ref, *refs):
    if own:
        sources, others, refs = refs[:10], refs[10:20], refs[20:]
        out_hbm, dx_hbm, db_hbm, dc_hbm = refs[:4]
        kept, refs = refs[4:14], refs[14:]
        e_ref, targets, refs = refs[0], refs[1:11], refs[11:]
        out_ref, dx_ref, db_ref, dc_ref, sem_out, sem_in = refs
    else:
        targets, refs = refs[:10], refs[14:]
        out_hbm, dx_hbm, db_hbm, dc_hbm = refs[:4]
        e_ref, out_ref, dx_ref, db_ref, dc_ref, sem_out = refs[4:]
    b_ref, c_ref, pair_ref, y_ref, z_ref, dxl_ref, xs_ref, gs_ref, dbl_ref, dcl_ref = targets
    base = base_of(own, sc_ref)
    loads = []
    if own:
        for half, (first, srcs, dsts) in enumerate(
            ((base, sources, targets), (base_of(False, sc_ref), others, kept))
        ):
            for i in range(HALF):
                row = []
                for k, (src, dst) in enumerate(zip(srcs, dsts)):
                    if k in (0, 1, 4):
                        src = src.at[:, columns(first, i, W if k == 4 else N)]
                    else:
                        src = src.at[i]
                    row.append(pltpu.make_async_copy(src, dst.at[i], sem_in.at[half, i, k]))
                    row[-1].start()
                loads.append(row)
    fill_spread(e_ref)
    stores = []
    for i in range(HALF):
        if own:
            for load in loads[i]:
                load.wait()
        b, c = b_ref[i], c_ref[i]
        rows = slice(i * N, (i + 1) * N)
        for k in range(W // CHUNK):
            cut = slice(k * CHUNK, (k + 1) * CHUNK)
            far = slice(W + k * CHUNK, W + (k + 1) * CHUNK)
            scale = jnp.dot(pair_ref[i], e_ref[:, cut], preferred_element_type=F32)
            mixed = y_ref[i, :, cut].astype(F32) + scale[0:T] * jnp.dot(
                c, el_ref[rows, cut], preferred_element_type=F32
            )
            mixed = mixed.astype(BF16).astype(F32)
            out_ref[i, :, cut] = (mixed * silu(z_ref[i, :, cut].astype(F32))).astype(BF16)
            dx_ref[i, :, cut] = dxl_ref[i, :, cut].astype(F32) + scale[T : 2 * T] * jnp.dot(
                b, el_ref[rows, far], preferred_element_type=F32
            )
        db_ref[i] = dbl_ref[i] + lax.dot_general(
            xs_ref[i], el_ref[rows, W:], NT, preferred_element_type=F32
        )
        dc_ref[i] = dcl_ref[i] + lax.dot_general(
            gs_ref[i], el_ref[rows, :W], NT, preferred_element_type=F32
        )
        for k, (src, dst, width) in enumerate(
            ((out_ref, out_hbm, W), (dx_ref, dx_hbm, W), (db_ref, db_hbm, N), (dc_ref, dc_hbm, N))
        ):
            stores.append(
                pltpu.make_async_copy(src.at[i], dst.at[:, columns(base, i, width)], sem_out.at[i, k])
            )
            stores[-1].start()
    for row in loads[HALF:]:
        for load in row:
            load.wait()
    for store in stores:
        store.wait()


LOADED = [
    ((HALF, T, N), BF16),
    ((HALF, T, N), BF16),
    ((HALF, 2 * T, LANES), BF16),
    ((HALF, T, W), BF16),
    ((HALF, T, W), BF16),
    ((HALF, T, W), BF16),
    ((HALF, T, W), BF16),
    ((HALF, T, W), BF16),
    ((HALF, T, N), F32),
    ((HALF, T, N), F32),
]
RESULTS = [
    ((T, NH * P_SIZE), BF16),
    ((T, NH * P_SIZE), F32),
    ((T, NG * N), F32),
    ((T, NG * N), F32),
]
STAGED = [
    pltpu.VMEM((HALF, T, W), BF16),
    pltpu.VMEM((HALF, T, W), F32),
    pltpu.VMEM((HALF, T, N), F32),
    pltpu.VMEM((HALF, T, N), F32),
    pltpu.SemaphoreType.DMA((HALF, 4)),
]


def in_order(local_parts, z, b, c):
    y, dx, xs, gs, pairs, db, dc = local_parts
    return [in_hbm(a) for a in (b, c, pairs, y, z, dx, xs, gs, db, dc)]


def final_own(sc, el, own_parts, other_parts):
    return pl.pallas_call(
        functools.partial(final_kernel, True),
        in_specs=[SMEM_SPEC, VMEM_SPEC] + [HBM_SPEC] * 20,
        out_specs=[HBM_SPEC] * 4 + [VMEM_SPEC] * 10,
        out_shape=[pltpu.HBM(*r) for r in RESULTS] + [jax.ShapeDtypeStruct(*r) for r in LOADED],
        scratch_shapes=[SPREAD]
        + [pltpu.VMEM(*r) for r in LOADED]
        + STAGED
        + [pltpu.SemaphoreType.DMA((2, HALF, 10))],
        compiler_params=params(24),
        name="final_own",
    )(sc, el, *own_parts, *other_parts)


def final_other(sc, el, loaded, earlier):
    return pl.pallas_call(
        functools.partial(final_kernel, False),
        in_specs=[SMEM_SPEC, VMEM_SPEC] + [VMEM_SPEC] * 10 + [HBM_SPEC] * 4,
        out_specs=[HBM_SPEC] * 4,
        out_shape=[pltpu.HBM(*r) for r in RESULTS],
        input_output_aliases={12 + k: k for k in range(4)},
        scratch_shapes=[SPREAD] + STAGED,
        compiler_params=params(16),
        name="final_other",
    )(sc, el, *loaded, *earlier)


def body(ssm_input, gate_input, b_input, c_input, dt_raw, dt_bias, a_log, skip_gain, out_grad):
    ctx_count = lax.axis_size("ctx")
    head_count = lax.axis_size("head")
    sc = (lax.axis_index("head") % 2).astype(jnp.int32)[None]
    bias, alog, skip = dt_bias[None, :], a_log[None, :], skip_gain[None, :]
    swap = [(k, k ^ 1) for k in range(head_count)]
    chips = [[2 * k + c for k in range(ctx_count * head_count // 2)] for c in range(2)]

    def exchange(parts):
        return lax.all_to_all(
            parts, ("ctx", "head"), split_axis=0, concat_axis=0, tiled=True, axis_index_groups=chips
        )

    tokens = (b_input, ssm_input, c_input, gate_input, out_grad)
    send, aux, aux_hbm, *kept = states_send(sc, dt_raw, bias, alog, *tokens)
    got = lax.ppermute(send, "head", swap)
    keep, keep_part = states_keep(sc, aux, *kept)
    payload, got_part = merge(sc, keep, got)
    gathered = exchange(payload)
    got_other = lax.ppermute(keep_part, "head", swap)
    loc_own = local(True, sc, aux_hbm, skip, got_part, *tokens)
    back = exchange(scan(gathered, loc_own[6]))
    loc_other = local(False, sc, aux_hbm, skip, got_other, *tokens)
    back, loc_other = lax.optimization_barrier((back, loc_other))
    el = back.reshape(HALF * N, 2 * W)
    el_other = lax.ppermute(el, "head", swap)
    shared = (gate_input, b_input, c_input)
    outs = final_own(sc, el, in_order(loc_own, *shared), in_order(loc_other, *shared))
    return tuple(final_other(sc, el_other, outs[4:], outs[:4]))


def solution(mesh):
    row_spec = P(("ctx", "head"), None)
    in_specs = (row_spec,) * 5 + (P(), P(), P(), row_spec)
    return jax.shard_map(
        body, mesh=mesh, in_specs=in_specs, out_specs=(row_spec,) * 4, check_vma=False
    )
```

```python
import functools

import jax
import jax.numpy as jnp
from jax import lax
from jax.experimental import pallas as pl
from jax.experimental.pallas import tpu as pltpu
from jax.sharding import PartitionSpec as P

NH = 128
P_SIZE = 64
N = 128
NG = 8
PER = NH // NG
W = PER * P_SIZE
T = 128
HALF = NG // 2
LANES = 128
WIDE = 2 * W + LANES
F32 = jnp.float32
BF16 = jnp.bfloat16


MIB = 1024 * 1024
NT = (((1,), (1,)), ((), ()))
CHUNK = 256
HBM_SPEC = pl.BlockSpec(memory_space=pl.ANY)
VMEM_SPEC = pl.BlockSpec(memory_space=pltpu.VMEM)
SMEM_SPEC = pl.BlockSpec(memory_space=pltpu.SMEM)
KEPT = 2
SPREAD = pltpu.VMEM((LANES, W), BF16)


def in_hbm(values):
    return pltpu.with_memory_space_constraint(values, pltpu.HBM)


def params(mib):
    return pltpu.CompilerParams(vmem_limit_bytes=mib * MIB)


def lane(shape):
    return lax.broadcasted_iota(jnp.int32, shape, len(shape) - 1)


def fill_spread(e_ref):
    row = lax.broadcasted_iota(jnp.int32, (LANES, W), 0)
    col = lax.broadcasted_iota(jnp.int32, (LANES, W), 1)
    e_ref[...] = jnp.where((row & 63) == (col >> 6), 1.0, 0.0).astype(BF16)


def to_half(values, base):
    return pltpu.roll(values, lax.rem(LANES - PER * base, LANES), 1)


def pair_up(values):
    high = values.astype(BF16).astype(F32)
    low = values - high
    return jnp.where(lane(values.shape) < 64, high, pltpu.roll(low, 64, 1))


def of_group(pairs, i):
    if i:
        pairs = pltpu.roll(pairs, LANES - PER * i, 1)
    return pairs.astype(BF16)


def silu(v):
    return v * (0.5 * jnp.tanh(0.5 * v) + 0.5)


def steps_of(dt_ref, bias_ref, alog_ref):
    u = jnp.exp(dt_ref[...].astype(F32) + bias_ref[...])
    one = 1.0 + u
    step = jnp.where(one == 1.0, u, jnp.log(one) * (u / jnp.where(one == 1.0, 1.0, one - 1.0)))
    rate = -step * jnp.exp(alog_ref[...])
    row = lax.broadcasted_iota(jnp.int32, (T, T), 0)
    col = lax.broadcasted_iota(jnp.int32, (T, T), 1)
    tri = jnp.where(row >= col, 1.0, 0.0).astype(BF16)
    running = jnp.zeros((T, NH), F32)
    for _ in range(3):
        piece = rate.astype(BF16)
        running = running + jnp.dot(tri, piece, preferred_element_type=F32)
        rate = rate - piece.astype(F32)
    from_start = jnp.exp(running)
    to_end = jnp.exp(running[T - 1 : T] - running) * step
    return step, running, from_start, to_end


def base_of(own, sc_ref):
    return HALF * sc_ref[0] if own else HALF * (1 - sc_ref[0])


def columns(base, i, width):
    return pl.ds(pl.multiple_of((base + i) * width, width), width)


def states_kernel(own, sc_ref, *refs):
    if own:
        aux_ref, kept, tokens, refs = refs[0], refs[1:6], refs[6:11], refs[11:]
        st_ref, part_hbm, e_ref, used, (sem, sem_out) = refs[0], refs[1], refs[2], refs[3:8], refs[8:]
        early = KEPT
    else:
        dt_hbm, bias_hbm, alog_hbm = refs[:3]
        tokens = refs[3:8]
        st_ref, aux_ref, aux_hbm = refs[8:11]
        kept = refs[11:16]
        e_ref = refs[16]
        used = refs[17:22]
        small = refs[22:25]
        sem, sem_small, sem_kept = refs[25:]
        early = 0
    base = base_of(own, sc_ref)
    stores = []

    def loads(first, groups, targets, sems):
        rows = []
        for k, i in enumerate(groups):
            row = []
            for j, (src, dst) in enumerate(zip(tokens, targets)):
                cut = columns(first, i, dst.shape[-1])
                row.append(pltpu.make_async_copy(src.at[:, cut], dst.at[k], sems.at[k, j]))
                row[-1].start()
            rows.append(row)
        return rows

    if not own:
        smalls = [
            pltpu.make_async_copy(s, d, sem_small.at[k])
            for k, (s, d) in enumerate(zip((dt_hbm, bias_hbm, alog_hbm), small))
        ]
        for copy in smalls:
            copy.start()
    copies = loads(base, range(early, HALF), used, sem)
    fill_spread(e_ref)
    if not own:
        for copy in smalls:
            copy.wait()
        for k, v in enumerate(steps_of(*small)):
            aux_ref[k] = v
        stores.append(pltpu.make_async_copy(aux_ref, aux_hbm, sem_small.at[3]))
        stores[0].start()
    from_start = pair_up(to_half(aux_ref[2], base))
    to_end = pair_up(to_half(aux_ref[3], base))
    for i in range(HALF):
        if i >= early:
            for copy in copies[i - early]:
                copy.wait()
        if not own and i == 0:
            ahead = loads(base_of(True, sc_ref), range(KEPT), kept, sem_kept)
        at = i if i < early else i - early
        b_ref, x_ref, c_ref, z_ref, og_ref = [
            r.at[at] for r in (kept if i < early else used)
        ]
        here = slice(i * N, (i + 1) * N)
        te = of_group(to_end, i)
        fs = of_group(from_start, i)
        bt = b_ref[...].T
        ct = c_ref[...].T
        for k in range(W // CHUNK):
            cut = slice(k * CHUNK, (k + 1) * CHUNK)
            e = e_ref[:, cut]
            xs = x_ref[:, cut].astype(F32) * jnp.dot(te, e, preferred_element_type=F32)
            st_ref[here, cut] = jnp.dot(
                bt, xs.astype(BF16), preferred_element_type=F32
            ).astype(BF16)
            gate = silu(z_ref[:, cut].astype(F32))
            hg = (og_ref[:, cut].astype(F32) * gate).astype(BF16)
            gs = hg.astype(F32) * jnp.dot(fs, e, preferred_element_type=F32)
            st_ref[here, slice(W + k * CHUNK, W + (k + 1) * CHUNK)] = jnp.dot(
                ct, gs.astype(BF16), preferred_element_type=F32
            ).astype(BF16)
        decay = jnp.broadcast_to(fs[T - 16 : T].astype(F32)[15:16], (N, LANES))
        st_ref[here, 2 * W :] = decay.astype(BF16)
        if own:
            stores += part_copies(st_ref, part_hbm, here, sc_ref[0], sem_out.at[i])
            for store in stores[-2:]:
                store.start()
    if not own:
        for row in ahead:
            for copy in row:
                copy.wait()
    for store in stores:
        store.wait()


def part_copies(st_ref, part_hbm, here, which, sem):
    cut = pl.ds(pl.multiple_of(which * W, W), W)
    return [
        pltpu.make_async_copy(st_ref.at[here, cut], part_hbm.at[here, :W], sem.at[0]),
        pltpu.make_async_copy(st_ref.at[here, 2 * W :], part_hbm.at[here, W:], sem.at[1]),
    ]


STATE = jax.ShapeDtypeStruct((HALF * N, WIDE), BF16)
PART = pltpu.HBM((HALF * N, W + LANES), BF16)


def token_shapes(groups):
    return [(groups, T, width) for width in (N, W, N, W, W)]


def states_send(sc, dt, bias, alog, *tokens):
    aux = jax.ShapeDtypeStruct((4, T, NH), F32)
    return pl.pallas_call(
        functools.partial(states_kernel, False),
        in_specs=[SMEM_SPEC] + [HBM_SPEC] * 8,
        out_specs=[VMEM_SPEC, VMEM_SPEC, HBM_SPEC] + [VMEM_SPEC] * 5,
        out_shape=[STATE, aux, pltpu.HBM((4, T, NH), F32)]
        + [jax.ShapeDtypeStruct(s, BF16) for s in token_shapes(KEPT)],
        scratch_shapes=[SPREAD]
        + [pltpu.VMEM(s, BF16) for s in token_shapes(HALF)]
        + [pltpu.VMEM((T, NH), BF16), pltpu.VMEM((1, NH), F32), pltpu.VMEM((1, NH), F32)]
        + [pltpu.SemaphoreType.DMA((HALF, 5)), pltpu.SemaphoreType.DMA((4,))]
        + [pltpu.SemaphoreType.DMA((KEPT, 5))],
        compiler_params=params(24),
        name="states_send",
    )(sc, *[in_hbm(a) for a in (dt, bias, alog, *tokens)])


def states_keep(sc, aux, kept, tokens):
    return pl.pallas_call(
        functools.partial(states_kernel, True),
        in_specs=[SMEM_SPEC] + [VMEM_SPEC] * 6 + [HBM_SPEC] * 5,
        out_specs=[VMEM_SPEC, HBM_SPEC],
        out_shape=[STATE, PART],
        scratch_shapes=[SPREAD]
        + [pltpu.VMEM(s, BF16) for s in token_shapes(HALF - KEPT)]
        + [pltpu.SemaphoreType.DMA((HALF - KEPT, 5)), pltpu.SemaphoreType.DMA((HALF, 2))],
        compiler_params=params(12),
        name="states_keep",
    )(sc, aux, *kept, *[in_hbm(a) for a in tokens])


def decay_row(state_ref, at, e_ref):
    pairs = state_ref[at : at + 16, 2 * W :]
    return jnp.dot(pairs, e_ref[...], preferred_element_type=F32)[0:1]


def merge_kernel(sc_ref, own_ref, got_ref, out_hbm, part_hbm, e_ref, out_ref, sem, sem_out):
    fill_spread(e_ref)
    core = sc_ref[0]

    def merge(r0, r1):
        stores = []
        for i in range(HALF):
            here = slice(i * N, (i + 1) * N)
            there = slice(i * N // 8, (i + 1) * N // 8)
            d0 = decay_row(r0, i * N, e_ref)
            d1 = decay_row(r1, i * N, e_ref)
            for k in range(W // CHUNK):
                cut = slice(k * CHUNK, (k + 1) * CHUNK)
                forward = d1[:, cut] * r0[here, cut].astype(F32) + r1[here, cut].astype(F32)
                out_ref[there, :, cut] = forward.reshape(N // 8, 8, CHUNK).astype(BF16)
                back = slice(W + k * CHUNK, W + (k + 1) * CHUNK)
                backward = r0[here, back].astype(F32) + d0[:, cut] * r1[here, back].astype(F32)
                out_ref[there, :, back] = backward.reshape(N // 8, 8, CHUNK).astype(BF16)
            p0 = r0[i * N : i * N + 16, 2 * W :].astype(F32)
            p1 = r1[i * N : i * N + 16, 2 * W :].astype(F32)
            p0 = p0 + pltpu.roll(p0, 64, 1)
            p1 = p1 + pltpu.roll(p1, 64, 1)
            both = pair_up(p0 * p1)[0:8]
            both = jnp.broadcast_to(both[None], (N // 8, 8, LANES))
            out_ref[there, :, 2 * W :] = both.astype(BF16)
            stores.append(pltpu.make_async_copy(out_ref.at[there], out_hbm.at[there], sem_out.at[i]))
            stores[-1].start()
        stores += part_copies(got_ref, part_hbm, slice(0, HALF * N), 1 - core, sem)
        for store in stores[-2:]:
            store.start()
        for store in stores:
            store.wait()

    @pl.when(core == 0)
    def _():
        merge(own_ref, got_ref)

    @pl.when(core != 0)
    def _():
        merge(got_ref, own_ref)


def merge(sc, own, got):
    return pl.pallas_call(
        merge_kernel,
        in_specs=[SMEM_SPEC, VMEM_SPEC, VMEM_SPEC],
        out_specs=[HBM_SPEC, HBM_SPEC],
        out_shape=[pltpu.HBM((HALF * N // 8, 8, WIDE), BF16), PART],
        scratch_shapes=[
            SPREAD,
            pltpu.VMEM((HALF * N // 8, 8, WIDE), BF16),
            pltpu.SemaphoreType.DMA((2,)),
            pltpu.SemaphoreType.DMA((HALF,)),
        ],
        compiler_params=params(16),
        name="merge_cores",
    )(sc, own, got)


def scan_kernel(chips, in_ref, after_ref, out_hbm, e_ref, d_ref, out_ref, sem):
    fill_spread(e_ref)
    pairs = in_ref[:, :, 2 * W :].astype(F32).reshape(chips * 8, LANES).astype(BF16)
    d_ref[...] = jnp.dot(pairs, e_ref[...], preferred_element_type=F32).reshape(chips, 8, W)
    zero = jnp.zeros((8, W), F32)

    def forward(k, e):
        out_ref[k, :, :W] = e.astype(BF16)
        return d_ref[k] * e + in_ref[k, :, :W].astype(F32)

    def backward(k, l):
        j = chips - 1 - k
        out_ref[j, :, W:] = l.astype(BF16)
        return d_ref[j] * l + in_ref[j, :, W : 2 * W].astype(F32)

    parts = ((0, chips, slice(0, W)), (chips // 2, chips, slice(W, 2 * W)), (0, chips // 2, slice(W, 2 * W)))
    stores = [
        pltpu.make_async_copy(out_ref.at[a:b, :, cut], out_hbm.at[a:b, :, cut], sem.at[k])
        for k, (a, b, cut) in enumerate(parts)
    ]
    lax.fori_loop(0, chips, forward, zero, unroll=8)
    stores[0].start()
    l = lax.fori_loop(0, chips // 2, backward, zero, unroll=8)
    stores[1].start()
    lax.fori_loop(chips // 2, chips, backward, l, unroll=8)
    stores[2].start()
    for store in stores:
        store.wait()


def scan(parts, after):
    chips = parts.shape[0]
    return pl.pallas_call(
        functools.partial(scan_kernel, chips),
        in_specs=[VMEM_SPEC, HBM_SPEC],
        out_specs=HBM_SPEC,
        out_shape=pltpu.HBM((chips, 8, 2 * W), BF16),
        scratch_shapes=[
            SPREAD,
            pltpu.VMEM((chips, 8, W), F32),
            pltpu.VMEM((chips, 8, 2 * W), BF16),
            pltpu.SemaphoreType.DMA((3,)),
        ],
        compiler_params=params(16),
        name="scan_chips",
    )(parts, in_hbm(after))


def local_kernel(
    own, sc_ref, aux_ref, skip_ref, got_ref, b_hbm, x_hbm, c_hbm, z_hbm, og_hbm, *refs
):
    if own:
        results, refs = refs[:7], refs[7:]
        fetched = ()
    else:
        ready, results, fetched, refs = refs[:5], refs[5:12], refs[12:20], refs[20:]
    y_ref, dx_ref, xs_ref, gs_ref, pair_ref, db_ref, dc_ref = results
    (
    e_ref, x_ref, z_ref, og_ref, b_ref, c_ref, ysum_ref, dxsum_ref, hg_ref,
    runc_ref, run_ref, step_ref, plain_ref, sem, *more,
    ) = refs
    base = base_of(own, sc_ref)
    core = sc_ref[0]
    copies = []
    if not own:
        first = base_of(True, sc_ref)
        sources = [r.at[:, columns(first, 0, w)] for r, w in ((b_hbm, N), (c_hbm, N), (z_hbm, W))]
        sources += [r.at[0] for r in ready]
        for k, (src, dst) in enumerate(zip(sources, fetched)):
            copies.append(pltpu.make_async_copy(src, dst, more[0].at[k]))
            copies[-1].start()
    for i in range(HALF):
        for k, (src, dst, width) in enumerate(
            (
                (b_hbm, b_ref, N),
                (x_hbm, x_ref, W),
                (c_hbm, c_ref, N),
                (z_hbm, z_ref, W),
                (og_hbm, og_ref, W),
            )
        ):
            copies.append(
                pltpu.make_async_copy(src.at[:, columns(base, i, width)], dst.at[i], sem.at[i, k])
            )
            copies[-1].start()
    fill_spread(e_ref)
    start = to_half(aux_ref[2], base)
    end = to_half(aux_ref[3], base)
    gain = to_half(jnp.broadcast_to(skip_ref[...], (16, NH)), base)
    run = to_half(aux_ref[1], base)
    run_t = run.T
    step_t = to_half(aux_ref[0], base).T
    for i in range(HALF):
        decay = got_ref[i * N : i * N + 16, W:].astype(F32)
        decay = (decay + pltpu.roll(decay, 64, 1))[0:1]
        fs, te, skip, run_c = [pltpu.roll(v, LANES - PER * i, 1) if i else v for v in (start, end, gain, run)]
        plain_ref[i, 0:T] = pair_up(fs).astype(BF16)
        plain_ref[i, T : 2 * T] = pair_up(te).astype(BF16)
        plain_ref[i, 2 * T : 2 * T + 16] = pair_up(skip).astype(BF16)
        pair_ref[i, 0:T] = pair_up(jnp.where(core == 0, fs, fs * decay)).astype(BF16)
        pair_ref[i, T : 2 * T] = pair_up(jnp.where(core == 0, te * decay, te)).astype(BF16)
        runc_ref[i] = run_c
        run_ref[i] = run_t[i * PER : (i + 1) * PER]
        step_ref[i] = step_t[i * PER : (i + 1) * PER]
    for copy in copies:
        copy.wait()
    row = lax.broadcasted_iota(jnp.int32, (T, T), 0)
    col = lax.broadcasted_iota(jnp.int32, (T, T), 1)
    below = row >= col
    left = col < P_SIZE

    def one_group(i, unused):
        b, c = b_ref[i], c_ref[i]
        cb = lax.dot_general(c, b, NT, preferred_element_type=F32)
        run_cols, run_rows, step_rows = runc_ref[i], run_ref[i], step_ref[i]
        mass = jnp.zeros((T, T), F32)
        for pair in range(PER // 2):
            here = slice(pair * LANES, (pair + 1) * LANES)
            e = e_ref[:, here]
            both = jnp.dot(pair_ref[i], e, preferred_element_type=F32)
            skip = jnp.dot(plain_ref[i, 2 * T : 2 * T + 16], e, preferred_element_type=F32)[0:1]
            x = x_ref[i, :, here]
            g = (og_ref[i, :, here].astype(F32) * silu(z_ref[i, :, here].astype(F32))).astype(BF16)
            hg_ref[:, here] = g
            gs_ref[i, :, here] = (g.astype(F32) * both[0:T]).astype(BF16)
            xs_ref[i, :, here] = (x.astype(F32) * both[T : 2 * T]).astype(BF16)
            ys, dxs = [], []
            for k in range(2):
                j = 2 * pair + k
                gap = run_cols[:, j : j + 1] - run_rows[j : j + 1, :]
                weight = jnp.exp(jnp.where(below, gap, -1e30)) * step_rows[j : j + 1, :]
                mine = left if k == 0 else ~left
                inner = lax.dot_general(
                    jnp.where(mine, g, jnp.zeros_like(g)), x, NT, preferred_element_type=F32
                )
                mass = mass + weight * inner
                joint = (weight * cb).astype(BF16)
                ys.append(jnp.dot(joint, x, preferred_element_type=F32))
                dxs.append(jnp.dot(joint.T, g, preferred_element_type=F32))
            ysum_ref[:, here] = jnp.where(left, ys[0], ys[1]) + skip * x.astype(F32)
            dxsum_ref[:, here] = jnp.where(left, dxs[0], dxs[1]) + skip * g.astype(F32)
        high = mass.astype(BF16)
        low = (mass - high.astype(F32)).astype(BF16)
        dc_ref[i] = jnp.dot(high, b, preferred_element_type=F32) + jnp.dot(
            low, b, preferred_element_type=F32
        )
        db_ref[i] = jnp.dot(high.T, c, preferred_element_type=F32) + jnp.dot(
            low.T, c, preferred_element_type=F32
        )
        rows = pl.ds(pl.multiple_of(i * N, N), N)

        @pl.when(core != 0)
        def _():
            partner = got_ref[rows, :W]
            fs = jnp.dot(plain_ref[i, 0:T], e_ref[...], preferred_element_type=F32)
            ysum_ref[...] += fs * jnp.dot(c, partner, preferred_element_type=F32)
            gs = (hg_ref[...].astype(F32) * fs).astype(BF16)
            dc_ref[i] += lax.dot_general(gs, partner, NT, preferred_element_type=F32)

        @pl.when(core == 0)
        def _():
            partner = got_ref[rows, :W]
            te = jnp.dot(plain_ref[i, T : 2 * T], e_ref[...], preferred_element_type=F32)
            dxsum_ref[...] += te * jnp.dot(b, partner, preferred_element_type=F32)
            xs = (x_ref[i].astype(F32) * te).astype(BF16)
            db_ref[i] += lax.dot_general(xs, partner, NT, preferred_element_type=F32)

        y_ref[i] = ysum_ref[...].astype(BF16)
        dx_ref[i] = dxsum_ref[...].astype(BF16)
        return unused

    lax.fori_loop(0, HALF, one_group, 0)


FETCHED = (
    [((T, N), BF16)] * 2 + [((T, W), BF16)] * 5 + [((2 * T, LANES), BF16)]
)


def local(own, sc, aux, skip, got, tokens, ready=()):
    wide = pltpu.HBM((HALF, T, W), BF16)
    thin = pltpu.HBM((HALF, T, N), F32)
    args = [in_hbm(a) for a in (aux, skip, got, *tokens, *ready)]
    fetched = [] if own else [jax.ShapeDtypeStruct(*f) for f in FETCHED]
    return pl.pallas_call(
        functools.partial(local_kernel, own),
        in_specs=[SMEM_SPEC, VMEM_SPEC, VMEM_SPEC, VMEM_SPEC] + [HBM_SPEC] * (5 + len(ready)),
        out_specs=[VMEM_SPEC] * (7 + len(fetched)),
        out_shape=[wide] * 4 + [pltpu.HBM((HALF, 2 * T, LANES), BF16)] + [thin] * 2 + fetched,
        scratch_shapes=[SPREAD]
        + [pltpu.VMEM((HALF, T, W), BF16)] * 3
        + [pltpu.VMEM((HALF, T, N), BF16)] * 2
        + [pltpu.VMEM((T, W), F32)] * 2
        + [pltpu.VMEM((T, W), BF16)]
        + [pltpu.VMEM((HALF, T, LANES), F32)]
        + [pltpu.VMEM((HALF, PER, T), F32)] * 2
        + [pltpu.VMEM((HALF, 2 * T + 16, LANES), BF16)]
        + [pltpu.SemaphoreType.DMA((HALF, 5))]
        + ([] if own else [pltpu.SemaphoreType.DMA((len(FETCHED),))]),
        compiler_params=params(24),
        name="local_own" if own else "local_other",
    )(sc, *args)


def final_kernel(own, sc_ref, el_ref, *refs):
    if own:
        b0, c0, z0, y0, dx0, xs0, gs0, pair0 = refs[:8]
        fetched = (b0, c0, pair0, y0, z0, dx0, xs0, gs0)
        refs = refs[8:]
        sources, others, refs = refs[:10], refs[10:20], refs[20:]
        out_hbm, dx_hbm, db_hbm, dc_hbm = refs[:4]
        kept, refs = refs[4:14], refs[14:]
        e_ref, targets, refs = refs[0], refs[1:11], refs[11:]
        out_ref, dx_ref, db_ref, dc_ref, sem_out, sem_in = refs
    else:
        targets, refs = refs[:10], refs[14:]
        out_hbm, dx_hbm, db_hbm, dc_hbm = refs[:4]
        e_ref, out_ref, dx_ref, db_ref, dc_ref, sem_out = refs[4:]
    base = base_of(own, sc_ref)

    def loads(first, srcs, dsts, sems, skip=()):
        rows = []
        for i in range(HALF):
            row = []
            for k, (src, dst) in enumerate(zip(srcs, dsts)):
                if i == 0 and k in skip:
                    continue
                if k in (0, 1, 4):
                    src = src.at[:, columns(first, i, W if k == 4 else N)]
                else:
                    src = src.at[i]
                row.append(pltpu.make_async_copy(src, dst.at[i], sems.at[i, k]))
                row[-1].start()
            rows.append(row)
        return rows

    copies = loads(base, sources, targets, sem_in.at[0], range(8)) if own else []
    ahead = []
    fill_spread(e_ref)
    stores = []
    for i in range(HALF):
        if own:
            for load in copies[i] if i else ():
                load.wait()
            if i == 1:
                ahead = loads(base_of(False, sc_ref), others, kept, sem_in.at[1])
        group = [r.at[i] for r in targets]
        if own and i == 0:
            group[:8] = fetched
        b_ref, c_ref, pair_ref, y_ref, z_ref, dxl_ref, xs_ref, gs_ref, dbl_ref, dcl_ref = group
        b, c = b_ref[...], c_ref[...]
        rows = slice(i * N, (i + 1) * N)
        for k in range(W // CHUNK):
            cut = slice(k * CHUNK, (k + 1) * CHUNK)
            far = slice(W + k * CHUNK, W + (k + 1) * CHUNK)
            scale = jnp.dot(pair_ref[...], e_ref[:, cut], preferred_element_type=F32)
            mixed = y_ref[:, cut].astype(F32) + scale[0:T] * jnp.dot(
                c, el_ref[rows, cut], preferred_element_type=F32
            )
            mixed = mixed.astype(BF16).astype(F32)
            out_ref[i, :, cut] = (mixed * silu(z_ref[:, cut].astype(F32))).astype(BF16)
            dx_ref[i, :, cut] = dxl_ref[:, cut].astype(F32) + scale[T : 2 * T] * jnp.dot(
                b, el_ref[rows, far], preferred_element_type=F32
            )
        for load in copies[0] if own and i == 0 else ():
            load.wait()
        db_ref[i] = dbl_ref[...] + lax.dot_general(
            xs_ref[...], el_ref[rows, W:], NT, preferred_element_type=F32
        )
        dc_ref[i] = dcl_ref[...] + lax.dot_general(
            gs_ref[...], el_ref[rows, :W], NT, preferred_element_type=F32
        )
        for k, (src, dst, width) in enumerate(
            ((out_ref, out_hbm, W), (dx_ref, dx_hbm, W), (db_ref, db_hbm, N), (dc_ref, dc_hbm, N))
        ):
            stores.append(
                pltpu.make_async_copy(src.at[i], dst.at[:, columns(base, i, width)], sem_out.at[i, k])
            )
            stores[-1].start()
    for row in ahead:
        for load in row:
            load.wait()
    for store in stores:
        store.wait()


LOADED = [
    ((HALF, T, N), BF16),
    ((HALF, T, N), BF16),
    ((HALF, 2 * T, LANES), BF16),
    ((HALF, T, W), BF16),
    ((HALF, T, W), BF16),
    ((HALF, T, W), BF16),
    ((HALF, T, W), BF16),
    ((HALF, T, W), BF16),
    ((HALF, T, N), F32),
    ((HALF, T, N), F32),
]
RESULTS = [
    ((T, NH * P_SIZE), BF16),
    ((T, NH * P_SIZE), F32),
    ((T, NG * N), F32),
    ((T, NG * N), F32),
]
STAGED = [
    pltpu.VMEM((HALF, T, W), BF16),
    pltpu.VMEM((HALF, T, W), F32),
    pltpu.VMEM((HALF, T, N), F32),
    pltpu.VMEM((HALF, T, N), F32),
    pltpu.SemaphoreType.DMA((HALF, 4)),
]


def in_order(local_parts, z, b, c):
    y, dx, xs, gs, pairs, db, dc = local_parts
    return [in_hbm(a) for a in (b, c, pairs, y, z, dx, xs, gs, db, dc)]


def final_own(sc, el, fetched, own_parts, other_parts):
    return pl.pallas_call(
        functools.partial(final_kernel, True),
        in_specs=[SMEM_SPEC, VMEM_SPEC] + [VMEM_SPEC] * 8 + [HBM_SPEC] * 20,
        out_specs=[HBM_SPEC] * 4 + [VMEM_SPEC] * 10,
        out_shape=[pltpu.HBM(*r) for r in RESULTS] + [jax.ShapeDtypeStruct(*r) for r in LOADED],
        scratch_shapes=[SPREAD]
        + [pltpu.VMEM(*r) for r in LOADED]
        + STAGED
        + [pltpu.SemaphoreType.DMA((2, HALF, 10))],
        compiler_params=params(24),
        name="final_own",
    )(sc, el, *fetched, *own_parts, *other_parts)


def final_other(sc, el, loaded, earlier):
    return pl.pallas_call(
        functools.partial(final_kernel, False),
        in_specs=[SMEM_SPEC, VMEM_SPEC] + [VMEM_SPEC] * 10 + [HBM_SPEC] * 4,
        out_specs=[HBM_SPEC] * 4,
        out_shape=[pltpu.HBM(*r) for r in RESULTS],
        input_output_aliases={12 + k: k for k in range(4)},
        scratch_shapes=[SPREAD] + STAGED,
        compiler_params=params(16),
        name="final_other",
    )(sc, el, *loaded, *earlier)


def body(ssm_input, gate_input, b_input, c_input, dt_raw, dt_bias, a_log, skip_gain, out_grad):
    ctx_count = lax.axis_size("ctx")
    head_count = lax.axis_size("head")
    sc = (lax.axis_index("head") % 2).astype(jnp.int32)[None]
    bias, alog, skip = dt_bias[None, :], a_log[None, :], skip_gain[None, :]
    swap = [(k, k ^ 1) for k in range(head_count)]
    chips = [[2 * k + c for k in range(ctx_count * head_count // 2)] for c in range(2)]

    def exchange(parts):
        return lax.all_to_all(
            parts, ("ctx", "head"), split_axis=0, concat_axis=0, tiled=True, axis_index_groups=chips
        )

    tokens = (b_input, ssm_input, c_input, gate_input, out_grad)
    send, aux, aux_hbm, *kept = states_send(sc, dt_raw, bias, alog, *tokens)
    got = lax.ppermute(send, "head", swap)
    keep, keep_part = states_keep(sc, aux, kept, tokens)
    payload, got_part = merge(sc, keep, got)
    gathered = exchange(payload)
    got_other = lax.ppermute(keep_part, "head", swap)
    loc_own = local(True, sc, aux_hbm, skip, got_part, tokens)
    back = exchange(scan(gathered, loc_own[6]))
    loc_other = local(False, sc, aux_hbm, skip, got_other, tokens, loc_own[:5])
    back, loc_other = lax.optimization_barrier((back, loc_other))
    el = back.reshape(HALF * N, 2 * W)
    el_other = lax.ppermute(el, "head", swap)
    shared = (gate_input, b_input, c_input)
    own_parts, other_parts = in_order(loc_own, *shared), in_order(loc_other[:7], *shared)
    outs = final_own(sc, el, loc_other[7:], own_parts, other_parts)
    return tuple(final_other(sc, el_other, outs[4:], outs[:4]))


def solution(mesh):
    row_spec = P(("ctx", "head"), None)
    in_specs = (row_spec,) * 5 + (P(), P(), P(), row_spec)
    return jax.shard_map(
        body, mesh=mesh, in_specs=in_specs, out_specs=(row_spec,) * 4, check_vma=False
    )
```

```python
import functools

import jax
import jax.numpy as jnp
from jax import lax
from jax.experimental import pallas as pl
from jax.experimental.pallas import tpu as pltpu
from jax.sharding import PartitionSpec as P

NH = 128
P_SIZE = 64
N = 128
NG = 8
PER = NH // NG
W = PER * P_SIZE
T = 128
HALF = NG // 2
LANES = 128
WIDE = 2 * W + LANES
F32 = jnp.float32
BF16 = jnp.bfloat16


MIB = 1024 * 1024
NT = (((1,), (1,)), ((), ()))
CHUNK = 256
HBM_SPEC = pl.BlockSpec(memory_space=pl.ANY)
VMEM_SPEC = pl.BlockSpec(memory_space=pltpu.VMEM)
SMEM_SPEC = pl.BlockSpec(memory_space=pltpu.SMEM)
KEPT = 3
SPREAD = pltpu.VMEM((LANES, W), BF16)


def in_hbm(values):
    return pltpu.with_memory_space_constraint(values, pltpu.HBM)


def params(mib):
    return pltpu.CompilerParams(vmem_limit_bytes=mib * MIB)


def lane(shape):
    return lax.broadcasted_iota(jnp.int32, shape, len(shape) - 1)


def fill_spread(e_ref):
    row = lax.broadcasted_iota(jnp.int32, (LANES, W), 0)
    col = lax.broadcasted_iota(jnp.int32, (LANES, W), 1)
    e_ref[...] = jnp.where((row & 63) == (col >> 6), 1.0, 0.0).astype(BF16)


def to_half(values, base):
    return pltpu.roll(values, lax.rem(LANES - PER * base, LANES), 1)


def pair_up(values):
    high = values.astype(BF16).astype(F32)
    low = values - high
    return jnp.where(lane(values.shape) < 64, high, pltpu.roll(low, 64, 1))


def of_group(pairs, i):
    if i:
        pairs = pltpu.roll(pairs, LANES - PER * i, 1)
    return pairs.astype(BF16)


def silu(v):
    return v * (0.5 * jnp.tanh(0.5 * v) + 0.5)


def steps_of(dt_ref, bias_ref, alog_ref):
    u = jnp.exp(dt_ref[...].astype(F32) + bias_ref[...])
    one = 1.0 + u
    step = jnp.where(one == 1.0, u, jnp.log(one) * (u / jnp.where(one == 1.0, 1.0, one - 1.0)))
    rate = -step * jnp.exp(alog_ref[...])
    row = lax.broadcasted_iota(jnp.int32, (T, T), 0)
    col = lax.broadcasted_iota(jnp.int32, (T, T), 1)
    tri = jnp.where(row >= col, 1.0, 0.0).astype(BF16)
    running = jnp.zeros((T, NH), F32)
    for _ in range(3):
        piece = rate.astype(BF16)
        running = running + jnp.dot(tri, piece, preferred_element_type=F32)
        rate = rate - piece.astype(F32)
    from_start = jnp.exp(running)
    to_end = jnp.exp(running[T - 1 : T] - running) * step
    return step, running, from_start, to_end


def base_of(own, sc_ref):
    return HALF * sc_ref[0] if own else HALF * (1 - sc_ref[0])


def columns(base, i, width):
    return pl.ds(pl.multiple_of((base + i) * width, width), width)


def states_kernel(own, sc_ref, *refs):
    if own:
        aux_ref, kept, tokens, refs = refs[0], refs[1:6], refs[6:11], refs[11:]
        st_ref, part_hbm, e_ref, used, (sem, sem_out) = refs[0], refs[1], refs[2], refs[3:8], refs[8:]
        early = KEPT
    else:
        dt_hbm, bias_hbm, alog_hbm = refs[:3]
        tokens = refs[3:8]
        st_ref, aux_ref, aux_hbm = refs[8:11]
        kept = refs[11:16]
        e_ref = refs[16]
        used = refs[17:22]
        small = refs[22:25]
        sem, sem_small, sem_kept = refs[25:]
        early = 0
    base = base_of(own, sc_ref)
    stores = []

    def loads(first, groups, targets, sems):
        rows = []
        for k, i in enumerate(groups):
            row = []
            for j, (src, dst) in enumerate(zip(tokens, targets)):
                cut = columns(first, i, dst.shape[-1])
                row.append(pltpu.make_async_copy(src.at[:, cut], dst.at[k], sems.at[k, j]))
                row[-1].start()
            rows.append(row)
        return rows

    if not own:
        smalls = [
            pltpu.make_async_copy(s, d, sem_small.at[k])
            for k, (s, d) in enumerate(zip((dt_hbm, bias_hbm, alog_hbm), small))
        ]
        for copy in smalls:
            copy.start()
    copies = loads(base, range(early, HALF), used, sem)
    fill_spread(e_ref)
    if not own:
        for copy in smalls:
            copy.wait()
        for k, v in enumerate(steps_of(*small)):
            aux_ref[k] = v
        stores.append(pltpu.make_async_copy(aux_ref, aux_hbm, sem_small.at[3]))
        stores[0].start()
    from_start = pair_up(to_half(aux_ref[2], base))
    to_end = pair_up(to_half(aux_ref[3], base))
    for i in range(HALF):
        if i >= early:
            for copy in copies[i - early]:
                copy.wait()
        if not own and i == 0:
            ahead = loads(base_of(True, sc_ref), range(KEPT), kept, sem_kept)
        at = i if i < early else i - early
        b_ref, x_ref, c_ref, z_ref, og_ref = [
            r.at[at] for r in (kept if i < early else used)
        ]
        here = slice(i * N, (i + 1) * N)
        te = of_group(to_end, i)
        fs = of_group(from_start, i)
        bt = b_ref[...].T
        ct = c_ref[...].T
        for k in range(W // CHUNK):
            cut = slice(k * CHUNK, (k + 1) * CHUNK)
            e = e_ref[:, cut]
            xs = x_ref[:, cut].astype(F32) * jnp.dot(te, e, preferred_element_type=F32)
            st_ref[here, cut] = jnp.dot(
                bt, xs.astype(BF16), preferred_element_type=F32
            ).astype(BF16)
            gate = silu(z_ref[:, cut].astype(F32))
            hg = (og_ref[:, cut].astype(F32) * gate).astype(BF16)
            gs = hg.astype(F32) * jnp.dot(fs, e, preferred_element_type=F32)
            st_ref[here, slice(W + k * CHUNK, W + (k + 1) * CHUNK)] = jnp.dot(
                ct, gs.astype(BF16), preferred_element_type=F32
            ).astype(BF16)
        decay = jnp.broadcast_to(fs[T - 16 : T].astype(F32)[15:16], (N, LANES))
        st_ref[here, 2 * W :] = decay.astype(BF16)
        if own:
            stores += part_copies(st_ref, part_hbm, here, sc_ref[0], sem_out.at[i])
            for store in stores[-2:]:
                store.start()
    if not own:
        for row in ahead:
            for copy in row:
                copy.wait()
    for store in stores:
        store.wait()


def part_copies(st_ref, part_hbm, here, which, sem):
    cut = pl.ds(pl.multiple_of(which * W, W), W)
    return [
        pltpu.make_async_copy(st_ref.at[here, cut], part_hbm.at[here, :W], sem.at[0]),
        pltpu.make_async_copy(st_ref.at[here, 2 * W :], part_hbm.at[here, W:], sem.at[1]),
    ]


STATE = jax.ShapeDtypeStruct((HALF * N, WIDE), BF16)
PART = pltpu.HBM((HALF * N, W + LANES), BF16)


def token_shapes(groups):
    return [(groups, T, width) for width in (N, W, N, W, W)]


def states_send(sc, dt, bias, alog, *tokens):
    aux = jax.ShapeDtypeStruct((4, T, NH), F32)
    return pl.pallas_call(
        functools.partial(states_kernel, False),
        in_specs=[SMEM_SPEC] + [HBM_SPEC] * 8,
        out_specs=[VMEM_SPEC, VMEM_SPEC, HBM_SPEC] + [VMEM_SPEC] * 5,
        out_shape=[STATE, aux, pltpu.HBM((4, T, NH), F32)]
        + [jax.ShapeDtypeStruct(s, BF16) for s in token_shapes(KEPT)],
        scratch_shapes=[SPREAD]
        + [pltpu.VMEM(s, BF16) for s in token_shapes(HALF)]
        + [pltpu.VMEM((T, NH), BF16), pltpu.VMEM((1, NH), F32), pltpu.VMEM((1, NH), F32)]
        + [pltpu.SemaphoreType.DMA((HALF, 5)), pltpu.SemaphoreType.DMA((4,))]
        + [pltpu.SemaphoreType.DMA((KEPT, 5))],
        compiler_params=params(24),
        name="states_send",
    )(sc, *[in_hbm(a) for a in (dt, bias, alog, *tokens)])


def states_keep(sc, aux, kept, tokens):
    return pl.pallas_call(
        functools.partial(states_kernel, True),
        in_specs=[SMEM_SPEC] + [VMEM_SPEC] * 6 + [HBM_SPEC] * 5,
        out_specs=[VMEM_SPEC, HBM_SPEC],
        out_shape=[STATE, PART],
        scratch_shapes=[SPREAD]
        + [pltpu.VMEM(s, BF16) for s in token_shapes(HALF - KEPT)]
        + [pltpu.SemaphoreType.DMA((HALF - KEPT, 5)), pltpu.SemaphoreType.DMA((HALF, 2))],
        compiler_params=params(12),
        name="states_keep",
    )(sc, aux, *kept, *[in_hbm(a) for a in tokens])


def decay_row(state_ref, at, e_ref):
    pairs = state_ref[at : at + 16, 2 * W :]
    return jnp.dot(pairs, e_ref[...], preferred_element_type=F32)[0:1]


def merge_kernel(sc_ref, own_ref, got_ref, out_hbm, part_hbm, e_ref, out_ref, sem, sem_out):
    fill_spread(e_ref)
    core = sc_ref[0]

    def merge(r0, r1):
        stores = []
        for i in range(HALF):
            here = slice(i * N, (i + 1) * N)
            there = slice(i * N // 8, (i + 1) * N // 8)
            d0 = decay_row(r0, i * N, e_ref)
            d1 = decay_row(r1, i * N, e_ref)
            for k in range(W // CHUNK):
                cut = slice(k * CHUNK, (k + 1) * CHUNK)
                forward = d1[:, cut] * r0[here, cut].astype(F32) + r1[here, cut].astype(F32)
                out_ref[there, :, cut] = forward.reshape(N // 8, 8, CHUNK).astype(BF16)
                back = slice(W + k * CHUNK, W + (k + 1) * CHUNK)
                backward = r0[here, back].astype(F32) + d0[:, cut] * r1[here, back].astype(F32)
                out_ref[there, :, back] = backward.reshape(N // 8, 8, CHUNK).astype(BF16)
            p0 = r0[i * N : i * N + 16, 2 * W :].astype(F32)
            p1 = r1[i * N : i * N + 16, 2 * W :].astype(F32)
            p0 = p0 + pltpu.roll(p0, 64, 1)
            p1 = p1 + pltpu.roll(p1, 64, 1)
            both = pair_up(p0 * p1)[0:8]
            both = jnp.broadcast_to(both[None], (N // 8, 8, LANES))
            out_ref[there, :, 2 * W :] = both.astype(BF16)
            stores.append(pltpu.make_async_copy(out_ref.at[there], out_hbm.at[there], sem_out.at[i]))
            stores[-1].start()
        stores += part_copies(got_ref, part_hbm, slice(0, HALF * N), 1 - core, sem)
        for store in stores[-2:]:
            store.start()
        for store in stores:
            store.wait()

    @pl.when(core == 0)
    def _():
        merge(own_ref, got_ref)

    @pl.when(core != 0)
    def _():
        merge(got_ref, own_ref)


def merge(sc, own, got):
    return pl.pallas_call(
        merge_kernel,
        in_specs=[SMEM_SPEC, VMEM_SPEC, VMEM_SPEC],
        out_specs=[HBM_SPEC, HBM_SPEC],
        out_shape=[pltpu.HBM((HALF * N // 8, 8, WIDE), BF16), PART],
        scratch_shapes=[
            SPREAD,
            pltpu.VMEM((HALF * N // 8, 8, WIDE), BF16),
            pltpu.SemaphoreType.DMA((2,)),
            pltpu.SemaphoreType.DMA((HALF,)),
        ],
        compiler_params=params(16),
        name="merge_cores",
    )(sc, own, got)


def scan_kernel(chips, in_ref, after_ref, out_hbm, e_ref, d_ref, out_ref, sem):
    fill_spread(e_ref)
    pairs = in_ref[:, :, 2 * W :].astype(F32).reshape(chips * 8, LANES).astype(BF16)
    d_ref[...] = jnp.dot(pairs, e_ref[...], preferred_element_type=F32).reshape(chips, 8, W)
    zero = jnp.zeros((8, W), F32)

    def forward(k, e):
        out_ref[k, :, :W] = e.astype(BF16)
        return d_ref[k] * e + in_ref[k, :, :W].astype(F32)

    def backward(k, l):
        j = chips - 1 - k
        out_ref[j, :, W:] = l.astype(BF16)
        return d_ref[j] * l + in_ref[j, :, W : 2 * W].astype(F32)

    parts = ((0, chips, slice(0, W)), (chips // 2, chips, slice(W, 2 * W)), (0, chips // 2, slice(W, 2 * W)))
    stores = [
        pltpu.make_async_copy(out_ref.at[a:b, :, cut], out_hbm.at[a:b, :, cut], sem.at[k])
        for k, (a, b, cut) in enumerate(parts)
    ]
    lax.fori_loop(0, chips, forward, zero, unroll=8)
    stores[0].start()
    l = lax.fori_loop(0, chips // 2, backward, zero, unroll=8)
    stores[1].start()
    lax.fori_loop(chips // 2, chips, backward, l, unroll=8)
    stores[2].start()
    for store in stores:
        store.wait()


def scan(parts, after):
    chips = parts.shape[0]
    return pl.pallas_call(
        functools.partial(scan_kernel, chips),
        in_specs=[VMEM_SPEC, HBM_SPEC],
        out_specs=HBM_SPEC,
        out_shape=pltpu.HBM((chips, 8, 2 * W), BF16),
        scratch_shapes=[
            SPREAD,
            pltpu.VMEM((chips, 8, W), F32),
            pltpu.VMEM((chips, 8, 2 * W), BF16),
            pltpu.SemaphoreType.DMA((3,)),
        ],
        compiler_params=params(16),
        name="scan_chips",
    )(parts, in_hbm(after))


def local_kernel(
    own, sc_ref, aux_ref, skip_ref, got_ref, b_hbm, x_hbm, c_hbm, z_hbm, og_hbm, *refs
):
    if own:
        results, refs = refs[:7], refs[7:]
        fetched = ()
    else:
        ready, results, fetched, refs = refs[:5], refs[5:12], refs[12:20], refs[20:]
    y_ref, dx_ref, xs_ref, gs_ref, pair_ref, db_ref, dc_ref = results
    (
    e_ref, x_ref, z_ref, og_ref, b_ref, c_ref, ysum_ref, dxsum_ref, hg_ref,
    runc_ref, run_ref, step_ref, plain_ref, sem, *more,
    ) = refs
    base = base_of(own, sc_ref)
    core = sc_ref[0]
    copies = []
    if not own:
        first = base_of(True, sc_ref)
        sources = [r.at[:, columns(first, 0, w)] for r, w in ((b_hbm, N), (c_hbm, N), (z_hbm, W))]
        sources += [r.at[0] for r in ready]
        for k, (src, dst) in enumerate(zip(sources, fetched)):
            copies.append(pltpu.make_async_copy(src, dst, more[0].at[k]))
            copies[-1].start()
    for i in range(HALF):
        for k, (src, dst, width) in enumerate(
            (
                (b_hbm, b_ref, N),
                (x_hbm, x_ref, W),
                (c_hbm, c_ref, N),
                (z_hbm, z_ref, W),
                (og_hbm, og_ref, W),
            )
        ):
            copies.append(
                pltpu.make_async_copy(src.at[:, columns(base, i, width)], dst.at[i], sem.at[i, k])
            )
            copies[-1].start()
    fill_spread(e_ref)
    start = to_half(aux_ref[2], base)
    end = to_half(aux_ref[3], base)
    gain = to_half(jnp.broadcast_to(skip_ref[...], (16, NH)), base)
    run = to_half(aux_ref[1], base)
    run_t = run.T
    step_t = to_half(aux_ref[0], base).T
    for i in range(HALF):
        decay = got_ref[i * N : i * N + 16, W:].astype(F32)
        decay = (decay + pltpu.roll(decay, 64, 1))[0:1]
        fs, te, skip, run_c = [pltpu.roll(v, LANES - PER * i, 1) if i else v for v in (start, end, gain, run)]
        plain_ref[i, 0:T] = pair_up(fs).astype(BF16)
        plain_ref[i, T : 2 * T] = pair_up(te).astype(BF16)
        plain_ref[i, 2 * T : 2 * T + 16] = pair_up(skip).astype(BF16)
        pair_ref[i, 0:T] = pair_up(jnp.where(core == 0, fs, fs * decay)).astype(BF16)
        pair_ref[i, T : 2 * T] = pair_up(jnp.where(core == 0, te * decay, te)).astype(BF16)
        runc_ref[i] = run_c
        run_ref[i] = run_t[i * PER : (i + 1) * PER]
        step_ref[i] = step_t[i * PER : (i + 1) * PER]
    for copy in copies:
        copy.wait()
    row = lax.broadcasted_iota(jnp.int32, (T, T), 0)
    col = lax.broadcasted_iota(jnp.int32, (T, T), 1)
    below = row >= col
    left = col < P_SIZE

    def one_group(i, unused):
        b, c = b_ref[i], c_ref[i]
        cb = lax.dot_general(c, b, NT, preferred_element_type=F32)
        run_cols, run_rows, step_rows = runc_ref[i], run_ref[i], step_ref[i]
        mass = jnp.zeros((T, T), F32)
        for pair in range(PER // 2):
            here = slice(pair * LANES, (pair + 1) * LANES)
            e = e_ref[:, here]
            both = jnp.dot(pair_ref[i], e, preferred_element_type=F32)
            skip = jnp.dot(plain_ref[i, 2 * T : 2 * T + 16], e, preferred_element_type=F32)[0:1]
            x = x_ref[i, :, here]
            g = (og_ref[i, :, here].astype(F32) * silu(z_ref[i, :, here].astype(F32))).astype(BF16)
            hg_ref[:, here] = g
            gs_ref[i, :, here] = (g.astype(F32) * both[0:T]).astype(BF16)
            xs_ref[i, :, here] = (x.astype(F32) * both[T : 2 * T]).astype(BF16)
            ys, dxs = [], []
            for k in range(2):
                j = 2 * pair + k
                gap = run_cols[:, j : j + 1] - run_rows[j : j + 1, :]
                weight = jnp.exp(jnp.where(below, gap, -1e30)) * step_rows[j : j + 1, :]
                mine = left if k == 0 else ~left
                inner = lax.dot_general(
                    jnp.where(mine, g, jnp.zeros_like(g)), x, NT, preferred_element_type=F32
                )
                mass = mass + weight * inner
                joint = (weight * cb).astype(BF16)
                ys.append(jnp.dot(joint, x, preferred_element_type=F32))
                dxs.append(jnp.dot(joint.T, g, preferred_element_type=F32))
            ysum_ref[:, here] = jnp.where(left, ys[0], ys[1]) + skip * x.astype(F32)
            dxsum_ref[:, here] = jnp.where(left, dxs[0], dxs[1]) + skip * g.astype(F32)
        high = mass.astype(BF16)
        low = (mass - high.astype(F32)).astype(BF16)
        dc_ref[i] = jnp.dot(high, b, preferred_element_type=F32) + jnp.dot(
            low, b, preferred_element_type=F32
        )
        db_ref[i] = jnp.dot(high.T, c, preferred_element_type=F32) + jnp.dot(
            low.T, c, preferred_element_type=F32
        )
        rows = pl.ds(pl.multiple_of(i * N, N), N)

        @pl.when(core != 0)
        def _():
            partner = got_ref[rows, :W]
            fs = jnp.dot(plain_ref[i, 0:T], e_ref[...], preferred_element_type=F32)
            ysum_ref[...] += fs * jnp.dot(c, partner, preferred_element_type=F32)
            gs = (hg_ref[...].astype(F32) * fs).astype(BF16)
            dc_ref[i] += lax.dot_general(gs, partner, NT, preferred_element_type=F32)

        @pl.when(core == 0)
        def _():
            partner = got_ref[rows, :W]
            te = jnp.dot(plain_ref[i, T : 2 * T], e_ref[...], preferred_element_type=F32)
            dxsum_ref[...] += te * jnp.dot(b, partner, preferred_element_type=F32)
            xs = (x_ref[i].astype(F32) * te).astype(BF16)
            db_ref[i] += lax.dot_general(xs, partner, NT, preferred_element_type=F32)

        y_ref[i] = ysum_ref[...].astype(BF16)
        dx_ref[i] = dxsum_ref[...].astype(BF16)
        return unused

    lax.fori_loop(0, HALF, one_group, 0)


FETCHED = (
    [((T, N), BF16)] * 2 + [((T, W), BF16)] * 5 + [((2 * T, LANES), BF16)]
)


def local(own, sc, aux, skip, got, tokens, ready=()):
    wide = pltpu.HBM((HALF, T, W), BF16)
    thin = pltpu.HBM((HALF, T, N), F32)
    args = [in_hbm(a) for a in (aux, skip, got, *tokens, *ready)]
    fetched = [] if own else [jax.ShapeDtypeStruct(*f) for f in FETCHED]
    return pl.pallas_call(
        functools.partial(local_kernel, own),
        in_specs=[SMEM_SPEC, VMEM_SPEC, VMEM_SPEC, VMEM_SPEC] + [HBM_SPEC] * (5 + len(ready)),
        out_specs=[VMEM_SPEC] * (7 + len(fetched)),
        out_shape=[wide] * 4 + [pltpu.HBM((HALF, 2 * T, LANES), BF16)] + [thin] * 2 + fetched,
        scratch_shapes=[SPREAD]
        + [pltpu.VMEM((HALF, T, W), BF16)] * 3
        + [pltpu.VMEM((HALF, T, N), BF16)] * 2
        + [pltpu.VMEM((T, W), F32)] * 2
        + [pltpu.VMEM((T, W), BF16)]
        + [pltpu.VMEM((HALF, T, LANES), F32)]
        + [pltpu.VMEM((HALF, PER, T), F32)] * 2
        + [pltpu.VMEM((HALF, 2 * T + 16, LANES), BF16)]
        + [pltpu.SemaphoreType.DMA((HALF, 5))]
        + ([] if own else [pltpu.SemaphoreType.DMA((len(FETCHED),))]),
        compiler_params=params(24),
        name="local_own" if own else "local_other",
    )(sc, *args)


def final_kernel(own, sc_ref, el_ref, *refs):
    if own:
        b0, c0, z0, y0, dx0, xs0, gs0, pair0 = refs[:8]
        fetched = (b0, c0, pair0, y0, z0, dx0, xs0, gs0)
        refs = refs[8:]
        sources, others, refs = refs[:10], refs[10:20], refs[20:]
        out_hbm, dx_hbm, db_hbm, dc_hbm = refs[:4]
        kept, refs = refs[4:14], refs[14:]
        e_ref, targets, refs = refs[0], refs[1:11], refs[11:]
        out_ref, dx_ref, db_ref, dc_ref, sem_out, sem_in = refs
    else:
        targets, refs = refs[:10], refs[14:]
        out_hbm, dx_hbm, db_hbm, dc_hbm = refs[:4]
        e_ref, out_ref, dx_ref, db_ref, dc_ref, sem_out = refs[4:]
    base = base_of(own, sc_ref)

    def loads(first, srcs, dsts, sems, skip=()):
        rows = []
        for i in range(HALF):
            row = []
            for k, (src, dst) in enumerate(zip(srcs, dsts)):
                if i == 0 and k in skip:
                    continue
                if k in (0, 1, 4):
                    src = src.at[:, columns(first, i, W if k == 4 else N)]
                else:
                    src = src.at[i]
                row.append(pltpu.make_async_copy(src, dst.at[i], sems.at[i, k]))
                row[-1].start()
            rows.append(row)
        return rows

    copies = loads(base, sources, targets, sem_in.at[0], range(8)) if own else []
    ahead = loads(base_of(False, sc_ref), others, kept, sem_in.at[1]) if own else []
    fill_spread(e_ref)
    stores = []
    for i in range(HALF):
        if own:
            for load in copies[i] if i else ():
                load.wait()
        group = [r.at[i] for r in targets]
        if own and i == 0:
            group[:8] = fetched
        b_ref, c_ref, pair_ref, y_ref, z_ref, dxl_ref, xs_ref, gs_ref, dbl_ref, dcl_ref = group
        b, c = b_ref[...], c_ref[...]
        rows = slice(i * N, (i + 1) * N)
        for k in range(W // CHUNK):
            cut = slice(k * CHUNK, (k + 1) * CHUNK)
            far = slice(W + k * CHUNK, W + (k + 1) * CHUNK)
            scale = jnp.dot(pair_ref[...], e_ref[:, cut], preferred_element_type=F32)
            mixed = y_ref[:, cut].astype(F32) + scale[0:T] * jnp.dot(
                c, el_ref[rows, cut], preferred_element_type=F32
            )
            mixed = mixed.astype(BF16).astype(F32)
            out_ref[i, :, cut] = (mixed * silu(z_ref[:, cut].astype(F32))).astype(BF16)
            dx_ref[i, :, cut] = dxl_ref[:, cut].astype(F32) + scale[T : 2 * T] * jnp.dot(
                b, el_ref[rows, far], preferred_element_type=F32
            )
        for load in copies[0] if own and i == 0 else ():
            load.wait()
        db_ref[i] = dbl_ref[...] + lax.dot_general(
            xs_ref[...], el_ref[rows, W:], NT, preferred_element_type=F32
        )
        dc_ref[i] = dcl_ref[...] + lax.dot_general(
            gs_ref[...], el_ref[rows, :W], NT, preferred_element_type=F32
        )
        for k, (src, dst, width) in enumerate(
            ((out_ref, out_hbm, W), (dx_ref, dx_hbm, W), (db_ref, db_hbm, N), (dc_ref, dc_hbm, N))
        ):
            stores.append(
                pltpu.make_async_copy(src.at[i], dst.at[:, columns(base, i, width)], sem_out.at[i, k])
            )
            stores[-1].start()
    for row in ahead:
        for load in row:
            load.wait()
    for store in stores:
        store.wait()


LOADED = [
    ((HALF, T, N), BF16),
    ((HALF, T, N), BF16),
    ((HALF, 2 * T, LANES), BF16),
    ((HALF, T, W), BF16),
    ((HALF, T, W), BF16),
    ((HALF, T, W), BF16),
    ((HALF, T, W), BF16),
    ((HALF, T, W), BF16),
    ((HALF, T, N), F32),
    ((HALF, T, N), F32),
]
RESULTS = [
    ((T, NH * P_SIZE), BF16),
    ((T, NH * P_SIZE), F32),
    ((T, NG * N), F32),
    ((T, NG * N), F32),
]
STAGED = [
    pltpu.VMEM((HALF, T, W), BF16),
    pltpu.VMEM((HALF, T, W), F32),
    pltpu.VMEM((HALF, T, N), F32),
    pltpu.VMEM((HALF, T, N), F32),
    pltpu.SemaphoreType.DMA((HALF, 4)),
]


def in_order(local_parts, z, b, c):
    y, dx, xs, gs, pairs, db, dc = local_parts
    return [in_hbm(a) for a in (b, c, pairs, y, z, dx, xs, gs, db, dc)]


def final_own(sc, el, fetched, own_parts, other_parts):
    return pl.pallas_call(
        functools.partial(final_kernel, True),
        in_specs=[SMEM_SPEC, VMEM_SPEC] + [VMEM_SPEC] * 8 + [HBM_SPEC] * 20,
        out_specs=[HBM_SPEC] * 4 + [VMEM_SPEC] * 10,
        out_shape=[pltpu.HBM(*r) for r in RESULTS] + [jax.ShapeDtypeStruct(*r) for r in LOADED],
        scratch_shapes=[SPREAD]
        + [pltpu.VMEM(*r) for r in LOADED]
        + STAGED
        + [pltpu.SemaphoreType.DMA((2, HALF, 10))],
        compiler_params=params(24),
        name="final_own",
    )(sc, el, *fetched, *own_parts, *other_parts)


def final_other(sc, el, loaded, earlier):
    return pl.pallas_call(
        functools.partial(final_kernel, False),
        in_specs=[SMEM_SPEC, VMEM_SPEC] + [VMEM_SPEC] * 10 + [HBM_SPEC] * 4,
        out_specs=[HBM_SPEC] * 4,
        out_shape=[pltpu.HBM(*r) for r in RESULTS],
        input_output_aliases={12 + k: k for k in range(4)},
        scratch_shapes=[SPREAD] + STAGED,
        compiler_params=params(16),
        name="final_other",
    )(sc, el, *loaded, *earlier)


def body(ssm_input, gate_input, b_input, c_input, dt_raw, dt_bias, a_log, skip_gain, out_grad):
    ctx_count = lax.axis_size("ctx")
    head_count = lax.axis_size("head")
    sc = (lax.axis_index("head") % 2).astype(jnp.int32)[None]
    bias, alog, skip = dt_bias[None, :], a_log[None, :], skip_gain[None, :]
    swap = [(k, k ^ 1) for k in range(head_count)]
    chips = [[2 * k + c for k in range(ctx_count * head_count // 2)] for c in range(2)]

    def exchange(parts):
        return lax.all_to_all(
            parts, ("ctx", "head"), split_axis=0, concat_axis=0, tiled=True, axis_index_groups=chips
        )

    tokens = (b_input, ssm_input, c_input, gate_input, out_grad)
    send, aux, aux_hbm, *kept = states_send(sc, dt_raw, bias, alog, *tokens)
    got = lax.ppermute(send, "head", swap)
    keep, keep_part = states_keep(sc, aux, kept, tokens)
    payload, got_part = merge(sc, keep, got)
    gathered = exchange(payload)
    got_other = lax.ppermute(keep_part, "head", swap)
    loc_own = local(True, sc, aux_hbm, skip, got_part, tokens)
    back = exchange(scan(gathered, loc_own[6]))
    loc_other = local(False, sc, aux_hbm, skip, got_other, tokens, loc_own[:5])
    back, loc_other = lax.optimization_barrier((back, loc_other))
    el = back.reshape(HALF * N, 2 * W)
    el_other = lax.ppermute(el, "head", swap)
    shared = (gate_input, b_input, c_input)
    own_parts, other_parts = in_order(loc_own, *shared), in_order(loc_other[:7], *shared)
    outs = final_own(sc, el, loc_other[7:], own_parts, other_parts)
    return tuple(final_other(sc, el_other, outs[4:], outs[:4]))


def solution(mesh):
    row_spec = P(("ctx", "head"), None)
    in_specs = (row_spec,) * 5 + (P(), P(), P(), row_spec)
    return jax.shard_map(
        body, mesh=mesh, in_specs=in_specs, out_specs=(row_spec,) * 4, check_vma=False
    )
```

```python
import functools

import jax
import jax.numpy as jnp
from jax import lax
from jax.experimental import pallas as pl
from jax.experimental.pallas import tpu as pltpu
from jax.sharding import PartitionSpec as P

NH = 128
P_SIZE = 64
N = 128
NG = 8
PER = NH // NG
W = PER * P_SIZE
T = 128
HALF = NG // 2
LANES = 128
WIDE = 2 * W + LANES
F32 = jnp.float32
BF16 = jnp.bfloat16


MIB = 1024 * 1024
NT = (((1,), (1,)), ((), ()))
CHUNK = 256
HBM_SPEC = pl.BlockSpec(memory_space=pl.ANY)
VMEM_SPEC = pl.BlockSpec(memory_space=pltpu.VMEM)
SMEM_SPEC = pl.BlockSpec(memory_space=pltpu.SMEM)
KEPT = 3
SPREAD = pltpu.VMEM((LANES, W), BF16)


def in_hbm(values):
    return pltpu.with_memory_space_constraint(values, pltpu.HBM)


def params(mib):
    return pltpu.CompilerParams(vmem_limit_bytes=mib * MIB)


def lane(shape):
    return lax.broadcasted_iota(jnp.int32, shape, len(shape) - 1)


def fill_spread(e_ref):
    row = lax.broadcasted_iota(jnp.int32, (LANES, W), 0)
    col = lax.broadcasted_iota(jnp.int32, (LANES, W), 1)
    e_ref[...] = jnp.where((row & 63) == (col >> 6), 1.0, 0.0).astype(BF16)


def to_half(values, base):
    return pltpu.roll(values, lax.rem(LANES - PER * base, LANES), 1)


def pair_up(values):
    high = values.astype(BF16).astype(F32)
    low = values - high
    return jnp.where(lane(values.shape) < 64, high, pltpu.roll(low, 64, 1))


def of_group(pairs, i):
    if i:
        pairs = pltpu.roll(pairs, LANES - PER * i, 1)
    return pairs.astype(BF16)


def silu(v):
    return v * (0.5 * jnp.tanh(0.5 * v) + 0.5)


def steps_of(dt_ref, bias_ref, alog_ref):
    u = jnp.exp(dt_ref[...].astype(F32) + bias_ref[...])
    one = 1.0 + u
    step = jnp.where(one == 1.0, u, jnp.log(one) * (u / jnp.where(one == 1.0, 1.0, one - 1.0)))
    rate = -step * jnp.exp(alog_ref[...])
    row = lax.broadcasted_iota(jnp.int32, (T, T), 0)
    col = lax.broadcasted_iota(jnp.int32, (T, T), 1)
    tri = jnp.where(row >= col, 1.0, 0.0).astype(BF16)
    running = jnp.zeros((T, NH), F32)
    for _ in range(3):
        piece = rate.astype(BF16)
        running = running + jnp.dot(tri, piece, preferred_element_type=F32)
        rate = rate - piece.astype(F32)
    from_start = jnp.exp(running)
    to_end = jnp.exp(running[T - 1 : T] - running) * step
    return step, running, from_start, to_end


def base_of(own, sc_ref):
    return HALF * sc_ref[0] if own else HALF * (1 - sc_ref[0])


def columns(base, i, width):
    return pl.ds(pl.multiple_of((base + i) * width, width), width)


def states_kernel(own, sc_ref, *refs):
    if own:
        aux_ref, kept, tokens, refs = refs[0], refs[1:6], refs[6:11], refs[11:]
        st_ref, part_hbm, e_ref, used, (sem, sem_out) = refs[0], refs[1], refs[2], refs[3:8], refs[8:]
        early = KEPT
    else:
        dt_hbm, bias_hbm, alog_hbm = refs[:3]
        tokens = refs[3:8]
        st_ref, aux_ref, aux_hbm = refs[8:11]
        kept = refs[11:16]
        e_ref = refs[16]
        used = refs[17:22]
        small = refs[22:25]
        sem, sem_small, sem_kept = refs[25:]
        early = 0
    base = base_of(own, sc_ref)
    stores = []

    def loads(first, groups, targets, sems):
        rows = []
        for k, i in enumerate(groups):
            row = []
            for j, (src, dst) in enumerate(zip(tokens, targets)):
                cut = columns(first, i, dst.shape[-1])
                row.append(pltpu.make_async_copy(src.at[:, cut], dst.at[k], sems.at[k, j]))
                row[-1].start()
            rows.append(row)
        return rows

    if not own:
        smalls = [
            pltpu.make_async_copy(s, d, sem_small.at[k])
            for k, (s, d) in enumerate(zip((dt_hbm, bias_hbm, alog_hbm), small))
        ]
        for copy in smalls:
            copy.start()
    copies = loads(base, range(early, HALF), used, sem)
    fill_spread(e_ref)
    if not own:
        for copy in smalls:
            copy.wait()
        for k, v in enumerate(steps_of(*small)):
            aux_ref[k] = v
        stores.append(pltpu.make_async_copy(aux_ref, aux_hbm, sem_small.at[3]))
        stores[0].start()
    from_start = pair_up(to_half(aux_ref[2], base))
    to_end = pair_up(to_half(aux_ref[3], base))
    for i in range(HALF):
        if i >= early:
            for copy in copies[i - early]:
                copy.wait()
        if not own and i == 0:
            ahead = loads(base_of(True, sc_ref), range(KEPT), kept, sem_kept)
        at = i if i < early else i - early
        b_ref, x_ref, c_ref, z_ref, og_ref = [
            r.at[at] for r in (kept if i < early else used)
        ]
        here = slice(i * N, (i + 1) * N)
        te = of_group(to_end, i)
        fs = of_group(from_start, i)
        bt = b_ref[...].T
        ct = c_ref[...].T
        for k in range(W // CHUNK):
            cut = slice(k * CHUNK, (k + 1) * CHUNK)
            e = e_ref[:, cut]
            xs = x_ref[:, cut].astype(F32) * jnp.dot(te, e, preferred_element_type=F32)
            st_ref[here, cut] = jnp.dot(
                bt, xs.astype(BF16), preferred_element_type=F32
            ).astype(BF16)
            gate = silu(z_ref[:, cut].astype(F32))
            hg = (og_ref[:, cut].astype(F32) * gate).astype(BF16)
            gs = hg.astype(F32) * jnp.dot(fs, e, preferred_element_type=F32)
            st_ref[here, slice(W + k * CHUNK, W + (k + 1) * CHUNK)] = jnp.dot(
                ct, gs.astype(BF16), preferred_element_type=F32
            ).astype(BF16)
        decay = jnp.broadcast_to(fs[T - 16 : T].astype(F32)[15:16], (N, LANES))
        st_ref[here, 2 * W :] = decay.astype(BF16)
        if own:
            stores += part_copies(st_ref, part_hbm, here, sc_ref[0], sem_out.at[i])
            for store in stores[-2:]:
                store.start()
    if not own:
        for row in ahead:
            for copy in row:
                copy.wait()
    for store in stores:
        store.wait()


def part_copies(st_ref, part_hbm, here, which, sem):
    cut = pl.ds(pl.multiple_of(which * W, W), W)
    return [
        pltpu.make_async_copy(st_ref.at[here, cut], part_hbm.at[here, :W], sem.at[0]),
        pltpu.make_async_copy(st_ref.at[here, 2 * W :], part_hbm.at[here, W:], sem.at[1]),
    ]


STATE = jax.ShapeDtypeStruct((HALF * N, WIDE), BF16)
PART = pltpu.HBM((HALF * N, W + LANES), BF16)


def token_shapes(groups):
    return [(groups, T, width) for width in (N, W, N, W, W)]


def states_send(sc, dt, bias, alog, *tokens):
    aux = jax.ShapeDtypeStruct((4, T, NH), F32)
    return pl.pallas_call(
        functools.partial(states_kernel, False),
        in_specs=[SMEM_SPEC] + [HBM_SPEC] * 8,
        out_specs=[VMEM_SPEC, VMEM_SPEC, HBM_SPEC] + [VMEM_SPEC] * 5,
        out_shape=[STATE, aux, pltpu.HBM((4, T, NH), F32)]
        + [jax.ShapeDtypeStruct(s, BF16) for s in token_shapes(KEPT)],
        scratch_shapes=[SPREAD]
        + [pltpu.VMEM(s, BF16) for s in token_shapes(HALF)]
        + [pltpu.VMEM((T, NH), BF16), pltpu.VMEM((1, NH), F32), pltpu.VMEM((1, NH), F32)]
        + [pltpu.SemaphoreType.DMA((HALF, 5)), pltpu.SemaphoreType.DMA((4,))]
        + [pltpu.SemaphoreType.DMA((KEPT, 5))],
        compiler_params=params(24),
        name="states_send",
    )(sc, *[in_hbm(a) for a in (dt, bias, alog, *tokens)])


def states_keep(sc, aux, kept, tokens):
    return pl.pallas_call(
        functools.partial(states_kernel, True),
        in_specs=[SMEM_SPEC] + [VMEM_SPEC] * 6 + [HBM_SPEC] * 5,
        out_specs=[VMEM_SPEC, HBM_SPEC],
        out_shape=[STATE, PART],
        scratch_shapes=[SPREAD]
        + [pltpu.VMEM(s, BF16) for s in token_shapes(HALF - KEPT)]
        + [pltpu.SemaphoreType.DMA((HALF - KEPT, 5)), pltpu.SemaphoreType.DMA((HALF, 2))],
        compiler_params=params(12),
        name="states_keep",
    )(sc, aux, *kept, *[in_hbm(a) for a in tokens])


def decay_row(state_ref, at, e_ref):
    pairs = state_ref[at : at + 16, 2 * W :]
    return jnp.dot(pairs, e_ref[...], preferred_element_type=F32)[0:1]


def merge_kernel(sc_ref, own_ref, got_ref, out_hbm, part_hbm, e_ref, out_ref, sem, sem_out):
    core = sc_ref[0]
    parts = part_copies(got_ref, part_hbm, slice(0, HALF * N), 1 - core, sem)
    for part in parts:
        part.start()
    fill_spread(e_ref)

    def merge(r0, r1):
        stores = []
        for i in range(HALF):
            here = slice(i * N, (i + 1) * N)
            there = slice(i * N // 8, (i + 1) * N // 8)
            d0 = decay_row(r0, i * N, e_ref)
            d1 = decay_row(r1, i * N, e_ref)
            for k in range(W // CHUNK):
                cut = slice(k * CHUNK, (k + 1) * CHUNK)
                forward = d1[:, cut] * r0[here, cut].astype(F32) + r1[here, cut].astype(F32)
                out_ref[there, :, cut] = forward.reshape(N // 8, 8, CHUNK).astype(BF16)
                back = slice(W + k * CHUNK, W + (k + 1) * CHUNK)
                backward = r0[here, back].astype(F32) + d0[:, cut] * r1[here, back].astype(F32)
                out_ref[there, :, back] = backward.reshape(N // 8, 8, CHUNK).astype(BF16)
            p0 = r0[i * N : i * N + 16, 2 * W :].astype(F32)
            p1 = r1[i * N : i * N + 16, 2 * W :].astype(F32)
            p0 = p0 + pltpu.roll(p0, 64, 1)
            p1 = p1 + pltpu.roll(p1, 64, 1)
            both = pair_up(p0 * p1)[0:8]
            both = jnp.broadcast_to(both[None], (N // 8, 8, LANES))
            out_ref[there, :, 2 * W :] = both.astype(BF16)
            stores.append(pltpu.make_async_copy(out_ref.at[there], out_hbm.at[there], sem_out.at[i]))
            stores[-1].start()
        for store in stores:
            store.wait()

    @pl.when(core == 0)
    def _():
        merge(own_ref, got_ref)

    @pl.when(core != 0)
    def _():
        merge(got_ref, own_ref)

    for part in parts:
        part.wait()


def merge(sc, own, got):
    return pl.pallas_call(
        merge_kernel,
        in_specs=[SMEM_SPEC, VMEM_SPEC, VMEM_SPEC],
        out_specs=[HBM_SPEC, HBM_SPEC],
        out_shape=[pltpu.HBM((HALF * N // 8, 8, WIDE), BF16), PART],
        scratch_shapes=[
            SPREAD,
            pltpu.VMEM((HALF * N // 8, 8, WIDE), BF16),
            pltpu.SemaphoreType.DMA((2,)),
            pltpu.SemaphoreType.DMA((HALF,)),
        ],
        compiler_params=params(16),
        name="merge_cores",
    )(sc, own, got)


def scan_kernel(chips, in_ref, after_ref, out_hbm, e_ref, d_ref, out_ref, sem):
    fill_spread(e_ref)
    pairs = in_ref[:, :, 2 * W :].astype(F32).reshape(chips * 8, LANES).astype(BF16)
    d_ref[...] = jnp.dot(pairs, e_ref[...], preferred_element_type=F32).reshape(chips, 8, W)
    zero = jnp.zeros((8, W), F32)

    def forward(k, e):
        out_ref[k, :, :W] = e.astype(BF16)
        return d_ref[k] * e + in_ref[k, :, :W].astype(F32)

    def backward(k, l):
        j = chips - 1 - k
        out_ref[j, :, W:] = l.astype(BF16)
        return d_ref[j] * l + in_ref[j, :, W : 2 * W].astype(F32)

    parts = ((0, chips, slice(0, W)), (chips // 2, chips, slice(W, 2 * W)), (0, chips // 2, slice(W, 2 * W)))
    stores = [
        pltpu.make_async_copy(out_ref.at[a:b, :, cut], out_hbm.at[a:b, :, cut], sem.at[k])
        for k, (a, b, cut) in enumerate(parts)
    ]
    lax.fori_loop(0, chips, forward, zero, unroll=8)
    stores[0].start()
    l = lax.fori_loop(0, chips // 2, backward, zero, unroll=8)
    stores[1].start()
    lax.fori_loop(chips // 2, chips, backward, l, unroll=8)
    stores[2].start()
    for store in stores:
        store.wait()


def scan(parts, after):
    chips = parts.shape[0]
    return pl.pallas_call(
        functools.partial(scan_kernel, chips),
        in_specs=[VMEM_SPEC, HBM_SPEC],
        out_specs=HBM_SPEC,
        out_shape=pltpu.HBM((chips, 8, 2 * W), BF16),
        scratch_shapes=[
            SPREAD,
            pltpu.VMEM((chips, 8, W), F32),
            pltpu.VMEM((chips, 8, 2 * W), BF16),
            pltpu.SemaphoreType.DMA((3,)),
        ],
        compiler_params=params(16),
        name="scan_chips",
    )(parts, in_hbm(after))


def local_kernel(
    own, sc_ref, aux_ref, skip_ref, got_ref, b_hbm, x_hbm, c_hbm, z_hbm, og_hbm, *refs
):
    if own:
        results, refs = refs[:7], refs[7:]
        fetched = ()
    else:
        ready, results, fetched, refs = refs[:5], refs[5:12], refs[12:20], refs[20:]
    y_ref, dx_ref, xs_ref, gs_ref, pair_ref, db_ref, dc_ref = results
    (
    e_ref, x_ref, z_ref, og_ref, b_ref, c_ref, ysum_ref, dxsum_ref, dbsum_ref, dcsum_ref, hg_ref,
    runc_ref, run_ref, step_ref, plain_ref, sem, *more,
    ) = refs
    base = base_of(own, sc_ref)
    core = sc_ref[0]
    copies = []
    if not own:
        first = base_of(True, sc_ref)
        sources = [r.at[:, columns(first, 0, w)] for r, w in ((b_hbm, N), (c_hbm, N), (z_hbm, W))]
        sources += [r.at[0] for r in ready]
        for k, (src, dst) in enumerate(zip(sources, fetched)):
            copies.append(pltpu.make_async_copy(src, dst, more[0].at[k]))
            copies[-1].start()
    for i in range(HALF):
        for k, (src, dst, width) in enumerate(
            (
                (b_hbm, b_ref, N),
                (x_hbm, x_ref, W),
                (c_hbm, c_ref, N),
                (z_hbm, z_ref, W),
                (og_hbm, og_ref, W),
            )
        ):
            copies.append(
                pltpu.make_async_copy(src.at[:, columns(base, i, width)], dst.at[i], sem.at[i, k])
            )
            copies[-1].start()
    fill_spread(e_ref)
    start = to_half(aux_ref[2], base)
    end = to_half(aux_ref[3], base)
    gain = to_half(jnp.broadcast_to(skip_ref[...], (16, NH)), base)
    run = to_half(aux_ref[1], base)
    run_t = run.T
    step_t = to_half(aux_ref[0], base).T
    for i in range(HALF):
        decay = got_ref[i * N : i * N + 16, W:].astype(F32)
        decay = (decay + pltpu.roll(decay, 64, 1))[0:1]
        fs, te, skip, run_c = [pltpu.roll(v, LANES - PER * i, 1) if i else v for v in (start, end, gain, run)]
        plain_ref[i, 0:T] = pair_up(fs).astype(BF16)
        plain_ref[i, T : 2 * T] = pair_up(te).astype(BF16)
        plain_ref[i, 2 * T : 2 * T + 16] = pair_up(skip).astype(BF16)
        pair_ref[i, 0:T] = pair_up(jnp.where(core == 0, fs, fs * decay)).astype(BF16)
        pair_ref[i, T : 2 * T] = pair_up(jnp.where(core == 0, te * decay, te)).astype(BF16)
        runc_ref[i] = run_c
        run_ref[i] = run_t[i * PER : (i + 1) * PER]
        step_ref[i] = step_t[i * PER : (i + 1) * PER]
    for copy in copies:
        copy.wait()
    row = lax.broadcasted_iota(jnp.int32, (T, T), 0)
    col = lax.broadcasted_iota(jnp.int32, (T, T), 1)
    below = row >= col
    left = col < P_SIZE

    def one_group(i, unused):
        b, c = b_ref[i], c_ref[i]
        cb = lax.dot_general(c, b, NT, preferred_element_type=F32)
        run_cols, run_rows, step_rows = runc_ref[i], run_ref[i], step_ref[i]
        mass = jnp.zeros((T, T), F32)
        for pair in range(PER // 2):
            here = slice(pair * LANES, (pair + 1) * LANES)
            e = e_ref[:, here]
            both = jnp.dot(pair_ref[i], e, preferred_element_type=F32)
            skip = jnp.dot(plain_ref[i, 2 * T : 2 * T + 16], e, preferred_element_type=F32)[0:1]
            x = x_ref[i, :, here]
            g = (og_ref[i, :, here].astype(F32) * silu(z_ref[i, :, here].astype(F32))).astype(BF16)
            hg_ref[:, here] = g
            gs_ref[i, :, here] = (g.astype(F32) * both[0:T]).astype(BF16)
            xs_ref[i, :, here] = (x.astype(F32) * both[T : 2 * T]).astype(BF16)
            ys, dxs = [], []
            for k in range(2):
                j = 2 * pair + k
                gap = run_cols[:, j : j + 1] - run_rows[j : j + 1, :]
                weight = jnp.exp(jnp.where(below, gap, -1e30)) * step_rows[j : j + 1, :]
                mine = left if k == 0 else ~left
                inner = lax.dot_general(
                    jnp.where(mine, g, jnp.zeros_like(g)), x, NT, preferred_element_type=F32
                )
                mass = mass + weight * inner
                joint = (weight * cb).astype(BF16)
                ys.append(jnp.dot(joint, x, preferred_element_type=F32))
                dxs.append(jnp.dot(joint.T, g, preferred_element_type=F32))
            ysum_ref[:, here] = jnp.where(left, ys[0], ys[1]) + skip * x.astype(F32)
            dxsum_ref[:, here] = jnp.where(left, dxs[0], dxs[1]) + skip * g.astype(F32)
        high = mass.astype(BF16)
        low = (mass - high.astype(F32)).astype(BF16)
        dcsum_ref[...] = jnp.dot(high, b, preferred_element_type=F32) + jnp.dot(
            low, b, preferred_element_type=F32
        )
        dbsum_ref[...] = jnp.dot(high.T, c, preferred_element_type=F32) + jnp.dot(
            low.T, c, preferred_element_type=F32
        )
        rows = pl.ds(pl.multiple_of(i * N, N), N)

        @pl.when(core != 0)
        def _():
            partner = got_ref[rows, :W]
            fs = jnp.dot(plain_ref[i, 0:T], e_ref[...], preferred_element_type=F32)
            ysum_ref[...] += fs * jnp.dot(c, partner, preferred_element_type=F32)
            gs = (hg_ref[...].astype(F32) * fs).astype(BF16)
            dcsum_ref[...] += lax.dot_general(gs, partner, NT, preferred_element_type=F32)

        @pl.when(core == 0)
        def _():
            partner = got_ref[rows, :W]
            te = jnp.dot(plain_ref[i, T : 2 * T], e_ref[...], preferred_element_type=F32)
            dxsum_ref[...] += te * jnp.dot(b, partner, preferred_element_type=F32)
            xs = (x_ref[i].astype(F32) * te).astype(BF16)
            dbsum_ref[...] += lax.dot_general(xs, partner, NT, preferred_element_type=F32)

        y_ref[i] = ysum_ref[...].astype(BF16)
        dx_ref[i] = dxsum_ref[...].astype(BF16)
        db_ref[i] = dbsum_ref[...].astype(BF16)
        dc_ref[i] = dcsum_ref[...].astype(BF16)
        return unused

    lax.fori_loop(0, HALF, one_group, 0)


FETCHED = (
    [((T, N), BF16)] * 2 + [((T, W), BF16)] * 5 + [((2 * T, LANES), BF16)]
)


def local(own, sc, aux, skip, got, tokens, ready=()):
    wide = pltpu.HBM((HALF, T, W), BF16)
    thin = pltpu.HBM((HALF, T, N), BF16)
    args = [in_hbm(a) for a in (aux, skip, got, *tokens, *ready)]
    fetched = [] if own else [jax.ShapeDtypeStruct(*f) for f in FETCHED]
    return pl.pallas_call(
        functools.partial(local_kernel, own),
        in_specs=[SMEM_SPEC, VMEM_SPEC, VMEM_SPEC, VMEM_SPEC] + [HBM_SPEC] * (5 + len(ready)),
        out_specs=[VMEM_SPEC] * (7 + len(fetched)),
        out_shape=[wide] * 4 + [pltpu.HBM((HALF, 2 * T, LANES), BF16)] + [thin] * 2 + fetched,
        scratch_shapes=[SPREAD]
        + [pltpu.VMEM((HALF, T, W), BF16)] * 3
        + [pltpu.VMEM((HALF, T, N), BF16)] * 2
        + [pltpu.VMEM((T, W), F32)] * 2
        + [pltpu.VMEM((T, N), F32)] * 2
        + [pltpu.VMEM((T, W), BF16)]
        + [pltpu.VMEM((HALF, T, LANES), F32)]
        + [pltpu.VMEM((HALF, PER, T), F32)] * 2
        + [pltpu.VMEM((HALF, 2 * T + 16, LANES), BF16)]
        + [pltpu.SemaphoreType.DMA((HALF, 5))]
        + ([] if own else [pltpu.SemaphoreType.DMA((len(FETCHED),))]),
        compiler_params=params(24),
        name="local_own" if own else "local_other",
    )(sc, *args)


def final_kernel(own, sc_ref, el_ref, *refs):
    if own:
        b0, c0, z0, y0, dx0, xs0, gs0, pair0 = refs[:8]
        fetched = (b0, c0, pair0, y0, z0, dx0, xs0, gs0)
        refs = refs[8:]
        sources, others, refs = refs[:10], refs[10:20], refs[20:]
        out_hbm, dx_hbm, db_hbm, dc_hbm = refs[:4]
        kept, refs = refs[4:14], refs[14:]
        e_ref, targets, refs = refs[0], refs[1:11], refs[11:]
        out_ref, dx_ref, db_ref, dc_ref, sem_out, sem_in = refs
    else:
        targets, refs = refs[:10], refs[14:]
        out_hbm, dx_hbm, db_hbm, dc_hbm = refs[:4]
        e_ref, out_ref, dx_ref, db_ref, dc_ref, sem_out = refs[4:]
    base = base_of(own, sc_ref)

    def loads(first, srcs, dsts, sems, skip=()):
        rows = []
        for i in range(HALF):
            row = []
            for k, (src, dst) in enumerate(zip(srcs, dsts)):
                if i == 0 and k in skip:
                    continue
                if k in (0, 1, 4):
                    src = src.at[:, columns(first, i, W if k == 4 else N)]
                else:
                    src = src.at[i]
                row.append(pltpu.make_async_copy(src, dst.at[i], sems.at[i, k]))
                row[-1].start()
            rows.append(row)
        return rows

    copies = loads(base, sources, targets, sem_in.at[0], range(8)) if own else []
    ahead = loads(base_of(False, sc_ref), others, kept, sem_in.at[1]) if own else []
    fill_spread(e_ref)
    stores = []
    for i in range(HALF):
        if own:
            for load in copies[i] if i else ():
                load.wait()
        group = [r.at[i] for r in targets]
        if own and i == 0:
            group[:8] = fetched
        b_ref, c_ref, pair_ref, y_ref, z_ref, dxl_ref, xs_ref, gs_ref, dbl_ref, dcl_ref = group
        b, c = b_ref[...], c_ref[...]
        rows = slice(i * N, (i + 1) * N)
        for k in range(W // CHUNK):
            cut = slice(k * CHUNK, (k + 1) * CHUNK)
            far = slice(W + k * CHUNK, W + (k + 1) * CHUNK)
            scale = jnp.dot(pair_ref[...], e_ref[:, cut], preferred_element_type=F32)
            mixed = y_ref[:, cut].astype(F32) + scale[0:T] * jnp.dot(
                c, el_ref[rows, cut], preferred_element_type=F32
            )
            mixed = mixed.astype(BF16).astype(F32)
            out_ref[i, :, cut] = (mixed * silu(z_ref[:, cut].astype(F32))).astype(BF16)
            dx_ref[i, :, cut] = dxl_ref[:, cut].astype(F32) + scale[T : 2 * T] * jnp.dot(
                b, el_ref[rows, far], preferred_element_type=F32
            )
        for load in copies[0] if own and i == 0 else ():
            load.wait()
        db_ref[i] = dbl_ref[...].astype(F32) + lax.dot_general(
            xs_ref[...], el_ref[rows, W:], NT, preferred_element_type=F32
        )
        dc_ref[i] = dcl_ref[...].astype(F32) + lax.dot_general(
            gs_ref[...], el_ref[rows, :W], NT, preferred_element_type=F32
        )
        for k, (src, dst, width) in enumerate(
            ((out_ref, out_hbm, W), (dx_ref, dx_hbm, W), (db_ref, db_hbm, N), (dc_ref, dc_hbm, N))
        ):
            stores.append(
                pltpu.make_async_copy(src.at[i], dst.at[:, columns(base, i, width)], sem_out.at[i, k])
            )
            stores[-1].start()
    for row in ahead:
        for load in row:
            load.wait()
    for store in stores:
        store.wait()


LOADED = [
    ((HALF, T, N), BF16),
    ((HALF, T, N), BF16),
    ((HALF, 2 * T, LANES), BF16),
    ((HALF, T, W), BF16),
    ((HALF, T, W), BF16),
    ((HALF, T, W), BF16),
    ((HALF, T, W), BF16),
    ((HALF, T, W), BF16),
    ((HALF, T, N), BF16),
    ((HALF, T, N), BF16),
]
RESULTS = [
    ((T, NH * P_SIZE), BF16),
    ((T, NH * P_SIZE), F32),
    ((T, NG * N), F32),
    ((T, NG * N), F32),
]
STAGED = [
    pltpu.VMEM((HALF, T, W), BF16),
    pltpu.VMEM((HALF, T, W), F32),
    pltpu.VMEM((HALF, T, N), F32),
    pltpu.VMEM((HALF, T, N), F32),
    pltpu.SemaphoreType.DMA((HALF, 4)),
]


def in_order(local_parts, z, b, c):
    y, dx, xs, gs, pairs, db, dc = local_parts
    return [in_hbm(a) for a in (b, c, pairs, y, z, dx, xs, gs, db, dc)]


def final_own(sc, el, fetched, own_parts, other_parts):
    return pl.pallas_call(
        functools.partial(final_kernel, True),
        in_specs=[SMEM_SPEC, VMEM_SPEC] + [VMEM_SPEC] * 8 + [HBM_SPEC] * 20,
        out_specs=[HBM_SPEC] * 4 + [VMEM_SPEC] * 10,
        out_shape=[pltpu.HBM(*r) for r in RESULTS] + [jax.ShapeDtypeStruct(*r) for r in LOADED],
        scratch_shapes=[SPREAD]
        + [pltpu.VMEM(*r) for r in LOADED]
        + STAGED
        + [pltpu.SemaphoreType.DMA((2, HALF, 10))],
        compiler_params=params(24),
        name="final_own",
    )(sc, el, *fetched, *own_parts, *other_parts)


def final_other(sc, el, loaded, earlier):
    return pl.pallas_call(
        functools.partial(final_kernel, False),
        in_specs=[SMEM_SPEC, VMEM_SPEC] + [VMEM_SPEC] * 10 + [HBM_SPEC] * 4,
        out_specs=[HBM_SPEC] * 4,
        out_shape=[pltpu.HBM(*r) for r in RESULTS],
        input_output_aliases={12 + k: k for k in range(4)},
        scratch_shapes=[SPREAD] + STAGED,
        compiler_params=params(16),
        name="final_other",
    )(sc, el, *loaded, *earlier)


def body(ssm_input, gate_input, b_input, c_input, dt_raw, dt_bias, a_log, skip_gain, out_grad):
    ctx_count = lax.axis_size("ctx")
    head_count = lax.axis_size("head")
    sc = (lax.axis_index("head") % 2).astype(jnp.int32)[None]
    bias, alog, skip = dt_bias[None, :], a_log[None, :], skip_gain[None, :]
    swap = [(k, k ^ 1) for k in range(head_count)]
    chips = [[2 * k + c for k in range(ctx_count * head_count // 2)] for c in range(2)]

    def exchange(parts):
        return lax.all_to_all(
            parts, ("ctx", "head"), split_axis=0, concat_axis=0, tiled=True, axis_index_groups=chips
        )

    tokens = (b_input, ssm_input, c_input, gate_input, out_grad)
    send, aux, aux_hbm, *kept = states_send(sc, dt_raw, bias, alog, *tokens)
    got = lax.ppermute(send, "head", swap)
    keep, keep_part = states_keep(sc, aux, kept, tokens)
    payload, got_part = merge(sc, keep, got)
    gathered = exchange(payload)
    got_other = lax.ppermute(keep_part, "head", swap)
    loc_own = local(True, sc, aux_hbm, skip, got_part, tokens)
    back = exchange(scan(gathered, loc_own[6]))
    loc_other = local(False, sc, aux_hbm, skip, got_other, tokens, loc_own[:5])
    back, loc_other = lax.optimization_barrier((back, loc_other))
    el = back.reshape(HALF * N, 2 * W)
    el_other = lax.ppermute(el, "head", swap)
    shared = (gate_input, b_input, c_input)
    own_parts, other_parts = in_order(loc_own, *shared), in_order(loc_other[:7], *shared)
    outs = final_own(sc, el, loc_other[7:], own_parts, other_parts)
    return tuple(final_other(sc, el_other, outs[4:], outs[:4]))


def solution(mesh):
    row_spec = P(("ctx", "head"), None)
    in_specs = (row_spec,) * 5 + (P(), P(), P(), row_spec)
    return jax.shard_map(
        body, mesh=mesh, in_specs=in_specs, out_specs=(row_spec,) * 4, check_vma=False
    )
```

```python
import functools

import jax
import jax.numpy as jnp
from jax import lax
from jax.experimental import pallas as pl
from jax.experimental.pallas import tpu as pltpu
from jax.sharding import PartitionSpec as P

NH = 128
P_SIZE = 64
N = 128
NG = 8
PER = NH // NG
W = PER * P_SIZE
T = 128
HALF = NG // 2
LANES = 128
WIDE = 2 * W + LANES
F32 = jnp.float32
BF16 = jnp.bfloat16


MIB = 1024 * 1024
NT = (((1,), (1,)), ((), ()))
CHUNK = 256
HBM_SPEC = pl.BlockSpec(memory_space=pl.ANY)
VMEM_SPEC = pl.BlockSpec(memory_space=pltpu.VMEM)
SMEM_SPEC = pl.BlockSpec(memory_space=pltpu.SMEM)
KEPT = 3
SPREAD = pltpu.VMEM((LANES, W), BF16)


def in_hbm(values):
    return pltpu.with_memory_space_constraint(values, pltpu.HBM)


def params(mib):
    return pltpu.CompilerParams(vmem_limit_bytes=mib * MIB)


def lane(shape):
    return lax.broadcasted_iota(jnp.int32, shape, len(shape) - 1)


def fill_spread(e_ref):
    row = lax.broadcasted_iota(jnp.int32, (LANES, W), 0)
    col = lax.broadcasted_iota(jnp.int32, (LANES, W), 1)
    e_ref[...] = jnp.where((row & 63) == (col >> 6), 1.0, 0.0).astype(BF16)


def to_half(values, base):
    return pltpu.roll(values, lax.rem(LANES - PER * base, LANES), 1)


def pair_up(values):
    high = values.astype(BF16).astype(F32)
    low = values - high
    return jnp.where(lane(values.shape) < 64, high, pltpu.roll(low, 64, 1))


def of_group(pairs, i):
    if i:
        pairs = pltpu.roll(pairs, LANES - PER * i, 1)
    return pairs.astype(BF16)


def silu(v):
    return v * (0.5 * jnp.tanh(0.5 * v) + 0.5)


def steps_of(dt_ref, bias_ref, alog_ref):
    u = jnp.exp(dt_ref[...].astype(F32) + bias_ref[...])
    one = 1.0 + u
    step = jnp.where(one == 1.0, u, jnp.log(one) * (u / jnp.where(one == 1.0, 1.0, one - 1.0)))
    rate = -step * jnp.exp(alog_ref[...])
    row = lax.broadcasted_iota(jnp.int32, (T, T), 0)
    col = lax.broadcasted_iota(jnp.int32, (T, T), 1)
    tri = jnp.where(row >= col, 1.0, 0.0).astype(BF16)
    running = jnp.zeros((T, NH), F32)
    for _ in range(3):
        piece = rate.astype(BF16)
        running = running + jnp.dot(tri, piece, preferred_element_type=F32)
        rate = rate - piece.astype(F32)
    from_start = jnp.exp(running)
    to_end = jnp.exp(running[T - 1 : T] - running) * step
    return step, running, from_start, to_end


def base_of(own, sc_ref):
    return HALF * sc_ref[0] if own else HALF * (1 - sc_ref[0])


def columns(base, i, width):
    return pl.ds(pl.multiple_of((base + i) * width, width), width)


def states_kernel(own, sc_ref, *refs):
    if own:
        aux_ref, kept, tokens, refs = refs[0], refs[1:6], refs[6:11], refs[11:]
        st_ref, part_hbm, e_ref, used, (sem, sem_out) = refs[0], refs[1], refs[2], refs[3:8], refs[8:]
        early = KEPT
    else:
        dt_hbm, bias_hbm, alog_hbm = refs[:3]
        tokens = refs[3:8]
        st_ref, aux_ref, aux_hbm = refs[8:11]
        kept = refs[11:16]
        e_ref = refs[16]
        used = refs[17:22]
        small = refs[22:25]
        sem, sem_small, sem_kept = refs[25:]
        early = 0
    base = base_of(own, sc_ref)
    stores = []

    def loads(first, groups, targets, sems):
        rows = []
        for k, i in enumerate(groups):
            row = []
            for j, (src, dst) in enumerate(zip(tokens, targets)):
                cut = columns(first, i, dst.shape[-1])
                row.append(pltpu.make_async_copy(src.at[:, cut], dst.at[k], sems.at[k, j]))
                row[-1].start()
            rows.append(row)
        return rows

    if not own:
        smalls = [
            pltpu.make_async_copy(s, d, sem_small.at[k])
            for k, (s, d) in enumerate(zip((dt_hbm, bias_hbm, alog_hbm), small))
        ]
        for copy in smalls:
            copy.start()
    copies = loads(base, range(early, HALF), used, sem)
    fill_spread(e_ref)
    if not own:
        for copy in smalls:
            copy.wait()
        for k, v in enumerate(steps_of(*small)):
            aux_ref[k] = v
        stores.append(pltpu.make_async_copy(aux_ref, aux_hbm, sem_small.at[3]))
        stores[0].start()
    from_start = pair_up(to_half(aux_ref[2], base))
    to_end = pair_up(to_half(aux_ref[3], base))
    for i in range(HALF):
        if i >= early:
            for copy in copies[i - early]:
                copy.wait()
        if not own and i == 0:
            ahead = loads(base_of(True, sc_ref), range(KEPT), kept, sem_kept)
        at = i if i < early else i - early
        b_ref, x_ref, c_ref, z_ref, og_ref = [
            r.at[at] for r in (kept if i < early else used)
        ]
        here = slice(i * N, (i + 1) * N)
        te = of_group(to_end, i)
        fs = of_group(from_start, i)
        bt = b_ref[...].T
        ct = c_ref[...].T
        for k in range(W // CHUNK):
            cut = slice(k * CHUNK, (k + 1) * CHUNK)
            e = e_ref[:, cut]
            xs = x_ref[:, cut].astype(F32) * jnp.dot(te, e, preferred_element_type=F32)
            st_ref[here, cut] = jnp.dot(
                bt, xs.astype(BF16), preferred_element_type=F32
            ).astype(BF16)
            gate = silu(z_ref[:, cut].astype(F32))
            hg = (og_ref[:, cut].astype(F32) * gate).astype(BF16)
            gs = hg.astype(F32) * jnp.dot(fs, e, preferred_element_type=F32)
            st_ref[here, slice(W + k * CHUNK, W + (k + 1) * CHUNK)] = jnp.dot(
                ct, gs.astype(BF16), preferred_element_type=F32
            ).astype(BF16)
        decay = jnp.broadcast_to(fs[T - 16 : T].astype(F32)[15:16], (N, LANES))
        st_ref[here, 2 * W :] = decay.astype(BF16)
        if own:
            stores += part_copies(st_ref, part_hbm, here, sc_ref[0], sem_out.at[i])
            for store in stores[-2:]:
                store.start()
    if not own:
        for row in ahead:
            for copy in row:
                copy.wait()
    for store in stores:
        store.wait()


def part_copies(st_ref, part_hbm, here, which, sem):
    cut = pl.ds(pl.multiple_of(which * W, W), W)
    return [
        pltpu.make_async_copy(st_ref.at[here, cut], part_hbm.at[here, :W], sem.at[0]),
        pltpu.make_async_copy(st_ref.at[here, 2 * W :], part_hbm.at[here, W:], sem.at[1]),
    ]


STATE = jax.ShapeDtypeStruct((HALF * N, WIDE), BF16)
PART = pltpu.HBM((HALF * N, W + LANES), BF16)


def token_shapes(groups):
    return [(groups, T, width) for width in (N, W, N, W, W)]


def states_send(sc, dt, bias, alog, *tokens):
    aux = jax.ShapeDtypeStruct((4, T, NH), F32)
    return pl.pallas_call(
        functools.partial(states_kernel, False),
        in_specs=[SMEM_SPEC] + [HBM_SPEC] * 8,
        out_specs=[VMEM_SPEC, VMEM_SPEC, HBM_SPEC] + [VMEM_SPEC] * 5,
        out_shape=[STATE, aux, pltpu.HBM((4, T, NH), F32)]
        + [jax.ShapeDtypeStruct(s, BF16) for s in token_shapes(KEPT)],
        scratch_shapes=[SPREAD]
        + [pltpu.VMEM(s, BF16) for s in token_shapes(HALF)]
        + [pltpu.VMEM((T, NH), BF16), pltpu.VMEM((1, NH), F32), pltpu.VMEM((1, NH), F32)]
        + [pltpu.SemaphoreType.DMA((HALF, 5)), pltpu.SemaphoreType.DMA((4,))]
        + [pltpu.SemaphoreType.DMA((KEPT, 5))],
        compiler_params=params(24),
        name="states_send",
    )(sc, *[in_hbm(a) for a in (dt, bias, alog, *tokens)])


def states_keep(sc, aux, kept, tokens):
    return pl.pallas_call(
        functools.partial(states_kernel, True),
        in_specs=[SMEM_SPEC] + [VMEM_SPEC] * 6 + [HBM_SPEC] * 5,
        out_specs=[VMEM_SPEC, HBM_SPEC],
        out_shape=[STATE, PART],
        scratch_shapes=[SPREAD]
        + [pltpu.VMEM(s, BF16) for s in token_shapes(HALF - KEPT)]
        + [pltpu.SemaphoreType.DMA((HALF - KEPT, 5)), pltpu.SemaphoreType.DMA((HALF, 2))],
        compiler_params=params(12),
        name="states_keep",
    )(sc, aux, *kept, *[in_hbm(a) for a in tokens])


def decay_row(state_ref, at, e_ref):
    pairs = state_ref[at : at + 16, 2 * W :]
    return jnp.dot(pairs, e_ref[...], preferred_element_type=F32)[0:1]


def merge_kernel(sc_ref, own_ref, got_ref, out_hbm, part_hbm, e_ref, out_ref, sem, sem_out):
    core = sc_ref[0]
    parts = part_copies(got_ref, part_hbm, slice(0, HALF * N), 1 - core, sem)
    for part in parts:
        part.start()
    fill_spread(e_ref)

    def merge(r0, r1):
        stores = []
        for i in range(HALF):
            here = slice(i * N, (i + 1) * N)
            there = slice(i * N // 8, (i + 1) * N // 8)
            d0 = decay_row(r0, i * N, e_ref)
            d1 = decay_row(r1, i * N, e_ref)
            for k in range(W // CHUNK):
                cut = slice(k * CHUNK, (k + 1) * CHUNK)
                forward = d1[:, cut] * r0[here, cut].astype(F32) + r1[here, cut].astype(F32)
                out_ref[there, :, cut] = forward.reshape(N // 8, 8, CHUNK).astype(BF16)
                back = slice(W + k * CHUNK, W + (k + 1) * CHUNK)
                backward = r0[here, back].astype(F32) + d0[:, cut] * r1[here, back].astype(F32)
                out_ref[there, :, back] = backward.reshape(N // 8, 8, CHUNK).astype(BF16)
            p0 = r0[i * N : i * N + 16, 2 * W :].astype(F32)
            p1 = r1[i * N : i * N + 16, 2 * W :].astype(F32)
            p0 = p0 + pltpu.roll(p0, 64, 1)
            p1 = p1 + pltpu.roll(p1, 64, 1)
            both = pair_up(p0 * p1)[0:8]
            both = jnp.broadcast_to(both[None], (N // 8, 8, LANES))
            out_ref[there, :, 2 * W :] = both.astype(BF16)
            stores.append(pltpu.make_async_copy(out_ref.at[there], out_hbm.at[there], sem_out.at[i]))
            stores[-1].start()
        for store in stores:
            store.wait()

    @pl.when(core == 0)
    def _():
        merge(own_ref, got_ref)

    @pl.when(core != 0)
    def _():
        merge(got_ref, own_ref)

    for part in parts:
        part.wait()


def merge(sc, own, got):
    return pl.pallas_call(
        merge_kernel,
        in_specs=[SMEM_SPEC, VMEM_SPEC, VMEM_SPEC],
        out_specs=[HBM_SPEC, HBM_SPEC],
        out_shape=[pltpu.HBM((HALF * N // 8, 8, WIDE), BF16), PART],
        scratch_shapes=[
            SPREAD,
            pltpu.VMEM((HALF * N // 8, 8, WIDE), BF16),
            pltpu.SemaphoreType.DMA((2,)),
            pltpu.SemaphoreType.DMA((HALF,)),
        ],
        compiler_params=params(16),
        name="merge_cores",
    )(sc, own, got)


def scan_kernel(chips, in_ref, after_ref, out_hbm, e_ref, d_ref, out_ref, sem):
    fill_spread(e_ref)
    pairs = in_ref[:, :, 2 * W :].astype(F32).reshape(chips * 8, LANES).astype(BF16)
    d_ref[...] = jnp.dot(pairs, e_ref[...], preferred_element_type=F32).reshape(chips, 8, W)
    zero = jnp.zeros((8, W), F32)

    def forward(k, e):
        out_ref[k, :, :W] = e.astype(BF16)
        return d_ref[k] * e + in_ref[k, :, :W].astype(F32)

    def backward(k, l):
        j = chips - 1 - k
        out_ref[j, :, W:] = l.astype(BF16)
        return d_ref[j] * l + in_ref[j, :, W : 2 * W].astype(F32)

    parts = ((0, chips, slice(0, W)), (chips // 2, chips, slice(W, 2 * W)), (0, chips // 2, slice(W, 2 * W)))
    stores = [
        pltpu.make_async_copy(out_ref.at[a:b, :, cut], out_hbm.at[a:b, :, cut], sem.at[k])
        for k, (a, b, cut) in enumerate(parts)
    ]
    lax.fori_loop(0, chips, forward, zero, unroll=8)
    stores[0].start()
    l = lax.fori_loop(0, chips // 2, backward, zero, unroll=8)
    stores[1].start()
    lax.fori_loop(chips // 2, chips, backward, l, unroll=8)
    stores[2].start()
    for store in stores:
        store.wait()


def scan(parts, after):
    chips = parts.shape[0]
    return pl.pallas_call(
        functools.partial(scan_kernel, chips),
        in_specs=[VMEM_SPEC, HBM_SPEC],
        out_specs=HBM_SPEC,
        out_shape=pltpu.HBM((chips, 8, 2 * W), BF16),
        scratch_shapes=[
            SPREAD,
            pltpu.VMEM((chips, 8, W), F32),
            pltpu.VMEM((chips, 8, 2 * W), BF16),
            pltpu.SemaphoreType.DMA((3,)),
        ],
        compiler_params=params(16),
        name="scan_chips",
    )(parts, in_hbm(after))


def local_kernel(
    own, sc_ref, aux_ref, skip_ref, got_ref, b_hbm, x_hbm, c_hbm, z_hbm, og_hbm, *refs
):
    if own:
        results, refs = refs[:7], refs[7:]
        fetched = ()
    else:
        ready, results, fetched, refs = refs[:5], refs[5:12], refs[12:20], refs[20:]
    y_ref, dx_ref, xs_ref, gs_ref, pair_ref, db_ref, dc_ref = results
    (
    e_ref, x_ref, z_ref, og_ref, b_ref, c_ref, ysum_ref, dxsum_ref, dbsum_ref, dcsum_ref, hg_ref,
    runc_ref, run_ref, step_ref, plain_ref, sem, *more,
    ) = refs
    base = base_of(own, sc_ref)
    core = sc_ref[0]
    copies = []
    if not own:
        first = base_of(True, sc_ref)
        sources = [r.at[:, columns(first, 0, w)] for r, w in ((b_hbm, N), (c_hbm, N), (z_hbm, W))]
        sources += [r.at[0] for r in ready]
        for k, (src, dst) in enumerate(zip(sources, fetched)):
            copies.append(pltpu.make_async_copy(src, dst, more[0].at[k]))
            copies[-1].start()
    for i in range(HALF):
        for k, (src, dst, width) in enumerate(
            (
                (b_hbm, b_ref, N),
                (x_hbm, x_ref, W),
                (c_hbm, c_ref, N),
                (z_hbm, z_ref, W),
                (og_hbm, og_ref, W),
            )
        ):
            copies.append(
                pltpu.make_async_copy(src.at[:, columns(base, i, width)], dst.at[i], sem.at[i, k])
            )
            copies[-1].start()
    fill_spread(e_ref)
    start = to_half(aux_ref[2], base)
    end = to_half(aux_ref[3], base)
    gain = to_half(jnp.broadcast_to(skip_ref[...], (16, NH)), base)
    run = to_half(aux_ref[1], base)
    run_t = run.T
    step_t = to_half(aux_ref[0], base).T
    for i in range(HALF):
        decay = got_ref[i * N : i * N + 16, W:].astype(F32)
        decay = (decay + pltpu.roll(decay, 64, 1))[0:1]
        fs, te, skip, run_c = [pltpu.roll(v, LANES - PER * i, 1) if i else v for v in (start, end, gain, run)]
        plain_ref[i, 0:T] = pair_up(fs).astype(BF16)
        plain_ref[i, T : 2 * T] = pair_up(te).astype(BF16)
        plain_ref[i, 2 * T : 2 * T + 16] = pair_up(skip).astype(BF16)
        pair_ref[i, 0:T] = pair_up(jnp.where(core == 0, fs, fs * decay)).astype(BF16)
        pair_ref[i, T : 2 * T] = pair_up(jnp.where(core == 0, te * decay, te)).astype(BF16)
        runc_ref[i] = run_c
        run_ref[i] = run_t[i * PER : (i + 1) * PER]
        step_ref[i] = step_t[i * PER : (i + 1) * PER]
    for copy in copies:
        copy.wait()
    row = lax.broadcasted_iota(jnp.int32, (T, T), 0)
    col = lax.broadcasted_iota(jnp.int32, (T, T), 1)
    below = row >= col
    left = col < P_SIZE

    def one_group(i, unused):
        b, c = b_ref[i], c_ref[i]
        cb = lax.dot_general(c, b, NT, preferred_element_type=F32)
        run_cols, run_rows, step_rows = runc_ref[i], run_ref[i], step_ref[i]
        mass = jnp.zeros((T, T), F32)
        for pair in range(PER // 2):
            here = slice(pair * LANES, (pair + 1) * LANES)
            e = e_ref[:, here]
            both = jnp.dot(pair_ref[i], e, preferred_element_type=F32)
            skip = jnp.dot(plain_ref[i, 2 * T : 2 * T + 16], e, preferred_element_type=F32)[0:1]
            x = x_ref[i, :, here]
            g = (og_ref[i, :, here].astype(F32) * silu(z_ref[i, :, here].astype(F32))).astype(BF16)
            hg_ref[:, here] = g
            gs_ref[i, :, here] = (g.astype(F32) * both[0:T]).astype(BF16)
            xs_ref[i, :, here] = (x.astype(F32) * both[T : 2 * T]).astype(BF16)
            ys, dxs = [], []
            for k in range(2):
                j = 2 * pair + k
                gap = run_cols[:, j : j + 1] - run_rows[j : j + 1, :]
                weight = jnp.exp(jnp.where(below, gap, -1e30)) * step_rows[j : j + 1, :]
                mine = left if k == 0 else ~left
                inner = lax.dot_general(
                    jnp.where(mine, g, jnp.zeros_like(g)), x, NT, preferred_element_type=F32
                )
                mass = mass + weight * inner
                joint = (weight * cb).astype(BF16)
                ys.append(jnp.dot(joint, x, preferred_element_type=F32))
                dxs.append(jnp.dot(joint.T, g, preferred_element_type=F32))
            ysum_ref[:, here] = jnp.where(left, ys[0], ys[1]) + skip * x.astype(F32)
            dxsum_ref[:, here] = jnp.where(left, dxs[0], dxs[1]) + skip * g.astype(F32)
        high = mass.astype(BF16)
        low = (mass - high.astype(F32)).astype(BF16)
        dcsum_ref[...] = jnp.dot(high, b, preferred_element_type=F32) + jnp.dot(
            low, b, preferred_element_type=F32
        )
        dbsum_ref[...] = jnp.dot(high.T, c, preferred_element_type=F32) + jnp.dot(
            low.T, c, preferred_element_type=F32
        )
        rows = pl.ds(pl.multiple_of(i * N, N), N)

        @pl.when(core != 0)
        def _():
            partner = got_ref[rows, :W]
            fs = jnp.dot(plain_ref[i, 0:T], e_ref[...], preferred_element_type=F32)
            ysum_ref[...] += fs * jnp.dot(c, partner, preferred_element_type=F32)
            gs = (hg_ref[...].astype(F32) * fs).astype(BF16)
            dcsum_ref[...] += lax.dot_general(gs, partner, NT, preferred_element_type=F32)

        @pl.when(core == 0)
        def _():
            partner = got_ref[rows, :W]
            te = jnp.dot(plain_ref[i, T : 2 * T], e_ref[...], preferred_element_type=F32)
            dxsum_ref[...] += te * jnp.dot(b, partner, preferred_element_type=F32)
            xs = (x_ref[i].astype(F32) * te).astype(BF16)
            dbsum_ref[...] += lax.dot_general(xs, partner, NT, preferred_element_type=F32)

        y_ref[i] = ysum_ref[...].astype(BF16)
        dx_ref[i] = dxsum_ref[...].astype(BF16)
        db_ref[i] = dbsum_ref[...].astype(BF16)
        dc_ref[i] = dcsum_ref[...].astype(BF16)
        return unused

    lax.fori_loop(0, HALF, one_group, 0)


FETCHED = (
    [((T, N), BF16)] * 2 + [((T, W), BF16)] * 5 + [((2 * T, LANES), BF16)]
)


def local(own, sc, aux, skip, got, tokens, ready=()):
    wide = pltpu.HBM((HALF, T, W), BF16)
    thin = pltpu.HBM((HALF, T, N), BF16)
    args = [in_hbm(a) for a in (aux, skip, got, *tokens, *ready)]
    fetched = [] if own else [jax.ShapeDtypeStruct(*f) for f in FETCHED]
    return pl.pallas_call(
        functools.partial(local_kernel, own),
        in_specs=[SMEM_SPEC, VMEM_SPEC, VMEM_SPEC, VMEM_SPEC] + [HBM_SPEC] * (5 + len(ready)),
        out_specs=[VMEM_SPEC] * (7 + len(fetched)),
        out_shape=[wide] * 4 + [pltpu.HBM((HALF, 2 * T, LANES), BF16)] + [thin] * 2 + fetched,
        scratch_shapes=[SPREAD]
        + [pltpu.VMEM((HALF, T, W), BF16)] * 3
        + [pltpu.VMEM((HALF, T, N), BF16)] * 2
        + [pltpu.VMEM((T, W), F32)] * 2
        + [pltpu.VMEM((T, N), F32)] * 2
        + [pltpu.VMEM((T, W), BF16)]
        + [pltpu.VMEM((HALF, T, LANES), F32)]
        + [pltpu.VMEM((HALF, PER, T), F32)] * 2
        + [pltpu.VMEM((HALF, 2 * T + 16, LANES), BF16)]
        + [pltpu.SemaphoreType.DMA((HALF, 5))]
        + ([] if own else [pltpu.SemaphoreType.DMA((len(FETCHED),))]),
        compiler_params=params(24),
        name="local_own" if own else "local_other",
    )(sc, *args)


def final_kernel(own, sc_ref, el_ref, *refs):
    if own:
        b0, c0, z0, y0, dx0, xs0, gs0, pair0 = refs[:8]
        fetched = (b0, c0, pair0, y0, z0, dx0, xs0, gs0)
        refs = refs[8:]
        sources, others, refs = refs[:10], refs[10:20], refs[20:]
        out_hbm, dx_hbm, db_hbm, dc_hbm = refs[:4]
        kept, refs = refs[4:14], refs[14:]
        e_ref, targets, refs = refs[0], refs[1:11], refs[11:]
        out_ref, dx_ref, db_ref, dc_ref, sem_out, sem_in = refs
    else:
        targets, refs = refs[:10], refs[14:]
        out_hbm, dx_hbm, db_hbm, dc_hbm = refs[:4]
        e_ref, out_ref, dx_ref, db_ref, dc_ref, sem_out = refs[4:]
    base = base_of(own, sc_ref)

    def loads(first, srcs, dsts, sems, skip=()):
        rows = []
        for i in range(HALF):
            row = []
            for k, (src, dst) in enumerate(zip(srcs, dsts)):
                if i == 0 and k in skip:
                    continue
                if k in (0, 1, 4):
                    src = src.at[:, columns(first, i, W if k == 4 else N)]
                else:
                    src = src.at[i]
                row.append(pltpu.make_async_copy(src, dst.at[i], sems.at[i, k]))
                row[-1].start()
            rows.append(row)
        return rows

    copies = loads(base, sources, targets, sem_in.at[0], range(8)) if own else []
    ahead = loads(base_of(False, sc_ref), others, kept, sem_in.at[1]) if own else []
    fill_spread(e_ref)
    stores = []

    def put(k, src, dst, width):
        stores.append(
            pltpu.make_async_copy(src.at[i], dst.at[:, columns(base, i, width)], sem_out.at[i, k])
        )
        stores[-1].start()

    for i in range(HALF):
        if own:
            for load in copies[i] if i else ():
                load.wait()
        group = [r.at[i] for r in targets]
        if own and i == 0:
            group[:8] = fetched
        b_ref, c_ref, pair_ref, y_ref, z_ref, dxl_ref, xs_ref, gs_ref, dbl_ref, dcl_ref = group
        b, c = b_ref[...], c_ref[...]
        rows = slice(i * N, (i + 1) * N)
        for k in range(W // CHUNK):
            cut = slice(k * CHUNK, (k + 1) * CHUNK)
            far = slice(W + k * CHUNK, W + (k + 1) * CHUNK)
            scale = jnp.dot(pair_ref[...], e_ref[:, cut], preferred_element_type=F32)
            mixed = y_ref[:, cut].astype(F32) + scale[0:T] * jnp.dot(
                c, el_ref[rows, cut], preferred_element_type=F32
            )
            mixed = mixed.astype(BF16).astype(F32)
            out_ref[i, :, cut] = (mixed * silu(z_ref[:, cut].astype(F32))).astype(BF16)
            dx_ref[i, :, cut] = dxl_ref[:, cut].astype(F32) + scale[T : 2 * T] * jnp.dot(
                b, el_ref[rows, far], preferred_element_type=F32
            )
        put(0, out_ref, out_hbm, W)
        put(1, dx_ref, dx_hbm, W)
        for load in copies[0] if own and i == 0 else ():
            load.wait()
        db_ref[i] = dbl_ref[...].astype(F32) + lax.dot_general(
            xs_ref[...], el_ref[rows, W:], NT, preferred_element_type=F32
        )
        dc_ref[i] = dcl_ref[...].astype(F32) + lax.dot_general(
            gs_ref[...], el_ref[rows, :W], NT, preferred_element_type=F32
        )
        put(2, db_ref, db_hbm, N)
        put(3, dc_ref, dc_hbm, N)
    for row in ahead:
        for load in row:
            load.wait()
    for store in stores:
        store.wait()


LOADED = [
    ((HALF, T, N), BF16),
    ((HALF, T, N), BF16),
    ((HALF, 2 * T, LANES), BF16),
    ((HALF, T, W), BF16),
    ((HALF, T, W), BF16),
    ((HALF, T, W), BF16),
    ((HALF, T, W), BF16),
    ((HALF, T, W), BF16),
    ((HALF, T, N), BF16),
    ((HALF, T, N), BF16),
]
RESULTS = [
    ((T, NH * P_SIZE), BF16),
    ((T, NH * P_SIZE), F32),
    ((T, NG * N), F32),
    ((T, NG * N), F32),
]
STAGED = [
    pltpu.VMEM((HALF, T, W), BF16),
    pltpu.VMEM((HALF, T, W), F32),
    pltpu.VMEM((HALF, T, N), F32),
    pltpu.VMEM((HALF, T, N), F32),
    pltpu.SemaphoreType.DMA((HALF, 4)),
]


def in_order(local_parts, z, b, c):
    y, dx, xs, gs, pairs, db, dc = local_parts
    return [in_hbm(a) for a in (b, c, pairs, y, z, dx, xs, gs, db, dc)]


def final_own(sc, el, fetched, own_parts, other_parts):
    return pl.pallas_call(
        functools.partial(final_kernel, True),
        in_specs=[SMEM_SPEC, VMEM_SPEC] + [VMEM_SPEC] * 8 + [HBM_SPEC] * 20,
        out_specs=[HBM_SPEC] * 4 + [VMEM_SPEC] * 10,
        out_shape=[pltpu.HBM(*r) for r in RESULTS] + [jax.ShapeDtypeStruct(*r) for r in LOADED],
        scratch_shapes=[SPREAD]
        + [pltpu.VMEM(*r) for r in LOADED]
        + STAGED
        + [pltpu.SemaphoreType.DMA((2, HALF, 10))],
        compiler_params=params(24),
        name="final_own",
    )(sc, el, *fetched, *own_parts, *other_parts)


def final_other(sc, el, loaded, earlier):
    return pl.pallas_call(
        functools.partial(final_kernel, False),
        in_specs=[SMEM_SPEC, VMEM_SPEC] + [VMEM_SPEC] * 10 + [HBM_SPEC] * 4,
        out_specs=[HBM_SPEC] * 4,
        out_shape=[pltpu.HBM(*r) for r in RESULTS],
        input_output_aliases={12 + k: k for k in range(4)},
        scratch_shapes=[SPREAD] + STAGED,
        compiler_params=params(16),
        name="final_other",
    )(sc, el, *loaded, *earlier)


def body(ssm_input, gate_input, b_input, c_input, dt_raw, dt_bias, a_log, skip_gain, out_grad):
    ctx_count = lax.axis_size("ctx")
    head_count = lax.axis_size("head")
    sc = (lax.axis_index("head") % 2).astype(jnp.int32)[None]
    bias, alog, skip = dt_bias[None, :], a_log[None, :], skip_gain[None, :]
    swap = [(k, k ^ 1) for k in range(head_count)]
    chips = [[2 * k + c for k in range(ctx_count * head_count // 2)] for c in range(2)]

    def exchange(parts):
        return lax.all_to_all(
            parts, ("ctx", "head"), split_axis=0, concat_axis=0, tiled=True, axis_index_groups=chips
        )

    tokens = (b_input, ssm_input, c_input, gate_input, out_grad)
    send, aux, aux_hbm, *kept = states_send(sc, dt_raw, bias, alog, *tokens)
    got = lax.ppermute(send, "head", swap)
    keep, keep_part = states_keep(sc, aux, kept, tokens)
    payload, got_part = merge(sc, keep, got)
    gathered = exchange(payload)
    got_other = lax.ppermute(keep_part, "head", swap)
    loc_own = local(True, sc, aux_hbm, skip, got_part, tokens)
    back = exchange(scan(gathered, loc_own[6]))
    loc_other = local(False, sc, aux_hbm, skip, got_other, tokens, loc_own[:5])
    back, loc_other = lax.optimization_barrier((back, loc_other))
    el = back.reshape(HALF * N, 2 * W)
    el_other = lax.ppermute(el, "head", swap)
    shared = (gate_input, b_input, c_input)
    own_parts, other_parts = in_order(loc_own, *shared), in_order(loc_other[:7], *shared)
    outs = final_own(sc, el, loc_other[7:], own_parts, other_parts)
    return tuple(final_other(sc, el_other, outs[4:], outs[:4]))


def solution(mesh):
    row_spec = P(("ctx", "head"), None)
    in_specs = (row_spec,) * 5 + (P(), P(), P(), row_spec)
    return jax.shard_map(
        body, mesh=mesh, in_specs=in_specs, out_specs=(row_spec,) * 4, check_vma=False
    )
```

```python
import functools

import jax
import jax.numpy as jnp
from jax import lax
from jax.experimental import pallas as pl
from jax.experimental.pallas import tpu as pltpu
from jax.sharding import PartitionSpec as P

NH = 128
P_SIZE = 64
N = 128
NG = 8
PER = NH // NG
W = PER * P_SIZE
T = 128
HALF = NG // 2
LANES = 128
WIDE = 2 * W + LANES
F32 = jnp.float32
BF16 = jnp.bfloat16


MIB = 1024 * 1024
NT = (((1,), (1,)), ((), ()))
CHUNK = 256
HBM_SPEC = pl.BlockSpec(memory_space=pl.ANY)
VMEM_SPEC = pl.BlockSpec(memory_space=pltpu.VMEM)
SMEM_SPEC = pl.BlockSpec(memory_space=pltpu.SMEM)
KEPT = 3
SPREAD = pltpu.VMEM((LANES, W), BF16)


def in_hbm(values):
    return pltpu.with_memory_space_constraint(values, pltpu.HBM)


def params(mib):
    return pltpu.CompilerParams(vmem_limit_bytes=mib * MIB)


def lane(shape):
    return lax.broadcasted_iota(jnp.int32, shape, len(shape) - 1)


def fill_spread(e_ref):
    row = lax.broadcasted_iota(jnp.int32, (LANES, W), 0)
    col = lax.broadcasted_iota(jnp.int32, (LANES, W), 1)
    e_ref[...] = jnp.where((row & 63) == (col >> 6), 1.0, 0.0).astype(BF16)


def to_half(values, base):
    return pltpu.roll(values, lax.rem(LANES - PER * base, LANES), 1)


def pair_up(values):
    high = values.astype(BF16).astype(F32)
    low = values - high
    return jnp.where(lane(values.shape) < 64, high, pltpu.roll(low, 64, 1))


def of_group(pairs, i):
    if i:
        pairs = pltpu.roll(pairs, LANES - PER * i, 1)
    return pairs.astype(BF16)


def silu(v):
    return v * (0.5 * jnp.tanh(0.5 * v) + 0.5)


def steps_of(dt_ref, bias_ref, alog_ref):
    u = jnp.exp(dt_ref[...].astype(F32) + bias_ref[...])
    one = 1.0 + u
    step = jnp.where(one == 1.0, u, jnp.log(one) * (u / jnp.where(one == 1.0, 1.0, one - 1.0)))
    rate = -step * jnp.exp(alog_ref[...])
    row = lax.broadcasted_iota(jnp.int32, (T, T), 0)
    col = lax.broadcasted_iota(jnp.int32, (T, T), 1)
    tri = jnp.where(row >= col, 1.0, 0.0).astype(BF16)
    running = jnp.zeros((T, NH), F32)
    for _ in range(3):
        piece = rate.astype(BF16)
        running = running + jnp.dot(tri, piece, preferred_element_type=F32)
        rate = rate - piece.astype(F32)
    from_start = jnp.exp(running)
    to_end = jnp.exp(running[T - 1 : T] - running) * step
    return step, running, from_start, to_end


def base_of(own, sc_ref):
    return HALF * sc_ref[0] if own else HALF * (1 - sc_ref[0])


def columns(base, i, width):
    return pl.ds(pl.multiple_of((base + i) * width, width), width)


def states_kernel(own, sc_ref, *refs):
    if own:
        aux_ref, kept, tokens, refs = refs[0], refs[1:6], refs[6:11], refs[11:]
        st_ref, part_hbm, e_ref, used, (sem, sem_out) = refs[0], refs[1], refs[2], refs[3:8], refs[8:]
        early = KEPT
    else:
        dt_hbm, bias_hbm, alog_hbm = refs[:3]
        tokens = refs[3:8]
        st_ref, aux_ref, aux_hbm = refs[8:11]
        kept = refs[11:16]
        e_ref = refs[16]
        used = refs[17:22]
        small = refs[22:25]
        sem, sem_small, sem_kept = refs[25:]
        early = 0
    base = base_of(own, sc_ref)
    stores = []

    def loads(first, groups, targets, sems):
        rows = []
        for k, i in enumerate(groups):
            row = []
            for j, (src, dst) in enumerate(zip(tokens, targets)):
                cut = columns(first, i, dst.shape[-1])
                row.append(pltpu.make_async_copy(src.at[:, cut], dst.at[k], sems.at[k, j]))
                row[-1].start()
            rows.append(row)
        return rows

    if not own:
        smalls = [
            pltpu.make_async_copy(s, d, sem_small.at[k])
            for k, (s, d) in enumerate(zip((dt_hbm, bias_hbm, alog_hbm), small))
        ]
        for copy in smalls:
            copy.start()
    copies = loads(base, range(early, HALF), used, sem)
    fill_spread(e_ref)
    if not own:
        for copy in smalls:
            copy.wait()
        for k, v in enumerate(steps_of(*small)):
            aux_ref[k] = v
        stores.append(pltpu.make_async_copy(aux_ref, aux_hbm, sem_small.at[3]))
        stores[0].start()
    from_start = pair_up(to_half(aux_ref[2], base))
    to_end = pair_up(to_half(aux_ref[3], base))
    for i in range(HALF):
        if i >= early:
            for copy in copies[i - early]:
                copy.wait()
        if not own and i == 0:
            ahead = loads(base_of(True, sc_ref), range(KEPT), kept, sem_kept)
        at = i if i < early else i - early
        b_ref, x_ref, c_ref, z_ref, og_ref = [
            r.at[at] for r in (kept if i < early else used)
        ]
        here = slice(i * N, (i + 1) * N)
        te = of_group(to_end, i)
        fs = of_group(from_start, i)
        bt = b_ref[...].T
        ct = c_ref[...].T
        for k in range(W // CHUNK):
            cut = slice(k * CHUNK, (k + 1) * CHUNK)
            e = e_ref[:, cut]
            xs = x_ref[:, cut].astype(F32) * jnp.dot(te, e, preferred_element_type=F32)
            st_ref[here, cut] = jnp.dot(
                bt, xs.astype(BF16), preferred_element_type=F32
            ).astype(BF16)
            gate = silu(z_ref[:, cut].astype(F32))
            hg = (og_ref[:, cut].astype(F32) * gate).astype(BF16)
            gs = hg.astype(F32) * jnp.dot(fs, e, preferred_element_type=F32)
            st_ref[here, slice(W + k * CHUNK, W + (k + 1) * CHUNK)] = jnp.dot(
                ct, gs.astype(BF16), preferred_element_type=F32
            ).astype(BF16)
        decay = jnp.broadcast_to(fs[T - 16 : T].astype(F32)[15:16], (N, LANES))
        st_ref[here, 2 * W :] = decay.astype(BF16)
        if own:
            stores += part_copies(st_ref, part_hbm, here, sc_ref[0], sem_out.at[i])
            for store in stores[-2:]:
                store.start()
    if not own:
        for row in ahead:
            for copy in row:
                copy.wait()
    for store in stores:
        store.wait()


def part_copies(st_ref, part_hbm, here, which, sem):
    cut = pl.ds(pl.multiple_of(which * W, W), W)
    return [
        pltpu.make_async_copy(st_ref.at[here, cut], part_hbm.at[here, :W], sem.at[0]),
        pltpu.make_async_copy(st_ref.at[here, 2 * W :], part_hbm.at[here, W:], sem.at[1]),
    ]


STATE = jax.ShapeDtypeStruct((HALF * N, WIDE), BF16)
PART = pltpu.HBM((HALF * N, W + LANES), BF16)


def token_shapes(groups):
    return [(groups, T, width) for width in (N, W, N, W, W)]


def states_send(sc, dt, bias, alog, *tokens):
    aux = jax.ShapeDtypeStruct((4, T, NH), F32)
    return pl.pallas_call(
        functools.partial(states_kernel, False),
        in_specs=[SMEM_SPEC] + [HBM_SPEC] * 8,
        out_specs=[VMEM_SPEC, VMEM_SPEC, HBM_SPEC] + [VMEM_SPEC] * 5,
        out_shape=[STATE, aux, pltpu.HBM((4, T, NH), F32)]
        + [jax.ShapeDtypeStruct(s, BF16) for s in token_shapes(KEPT)],
        scratch_shapes=[SPREAD]
        + [pltpu.VMEM(s, BF16) for s in token_shapes(HALF)]
        + [pltpu.VMEM((T, NH), BF16), pltpu.VMEM((1, NH), F32), pltpu.VMEM((1, NH), F32)]
        + [pltpu.SemaphoreType.DMA((HALF, 5)), pltpu.SemaphoreType.DMA((4,))]
        + [pltpu.SemaphoreType.DMA((KEPT, 5))],
        compiler_params=params(24),
        name="states_send",
    )(sc, *[in_hbm(a) for a in (dt, bias, alog, *tokens)])


def states_keep(sc, aux, kept, tokens):
    return pl.pallas_call(
        functools.partial(states_kernel, True),
        in_specs=[SMEM_SPEC] + [VMEM_SPEC] * 6 + [HBM_SPEC] * 5,
        out_specs=[VMEM_SPEC, HBM_SPEC],
        out_shape=[STATE, PART],
        scratch_shapes=[SPREAD]
        + [pltpu.VMEM(s, BF16) for s in token_shapes(HALF - KEPT)]
        + [pltpu.SemaphoreType.DMA((HALF - KEPT, 5)), pltpu.SemaphoreType.DMA((HALF, 2))],
        compiler_params=params(12),
        name="states_keep",
    )(sc, aux, *kept, *[in_hbm(a) for a in tokens])


def decay_row(state_ref, at, e_ref):
    pairs = state_ref[at : at + 16, 2 * W :]
    return jnp.dot(pairs, e_ref[...], preferred_element_type=F32)[0:1]


def merge_kernel(sc_ref, own_ref, got_ref, out_hbm, part_hbm, e_ref, out_ref, sem, sem_out):
    core = sc_ref[0]
    parts = part_copies(got_ref, part_hbm, slice(0, HALF * N), 1 - core, sem)
    for part in parts:
        part.start()
    fill_spread(e_ref)

    def merge(r0, r1):
        stores = []
        for i in range(HALF):
            here = slice(i * N, (i + 1) * N)
            there = slice(i * N // 8, (i + 1) * N // 8)
            d0 = decay_row(r0, i * N, e_ref)
            d1 = decay_row(r1, i * N, e_ref)
            for k in range(W // CHUNK):
                cut = slice(k * CHUNK, (k + 1) * CHUNK)
                forward = d1[:, cut] * r0[here, cut].astype(F32) + r1[here, cut].astype(F32)
                out_ref[there, :, cut] = forward.reshape(N // 8, 8, CHUNK).astype(BF16)
                back = slice(W + k * CHUNK, W + (k + 1) * CHUNK)
                backward = r0[here, back].astype(F32) + d0[:, cut] * r1[here, back].astype(F32)
                out_ref[there, :, back] = backward.reshape(N // 8, 8, CHUNK).astype(BF16)
            p0 = r0[i * N : i * N + 16, 2 * W :].astype(F32)
            p1 = r1[i * N : i * N + 16, 2 * W :].astype(F32)
            p0 = p0 + pltpu.roll(p0, 64, 1)
            p1 = p1 + pltpu.roll(p1, 64, 1)
            both = pair_up(p0 * p1)[0:8]
            both = jnp.broadcast_to(both[None], (N // 8, 8, LANES))
            out_ref[there, :, 2 * W :] = both.astype(BF16)
            stores.append(pltpu.make_async_copy(out_ref.at[there], out_hbm.at[there], sem_out.at[i]))
            stores[-1].start()
        for store in stores:
            store.wait()

    @pl.when(core == 0)
    def _():
        merge(own_ref, got_ref)

    @pl.when(core != 0)
    def _():
        merge(got_ref, own_ref)

    for part in parts:
        part.wait()


def merge(sc, own, got):
    return pl.pallas_call(
        merge_kernel,
        in_specs=[SMEM_SPEC, VMEM_SPEC, VMEM_SPEC],
        out_specs=[HBM_SPEC, HBM_SPEC],
        out_shape=[pltpu.HBM((HALF * N // 8, 8, WIDE), BF16), PART],
        scratch_shapes=[
            SPREAD,
            pltpu.VMEM((HALF * N // 8, 8, WIDE), BF16),
            pltpu.SemaphoreType.DMA((2,)),
            pltpu.SemaphoreType.DMA((HALF,)),
        ],
        compiler_params=params(16),
        name="merge_cores",
    )(sc, own, got)


def scan_kernel(chips, in_ref, after_ref, out_hbm, e_ref, d_ref, out_ref, sem):
    fill_spread(e_ref)
    pairs = in_ref[:, :, 2 * W :].astype(F32).reshape(chips * 8, LANES).astype(BF16)
    d_ref[...] = jnp.dot(pairs, e_ref[...], preferred_element_type=F32).reshape(chips, 8, W)
    zero = jnp.zeros((8, W), F32)

    def forward(k, e):
        out_ref[k, :, :W] = e.astype(BF16)
        return d_ref[k] * e + in_ref[k, :, :W].astype(F32)

    def backward(k, l):
        j = chips - 1 - k
        out_ref[j, :, W:] = l.astype(BF16)
        return d_ref[j] * l + in_ref[j, :, W : 2 * W].astype(F32)

    parts = ((0, chips, slice(0, W)), (chips // 4, chips, slice(W, 2 * W)), (0, chips // 4, slice(W, 2 * W)))
    stores = [
        pltpu.make_async_copy(out_ref.at[a:b, :, cut], out_hbm.at[a:b, :, cut], sem.at[k])
        for k, (a, b, cut) in enumerate(parts)
    ]
    lax.fori_loop(0, chips, forward, zero, unroll=8)
    stores[0].start()
    l = lax.fori_loop(0, chips - chips // 4, backward, zero, unroll=8)
    stores[1].start()
    lax.fori_loop(chips - chips // 4, chips, backward, l, unroll=8)
    stores[2].start()
    for store in stores:
        store.wait()


def scan(parts, after):
    chips = parts.shape[0]
    return pl.pallas_call(
        functools.partial(scan_kernel, chips),
        in_specs=[VMEM_SPEC, HBM_SPEC],
        out_specs=HBM_SPEC,
        out_shape=pltpu.HBM((chips, 8, 2 * W), BF16),
        scratch_shapes=[
            SPREAD,
            pltpu.VMEM((chips, 8, W), F32),
            pltpu.VMEM((chips, 8, 2 * W), BF16),
            pltpu.SemaphoreType.DMA((3,)),
        ],
        compiler_params=params(16),
        name="scan_chips",
    )(parts, in_hbm(after))


def local_kernel(
    own, sc_ref, aux_ref, skip_ref, got_ref, b_hbm, x_hbm, c_hbm, z_hbm, og_hbm, *refs
):
    if own:
        results, refs = refs[:7], refs[7:]
        fetched = ()
    else:
        ready, results, fetched, refs = refs[:5], refs[5:12], refs[12:20], refs[20:]
    y_ref, dx_ref, xs_ref, gs_ref, pair_ref, db_ref, dc_ref = results
    (
    e_ref, x_ref, z_ref, og_ref, b_ref, c_ref, ysum_ref, dxsum_ref, dbsum_ref, dcsum_ref, hg_ref,
    runc_ref, run_ref, step_ref, plain_ref, sem, *more,
    ) = refs
    base = base_of(own, sc_ref)
    core = sc_ref[0]
    copies = []
    if not own:
        first = base_of(True, sc_ref)
        sources = [r.at[:, columns(first, 0, w)] for r, w in ((b_hbm, N), (c_hbm, N), (z_hbm, W))]
        sources += [r.at[0] for r in ready]
        for k, (src, dst) in enumerate(zip(sources, fetched)):
            copies.append(pltpu.make_async_copy(src, dst, more[0].at[k]))
            copies[-1].start()
    for i in range(HALF):
        for k, (src, dst, width) in enumerate(
            (
                (b_hbm, b_ref, N),
                (x_hbm, x_ref, W),
                (c_hbm, c_ref, N),
                (z_hbm, z_ref, W),
                (og_hbm, og_ref, W),
            )
        ):
            copies.append(
                pltpu.make_async_copy(src.at[:, columns(base, i, width)], dst.at[i], sem.at[i, k])
            )
            copies[-1].start()
    fill_spread(e_ref)
    start = to_half(aux_ref[2], base)
    end = to_half(aux_ref[3], base)
    gain = to_half(jnp.broadcast_to(skip_ref[...], (16, NH)), base)
    run = to_half(aux_ref[1], base)
    run_t = run.T
    step_t = to_half(aux_ref[0], base).T
    for i in range(HALF):
        decay = got_ref[i * N : i * N + 16, W:].astype(F32)
        decay = (decay + pltpu.roll(decay, 64, 1))[0:1]
        fs, te, skip, run_c = [pltpu.roll(v, LANES - PER * i, 1) if i else v for v in (start, end, gain, run)]
        plain_ref[i, 0:T] = pair_up(fs).astype(BF16)
        plain_ref[i, T : 2 * T] = pair_up(te).astype(BF16)
        plain_ref[i, 2 * T : 2 * T + 16] = pair_up(skip).astype(BF16)
        pair_ref[i, 0:T] = pair_up(jnp.where(core == 0, fs, fs * decay)).astype(BF16)
        pair_ref[i, T : 2 * T] = pair_up(jnp.where(core == 0, te * decay, te)).astype(BF16)
        runc_ref[i] = run_c
        run_ref[i] = run_t[i * PER : (i + 1) * PER]
        step_ref[i] = step_t[i * PER : (i + 1) * PER]
    for copy in copies:
        copy.wait()
    row = lax.broadcasted_iota(jnp.int32, (T, T), 0)
    col = lax.broadcasted_iota(jnp.int32, (T, T), 1)
    below = row >= col
    left = col < P_SIZE

    def one_group(i, unused):
        b, c = b_ref[i], c_ref[i]
        cb = lax.dot_general(c, b, NT, preferred_element_type=F32)
        run_cols, run_rows, step_rows = runc_ref[i], run_ref[i], step_ref[i]
        mass = jnp.zeros((T, T), F32)
        for pair in range(PER // 2):
            here = slice(pair * LANES, (pair + 1) * LANES)
            e = e_ref[:, here]
            both = jnp.dot(pair_ref[i], e, preferred_element_type=F32)
            skip = jnp.dot(plain_ref[i, 2 * T : 2 * T + 16], e, preferred_element_type=F32)[0:1]
            x = x_ref[i, :, here]
            g = (og_ref[i, :, here].astype(F32) * silu(z_ref[i, :, here].astype(F32))).astype(BF16)
            hg_ref[:, here] = g
            gs_ref[i, :, here] = (g.astype(F32) * both[0:T]).astype(BF16)
            xs_ref[i, :, here] = (x.astype(F32) * both[T : 2 * T]).astype(BF16)
            ys, dxs = [], []
            for k in range(2):
                j = 2 * pair + k
                gap = run_cols[:, j : j + 1] - run_rows[j : j + 1, :]
                weight = jnp.exp(jnp.where(below, gap, -1e30)) * step_rows[j : j + 1, :]
                mine = left if k == 0 else ~left
                inner = lax.dot_general(
                    jnp.where(mine, g, jnp.zeros_like(g)), x, NT, preferred_element_type=F32
                )
                mass = mass + weight * inner
                joint = (weight * cb).astype(BF16)
                ys.append(jnp.dot(joint, x, preferred_element_type=F32))
                dxs.append(jnp.dot(joint.T, g, preferred_element_type=F32))
            ysum_ref[:, here] = jnp.where(left, ys[0], ys[1]) + skip * x.astype(F32)
            dxsum_ref[:, here] = jnp.where(left, dxs[0], dxs[1]) + skip * g.astype(F32)
        high = mass.astype(BF16)
        low = (mass - high.astype(F32)).astype(BF16)
        dcsum_ref[...] = jnp.dot(high, b, preferred_element_type=F32) + jnp.dot(
            low, b, preferred_element_type=F32
        )
        dbsum_ref[...] = jnp.dot(high.T, c, preferred_element_type=F32) + jnp.dot(
            low.T, c, preferred_element_type=F32
        )
        rows = pl.ds(pl.multiple_of(i * N, N), N)

        @pl.when(core != 0)
        def _():
            partner = got_ref[rows, :W]
            fs = jnp.dot(plain_ref[i, 0:T], e_ref[...], preferred_element_type=F32)
            ysum_ref[...] += fs * jnp.dot(c, partner, preferred_element_type=F32)
            gs = (hg_ref[...].astype(F32) * fs).astype(BF16)
            dcsum_ref[...] += lax.dot_general(gs, partner, NT, preferred_element_type=F32)

        @pl.when(core == 0)
        def _():
            partner = got_ref[rows, :W]
            te = jnp.dot(plain_ref[i, T : 2 * T], e_ref[...], preferred_element_type=F32)
            dxsum_ref[...] += te * jnp.dot(b, partner, preferred_element_type=F32)
            xs = (x_ref[i].astype(F32) * te).astype(BF16)
            dbsum_ref[...] += lax.dot_general(xs, partner, NT, preferred_element_type=F32)

        y_ref[i] = ysum_ref[...].astype(BF16)
        dx_ref[i] = dxsum_ref[...].astype(BF16)
        db_ref[i] = dbsum_ref[...].astype(BF16)
        dc_ref[i] = dcsum_ref[...].astype(BF16)
        return unused

    lax.fori_loop(0, HALF, one_group, 0)


FETCHED = (
    [((T, N), BF16)] * 2 + [((T, W), BF16)] * 5 + [((2 * T, LANES), BF16)]
)


def local(own, sc, aux, skip, got, tokens, ready=()):
    wide = pltpu.HBM((HALF, T, W), BF16)
    thin = pltpu.HBM((HALF, T, N), BF16)
    args = [in_hbm(a) for a in (aux, skip, got, *tokens, *ready)]
    fetched = [] if own else [jax.ShapeDtypeStruct(*f) for f in FETCHED]
    return pl.pallas_call(
        functools.partial(local_kernel, own),
        in_specs=[SMEM_SPEC, VMEM_SPEC, VMEM_SPEC, VMEM_SPEC] + [HBM_SPEC] * (5 + len(ready)),
        out_specs=[VMEM_SPEC] * (7 + len(fetched)),
        out_shape=[wide] * 4 + [pltpu.HBM((HALF, 2 * T, LANES), BF16)] + [thin] * 2 + fetched,
        scratch_shapes=[SPREAD]
        + [pltpu.VMEM((HALF, T, W), BF16)] * 3
        + [pltpu.VMEM((HALF, T, N), BF16)] * 2
        + [pltpu.VMEM((T, W), F32)] * 2
        + [pltpu.VMEM((T, N), F32)] * 2
        + [pltpu.VMEM((T, W), BF16)]
        + [pltpu.VMEM((HALF, T, LANES), F32)]
        + [pltpu.VMEM((HALF, PER, T), F32)] * 2
        + [pltpu.VMEM((HALF, 2 * T + 16, LANES), BF16)]
        + [pltpu.SemaphoreType.DMA((HALF, 5))]
        + ([] if own else [pltpu.SemaphoreType.DMA((len(FETCHED),))]),
        compiler_params=params(24),
        name="local_own" if own else "local_other",
    )(sc, *args)


def final_kernel(own, sc_ref, el_ref, *refs):
    if own:
        b0, c0, z0, y0, dx0, xs0, gs0, pair0 = refs[:8]
        fetched = (b0, c0, pair0, y0, z0, dx0, xs0, gs0)
        refs = refs[8:]
        sources, others, refs = refs[:10], refs[10:20], refs[20:]
        out_hbm, dx_hbm, db_hbm, dc_hbm = refs[:4]
        kept, refs = refs[4:14], refs[14:]
        e_ref, targets, refs = refs[0], refs[1:11], refs[11:]
        out_ref, dx_ref, db_ref, dc_ref, sem_out, sem_in = refs
    else:
        targets, refs = refs[:10], refs[14:]
        out_hbm, dx_hbm, db_hbm, dc_hbm = refs[:4]
        e_ref, out_ref, dx_ref, db_ref, dc_ref, sem_out = refs[4:]
    base = base_of(own, sc_ref)

    def loads(first, srcs, dsts, sems, skip=()):
        rows = []
        for i in range(HALF):
            row = []
            for k, (src, dst) in enumerate(zip(srcs, dsts)):
                if i == 0 and k in skip:
                    continue
                if k in (0, 1, 4):
                    src = src.at[:, columns(first, i, W if k == 4 else N)]
                else:
                    src = src.at[i]
                row.append(pltpu.make_async_copy(src, dst.at[i], sems.at[i, k]))
                row[-1].start()
            rows.append(row)
        return rows

    copies = loads(base, sources, targets, sem_in.at[0], range(8)) if own else []
    ahead = loads(base_of(False, sc_ref), others, kept, sem_in.at[1]) if own else []
    fill_spread(e_ref)
    stores = []

    def put(k, src, dst, width):
        stores.append(
            pltpu.make_async_copy(src.at[i], dst.at[:, columns(base, i, width)], sem_out.at[i, k])
        )
        stores[-1].start()

    for i in range(HALF):
        if own:
            for load in copies[i] if i else ():
                load.wait()
        group = [r.at[i] for r in targets]
        if own and i == 0:
            group[:8] = fetched
        b_ref, c_ref, pair_ref, y_ref, z_ref, dxl_ref, xs_ref, gs_ref, dbl_ref, dcl_ref = group
        b, c = b_ref[...], c_ref[...]
        rows = slice(i * N, (i + 1) * N)
        for k in range(W // CHUNK):
            cut = slice(k * CHUNK, (k + 1) * CHUNK)
            far = slice(W + k * CHUNK, W + (k + 1) * CHUNK)
            scale = jnp.dot(pair_ref[...], e_ref[:, cut], preferred_element_type=F32)
            mixed = y_ref[:, cut].astype(F32) + scale[0:T] * jnp.dot(
                c, el_ref[rows, cut], preferred_element_type=F32
            )
            mixed = mixed.astype(BF16).astype(F32)
            out_ref[i, :, cut] = (mixed * silu(z_ref[:, cut].astype(F32))).astype(BF16)
            dx_ref[i, :, cut] = dxl_ref[:, cut].astype(F32) + scale[T : 2 * T] * jnp.dot(
                b, el_ref[rows, far], preferred_element_type=F32
            )
        put(0, out_ref, out_hbm, W)
        put(1, dx_ref, dx_hbm, W)
        for load in copies[0] if own and i == 0 else ():
            load.wait()
        db_ref[i] = dbl_ref[...].astype(F32) + lax.dot_general(
            xs_ref[...], el_ref[rows, W:], NT, preferred_element_type=F32
        )
        dc_ref[i] = dcl_ref[...].astype(F32) + lax.dot_general(
            gs_ref[...], el_ref[rows, :W], NT, preferred_element_type=F32
        )
        put(2, db_ref, db_hbm, N)
        put(3, dc_ref, dc_hbm, N)
    for row in ahead:
        for load in row:
            load.wait()
    for store in stores:
        store.wait()


LOADED = [
    ((HALF, T, N), BF16),
    ((HALF, T, N), BF16),
    ((HALF, 2 * T, LANES), BF16),
    ((HALF, T, W), BF16),
    ((HALF, T, W), BF16),
    ((HALF, T, W), BF16),
    ((HALF, T, W), BF16),
    ((HALF, T, W), BF16),
    ((HALF, T, N), BF16),
    ((HALF, T, N), BF16),
]
RESULTS = [
    ((T, NH * P_SIZE), BF16),
    ((T, NH * P_SIZE), F32),
    ((T, NG * N), F32),
    ((T, NG * N), F32),
]
STAGED = [
    pltpu.VMEM((HALF, T, W), BF16),
    pltpu.VMEM((HALF, T, W), F32),
    pltpu.VMEM((HALF, T, N), F32),
    pltpu.VMEM((HALF, T, N), F32),
    pltpu.SemaphoreType.DMA((HALF, 4)),
]


def in_order(local_parts, z, b, c):
    y, dx, xs, gs, pairs, db, dc = local_parts
    return [in_hbm(a) for a in (b, c, pairs, y, z, dx, xs, gs, db, dc)]


def final_own(sc, el, fetched, own_parts, other_parts):
    return pl.pallas_call(
        functools.partial(final_kernel, True),
        in_specs=[SMEM_SPEC, VMEM_SPEC] + [VMEM_SPEC] * 8 + [HBM_SPEC] * 20,
        out_specs=[HBM_SPEC] * 4 + [VMEM_SPEC] * 10,
        out_shape=[pltpu.HBM(*r) for r in RESULTS] + [jax.ShapeDtypeStruct(*r) for r in LOADED],
        scratch_shapes=[SPREAD]
        + [pltpu.VMEM(*r) for r in LOADED]
        + STAGED
        + [pltpu.SemaphoreType.DMA((2, HALF, 10))],
        compiler_params=params(24),
        name="final_own",
    )(sc, el, *fetched, *own_parts, *other_parts)


def final_other(sc, el, loaded, earlier):
    return pl.pallas_call(
        functools.partial(final_kernel, False),
        in_specs=[SMEM_SPEC, VMEM_SPEC] + [VMEM_SPEC] * 10 + [HBM_SPEC] * 4,
        out_specs=[HBM_SPEC] * 4,
        out_shape=[pltpu.HBM(*r) for r in RESULTS],
        input_output_aliases={12 + k: k for k in range(4)},
        scratch_shapes=[SPREAD] + STAGED,
        compiler_params=params(16),
        name="final_other",
    )(sc, el, *loaded, *earlier)


def body(ssm_input, gate_input, b_input, c_input, dt_raw, dt_bias, a_log, skip_gain, out_grad):
    ctx_count = lax.axis_size("ctx")
    head_count = lax.axis_size("head")
    sc = (lax.axis_index("head") % 2).astype(jnp.int32)[None]
    bias, alog, skip = dt_bias[None, :], a_log[None, :], skip_gain[None, :]
    swap = [(k, k ^ 1) for k in range(head_count)]
    chips = [[2 * k + c for k in range(ctx_count * head_count // 2)] for c in range(2)]

    def exchange(parts):
        return lax.all_to_all(
            parts, ("ctx", "head"), split_axis=0, concat_axis=0, tiled=True, axis_index_groups=chips
        )

    tokens = (b_input, ssm_input, c_input, gate_input, out_grad)
    send, aux, aux_hbm, *kept = states_send(sc, dt_raw, bias, alog, *tokens)
    got = lax.ppermute(send, "head", swap)
    keep, keep_part = states_keep(sc, aux, kept, tokens)
    payload, got_part = merge(sc, keep, got)
    gathered = exchange(payload)
    got_other = lax.ppermute(keep_part, "head", swap)
    loc_own = local(True, sc, aux_hbm, skip, got_part, tokens)
    back = exchange(scan(gathered, loc_own[6]))
    loc_other = local(False, sc, aux_hbm, skip, got_other, tokens, loc_own[:5])
    back, loc_other = lax.optimization_barrier((back, loc_other))
    el = back.reshape(HALF * N, 2 * W)
    el_other = lax.ppermute(el, "head", swap)
    shared = (gate_input, b_input, c_input)
    own_parts, other_parts = in_order(loc_own, *shared), in_order(loc_other[:7], *shared)
    outs = final_own(sc, el, loc_other[7:], own_parts, other_parts)
    return tuple(final_other(sc, el_other, outs[4:], outs[:4]))


def solution(mesh):
    row_spec = P(("ctx", "head"), None)
    in_specs = (row_spec,) * 5 + (P(), P(), P(), row_spec)
    return jax.shard_map(
        body, mesh=mesh, in_specs=in_specs, out_specs=(row_spec,) * 4, check_vma=False
    )
```
